32 devices in a mesh: groups: 1, ctx: 8 (over z, y), bal: 4 (over x, core), head: 1.
Axes of the slice: x: 2, y: 2, z: 4, core: 2. Of those that a mesh axis runs over, the one named last changes fastest.
Arguments:
- queries: bfloat16 [16384, 2560], P(('groups', 'ctx', 'bal'), 'head'), may hold values from -32 to 32
- keys: bfloat16 [16384, 2560], P(('groups', 'ctx', 'bal'), 'head'), may hold values from -32 to 32
- values: bfloat16 [16384, 2560], P(('groups', 'ctx', 'bal'), 'head'), may hold values from -6 to 6
- output_gradient: bfloat16 [16384, 2560], P(('groups', 'ctx', 'bal'), 'head'), may hold values from -6 to 6
- dilation_phase: int32 [20], P('head'), may hold values from 0 to 127
- segment_device_count: int32 [20], P('head'), may hold values from 1 to 32, as said below
- owner: int32 [128], P('groups'), may hold values from 0 to 127, as said below
Outputs:
- attended: bfloat16 [16384, 2560], P(('groups', 'ctx', 'bal'), 'head')
- query_grad: bfloat16 [16384, 2560], P(('groups', 'ctx', 'bal'), 'head')
- key_grad: bfloat16 [16384, 2560], P(('groups', 'ctx', 'bal'), 'head')
- value_grad: bfloat16 [16384, 2560], P(('groups', 'ctx', 'bal'), 'head')
The draws below stay inside these ranges and needn't reach their ends.
Inputs may be any that keep to these rules, and one draw needn't show every extreme that they name: `segment_device_count`: every entry is a power of two. The device at index d of the 32 devices of a document (context shard major) holds blocks d * 4 onward. owner is one to one and keeps every block in its context shard of 4 devices: a block of the device at index b of a shard goes to some device e of that shard, into its slot b + t with 0 <= t < 1, and every device hands exactly 1 of its blocks to each device of its shard, itself included.
All inputs are finite; a program needn't handle non-finite values.
Results may differ from the reference program's by a relative error of at most 0.013.
The reference program's roundings to bfloat16 on the way count: a program that leaves them out, or rounds other values in their place, can miss the bound.
Values may be sent and summed in bfloat16 or wider, within the bound.
No kernel may reach another device: no remote copies, remote signals or barrier semaphores. Data moves between devices by JAX's collectives and lax.ppermute only.
A program may use at most 128 MiB of HBM per device.

```python
import math
import jax
import jax.numpy as jnp
from jax import lax

HEAD_TOTAL = 20
HEAD_DIM = 128
BLOCK_TOKENS = 128
DILATION_STEP = 128
TOK_DEV = 512
SHARD = 4
DEV_SEQ = 32
TOKENS = 16384
NBLK = 128
CAP = 1


def draw_queries(key, part):
    key = jax.random.fold_in(key, 11)
    full_shape = (TOKENS, HEAD_TOTAL * HEAD_DIM)
    return jax.random.truncated_normal(key, -4.5, 4.5, full_shape, jnp.float32).astype(jnp.bfloat16)


def draw_keys(key, part):
    key = jax.random.fold_in(key, 13)
    sample_key, scale_key = jax.random.split(key)
    full_shape = (TOKENS, HEAD_TOTAL * HEAD_DIM)
    drawn_draw = jax.random.truncated_normal(sample_key, -4.5, 4.5, full_shape, jnp.float32)
    spread = jnp.exp(jax.random.uniform(scale_key, (TOKENS, 1), jnp.float32, math.log(0.3), math.log(3.0)))
    return (drawn_draw * spread).astype(jnp.bfloat16)


def draw_segment_device_count(key, part):
    key = jax.random.fold_in(key, 5)
    top_level = DEV_SEQ.bit_length() - 1
    level_key, order_key = jax.random.split(key)
    exponents = jax.random.randint(level_key, (HEAD_TOTAL,), 0, top_level + 1)
    head_order = jax.random.permutation(order_key, HEAD_TOTAL)
    exponents = exponents.at[head_order[0]].set(0).at[head_order[1]].set(top_level)
    return jnp.left_shift(jnp.ones((HEAD_TOTAL,), jnp.int32), exponents.astype(jnp.int32))


def draw_owner(key, part):
    key = jax.random.fold_in(key, 9)
    per_device = TOK_DEV // BLOCK_TOKENS
    device_keys = jax.random.split(key, DEV_SEQ + 1)
    slot_rank = jax.vmap(lambda one_key: jax.random.permutation(one_key, per_device))(device_keys[:DEV_SEQ])
    rotation = jax.random.randint(device_keys[DEV_SEQ], (DEV_SEQ, 1), 0, SHARD)
    device_number = jnp.arange(DEV_SEQ, dtype=jnp.int32)[:, None]
    destination = (slot_rank // CAP + rotation) % SHARD
    table = device_number // SHARD * (SHARD * per_device) + destination * per_device + device_number % SHARD * CAP + slot_rank % CAP
    return table.reshape(NBLK).astype(jnp.int32)


def set_ends(values, stream_key, smallest, high):
    longest = values.shape.index(max(values.shape))
    spots = []
    for shift in (0, 1):
        where = [jax.random.randint(jax.random.fold_in(stream_key, axis), (), 0, length) for axis, length in enumerate(values.shape)]
        where[longest] = (where[longest] + shift) % values.shape[longest]
        spots.append(tuple(where))
    return values.at[spots[0]].set(smallest).at[spots[1]].set(high)


def block_levels(rng, dims, cuts, smallest, top_value):
    factor_of = 1.0
    for axis_at, blocks in cuts:
        heights = jax.random.uniform(jax.random.fold_in(jax.random.fold_in(rng, 6), axis_at), (blocks,), jnp.float32, smallest / len(cuts), top_value / len(cuts))
        factor_of = factor_of * jnp.repeat(jnp.exp(heights), dims[axis_at] // blocks).reshape((-1,) + (1,) * (len(dims) - 1 - axis_at))
    return factor_of


def centred(own_key, shape, scale, bound, shards=(), held_as=jnp.bfloat16):
    entries = jax.random.normal(own_key, shape, jnp.float32) * scale
    if len(shards) > 0:
        entries = block_levels(own_key, shape, shards, -0.22, 0.18) * entries
    return jnp.clip(entries, min=-bound, max=bound).astype(held_as)


def setup_inputs(seed: int = 0, part: int = 0) -> dict:
    streams_of = jax.random.split(jax.random.key(seed), 8)
    part_splits = jax.random.split(jax.random.fold_in(streams_of[7], part), 8)
    return {
        "queries": draw_queries(jax.random.fold_in(jax.random.fold_in(streams_of[7], part), 71), part),
        "keys": draw_keys(jax.random.fold_in(jax.random.fold_in(streams_of[7], part), 71), part),
        "values": centred(part_splits[2], (TOKENS, HEAD_TOTAL * HEAD_DIM), 1.0, 6.0, ((0, 32),)),
        "output_gradient": centred(part_splits[3], (TOKENS, HEAD_TOTAL * HEAD_DIM), 1.0, 6.0, ((0, 32),)),
        "dilation_phase": set_ends(jax.random.randint(streams_of[4], (HEAD_TOTAL,), 0, DILATION_STEP), jax.random.fold_in(streams_of[4], 1), 0, DILATION_STEP - 1).astype(jnp.int32),
        "segment_device_count": draw_segment_device_count(jax.random.fold_in(streams_of[7], 71), part),
        "owner": draw_owner(jax.random.fold_in(jax.random.fold_in(streams_of[7], part), 71), part),
    }


def xpos_tables(positions, head_width, token_sequence):
    half_dim = head_width // 2
    pair_index = jnp.arange(half_dim, dtype=jnp.float32)
    inverse = jnp.exp(pair_index * (-2.0 * math.log(10000.0) / head_width))
    angles = positions.astype(jnp.float32)[:, None] * inverse[None, :]
    zeta_base = (2.0 * pair_index / head_width + 0.4) / 1.4
    exponent = (2.0 * positions.astype(jnp.float32) - token_sequence) / token_sequence
    growth = jnp.exp(exponent[:, None] * jnp.log(zeta_base)[None, :])
    return (jnp.cos(angles), jnp.sin(angles), jnp.concatenate([growth, growth], axis=1))

def turn_forward(tensor, cosine, sine_table):
    half_dim = tensor.shape[-1] // 2
    leading = tensor[..., :half_dim]
    trailing = tensor[..., half_dim:]
    cosine = cosine[:, None, :]
    sine_table = sine_table[:, None, :]
    return jnp.concatenate([leading * cosine - trailing * sine_table, trailing * cosine + leading * sine_table], axis=-1)

def turn_back(tensor, cosine, sine_table):
    half_dim = tensor.shape[-1] // 2
    leading = tensor[..., :half_dim]
    trailing = tensor[..., half_dim:]
    cosine = cosine[:, None, :]
    sine_table = sine_table[:, None, :]
    return jnp.concatenate([leading * cosine + trailing * sine_table, trailing * cosine - leading * sine_table], axis=-1)

def attend(head_query, key_per_head, value_per_head, head_grad, distant_key, distant_value, query_position, position_of_key, segment_tokens, inverse_square_root):
    count_of_rows = head_query.shape[0]
    head_width = head_query.shape[1]
    blocks = count_of_rows // BLOCK_TOKENS
    blocks_of_queries = head_query.reshape(blocks, BLOCK_TOKENS, head_width).astype(jnp.float32)
    blocks_of_keys = key_per_head.reshape(blocks, BLOCK_TOKENS, head_width).astype(jnp.float32)
    blocks_of_values = value_per_head.reshape(blocks, BLOCK_TOKENS, head_width).astype(jnp.float32)
    gradient_blocks = head_grad.reshape(blocks, BLOCK_TOKENS, head_width).astype(jnp.float32)
    causal = jnp.arange(BLOCK_TOKENS)[:, None] >= jnp.arange(BLOCK_TOKENS)[None, :]
    nearby_score = jnp.einsum('fti,fni->ftn', blocks_of_queries, blocks_of_keys) * inverse_square_root
    nearby_score = jnp.where(causal[None], nearby_score, -jnp.inf)
    remote = jnp.dot(head_query, distant_key.T, preferred_element_type=jnp.float32) * inverse_square_root
    same_segment = query_position[:, None] // segment_tokens == position_of_key[None, :] // segment_tokens
    earlier = position_of_key[None, :] // BLOCK_TOKENS < query_position[:, None] // BLOCK_TOKENS
    remote = jnp.where(same_segment & earlier, remote, -jnp.inf)
    row_top = jnp.maximum(lax.optimization_barrier(jnp.max(nearby_score, axis=2)).reshape(count_of_rows), lax.optimization_barrier(jnp.max(remote, axis=1)))
    local_exp = jnp.exp(nearby_score - row_top.reshape(blocks, BLOCK_TOKENS, 1))
    remote_exp = jnp.exp(remote - row_top[:, None])
    row_total = lax.optimization_barrier(jnp.sum(local_exp, axis=2)).reshape(count_of_rows) + lax.optimization_barrier(jnp.sum(remote_exp, axis=1))
    local_prob = local_exp / row_total.reshape(blocks, BLOCK_TOKENS, 1)
    remote_prob = remote_exp / row_total[:, None]
    nearby_half = local_prob.astype(jnp.bfloat16)
    remote_half = remote_prob.astype(jnp.bfloat16)
    attention_output = jnp.einsum('xul,xlc->xuc', nearby_half.astype(jnp.float32), blocks_of_values).reshape(count_of_rows, head_width)
    attention_output = attention_output + jnp.dot(remote_half, distant_value, preferred_element_type=jnp.float32)
    row_delta = lax.optimization_barrier(jnp.sum(head_grad.astype(jnp.float32) * attention_output, axis=1))
    nearby_probability_gradient = jnp.einsum('fti,fni->ftn', gradient_blocks, blocks_of_values)
    remote_dprob = jnp.dot(head_grad, distant_value.T, preferred_element_type=jnp.float32)
    nearby_score_gradient = (local_prob * (nearby_probability_gradient - row_delta.reshape(blocks, BLOCK_TOKENS, 1))).astype(jnp.bfloat16)
    remote_dscore = (remote_prob * (remote_dprob - row_delta[:, None])).astype(jnp.bfloat16)
    query_gradient = jnp.einsum('xul,xlc->xuc', nearby_score_gradient.astype(jnp.float32), blocks_of_keys).reshape(count_of_rows, head_width)
    query_gradient = (query_gradient + jnp.dot(remote_dscore, distant_key, preferred_element_type=jnp.float32)) * inverse_square_root
    key_gradient = jnp.einsum('eml,emn->eln', nearby_score_gradient.astype(jnp.float32), blocks_of_queries).reshape(count_of_rows, head_width) * inverse_square_root
    value_gradient = jnp.einsum('eml,emn->eln', nearby_half.astype(jnp.float32), gradient_blocks).reshape(count_of_rows, head_width)
    return (attention_output, query_gradient, key_gradient, value_gradient, remote_half, remote_dscore)

def to_owners(matrix, owner):
    block_rows = matrix.reshape(owner.shape[0], BLOCK_TOKENS, matrix.shape[1])
    placed = jnp.zeros_like(block_rows).at[owner].set(block_rows)
    return placed.reshape(matrix.shape)

def reference(queries, keys, values, output_gradient, dilation_phase, segment_device_count, owner):
    token_sequence = queries.shape[0]
    count_of_heads = dilation_phase.shape[0]
    head_width = queries.shape[1] // count_of_heads
    inverse_square_root = 1.0 / math.sqrt(head_width)
    distant_count = token_sequence // DILATION_STEP
    positions = jnp.arange(token_sequence, dtype=jnp.int32)
    cosine, sine_table, growth = xpos_tables(positions, head_width, token_sequence)
    head_shape = (token_sequence, count_of_heads, head_width)
    turned_query = (turn_forward(queries.reshape(head_shape).astype(jnp.float32), cosine, sine_table) * growth[:, None, :]).astype(jnp.bfloat16)
    rotated_key = (turn_forward(keys.reshape(head_shape).astype(jnp.float32), cosine, sine_table) / growth[:, None, :]).astype(jnp.bfloat16)
    heads_of_values = values.reshape(head_shape)
    grad_heads = output_gradient.reshape(head_shape)

    def one_head(index_of_head):
        head_query = lax.dynamic_index_in_dim(turned_query, index_of_head, 1, False)
        key_per_head = lax.dynamic_index_in_dim(rotated_key, index_of_head, 1, False)
        value_per_head = lax.dynamic_index_in_dim(heads_of_values, index_of_head, 1, False)
        head_grad = lax.dynamic_index_in_dim(grad_heads, index_of_head, 1, False)
        shift_amount = dilation_phase[index_of_head]
        segment_tokens = segment_device_count[index_of_head] * TOK_DEV
        distant_key = lax.dynamic_index_in_dim(key_per_head.reshape(distant_count, DILATION_STEP, head_width), shift_amount, 1, False)
        distant_value = lax.dynamic_index_in_dim(value_per_head.reshape(distant_count, DILATION_STEP, head_width), shift_amount, 1, False)
        position_of_key = jnp.arange(distant_count, dtype=jnp.int32) * DILATION_STEP + shift_amount
        attention_output, query_gradient, key_gradient, value_gradient, remote_half, remote_dscore = attend(head_query, key_per_head, value_per_head, head_grad, distant_key, distant_value, positions, position_of_key, segment_tokens, inverse_square_root)
        distant_key_gradient = jnp.dot(remote_dscore.T, head_query, preferred_element_type=jnp.float32) * inverse_square_root
        distant_value_gradient = jnp.dot(remote_half.T, head_grad, preferred_element_type=jnp.float32)
        picked_rows = (jnp.arange(DILATION_STEP, dtype=jnp.int32) == shift_amount).astype(jnp.float32)
        key_gradient = (key_gradient.reshape(distant_count, DILATION_STEP, head_width) + distant_key_gradient[:, None, :] * picked_rows[None, :, None]).reshape(token_sequence, head_width)
        value_gradient = (value_gradient.reshape(distant_count, DILATION_STEP, head_width) + distant_value_gradient[:, None, :] * picked_rows[None, :, None]).reshape(token_sequence, head_width)
        return (attention_output, query_gradient, key_gradient, value_gradient)
    attention_output, query_gradient, key_gradient, value_gradient = lax.map(one_head, jnp.arange(count_of_heads, dtype=jnp.int32))
    attention_output = jnp.swapaxes(attention_output, 0, 1)
    query_grad = turn_back(jnp.swapaxes(query_gradient, 0, 1), cosine, sine_table) * growth[:, None, :]
    key_grad = turn_back(jnp.swapaxes(key_gradient, 0, 1), cosine, sine_table) / growth[:, None, :]
    value_grad = jnp.swapaxes(value_gradient, 0, 1)
    row_width = count_of_heads * head_width
    return (to_owners(attention_output.astype(jnp.bfloat16).reshape(token_sequence, row_width), owner), to_owners(query_grad.astype(jnp.bfloat16).reshape(token_sequence, row_width), owner), to_owners(key_grad.astype(jnp.bfloat16).reshape(token_sequence, row_width), owner), to_owners(value_grad.astype(jnp.bfloat16).reshape(token_sequence, row_width), owner))
```

```python
import functools
import math

import jax
import jax.numpy as jnp
from jax import lax
from jax.experimental import pallas as pl
from jax.experimental.pallas import tpu as pltpu
from jax.sharding import PartitionSpec as P

BLOCK = 128
HEAD = 128
LOG2E = 1.4426950408889634
NT = (((1,), (1,)), ((), ()))
TN = (((0,), (0,)), ((), ()))


def tables(positions, total):
    half = HEAD // 2
    pair = jnp.arange(half, dtype=jnp.float32)
    inverse = jnp.exp(pair * (-2.0 * math.log(10000.0) / HEAD))
    where = positions.astype(jnp.float32)[..., None]
    angles = where * inverse
    base = (2.0 * pair / HEAD + 0.4) / 1.4
    growth = jnp.exp((2.0 * where - total) / total * jnp.log(base))
    cosine, sine = jnp.cos(angles), jnp.sin(angles)

    def pack(scale):
        first, second = cosine * scale, sine * scale
        return (
            jnp.concatenate([first, first], axis=-1),
            jnp.concatenate([-second, second], axis=-1),
        )

    return pack(growth) + pack(1.0 / growth)


def dot(left, right, dims=None):
    if dims is None:
        dims = (((1,), (0,)), ((), ()))
    return lax.dot_general(left, right, dims, preferred_element_type=jnp.float32)


def pick_kernel(heads, blocks, phase, k_ref, v_ref, out_ref):
    step = pl.program_id(0)
    spot = lax.broadcasted_iota(jnp.int32, (16, HEAD), 0)
    line = lax.broadcasted_iota(jnp.int32, (2 * blocks, HEAD), 0)
    for head in range(heads):
        at = phase[head]
        start = pl.multiple_of(at // 16 * 16, 16)
        lanes = slice(head * HEAD, (head + 1) * HEAD)
        rows = []
        for ref in (k_ref, v_ref):
            tile = ref[pl.ds(start, 16), lanes].astype(jnp.float32)
            tile = jnp.where(spot == at - start, tile, 0.0)
            rows.append(jnp.sum(tile, axis=0, keepdims=True))
        fresh = jnp.where(line == step, rows[0], jnp.where(line == step + blocks, rows[1], 0.0))

        @pl.when(step == 0)
        def _():
            out_ref[:, lanes] = fresh

        @pl.when(step > 0)
        def _():
            out_ref[:, lanes] = out_ref[:, lanes] + fresh


def attend_kernel(
    per_step,
    blocks,
    count,
    info,
    phase,
    seg,
    q_ref,
    k_ref,
    v_ref,
    g_ref,
    far_ref,
    pull_ref,
    push_ref,
    cq_ref,
    sq_ref,
    ck_ref,
    sk_ref,
    *rest,
):
    outs = rest[:blocks]
    pay_ref = rest[blocks]
    near_k, near_v, far_sum = rest[blocks + 1 :]
    scale = 1.0 / math.sqrt(HEAD)
    key_at = lax.broadcasted_iota(jnp.int32, (BLOCK, BLOCK), 0)
    query_at = lax.broadcasted_iota(jnp.int32, (BLOCK, BLOCK), 1)
    causal = key_at <= query_at
    far_at = lax.broadcasted_iota(jnp.int32, (count, BLOCK), 0)
    half = HEAD // 2
    for sub in range(per_step):
        head = pl.program_id(0) * per_step + sub
        lanes = slice(sub * HEAD, (sub + 1) * HEAD)
        both = dot(pull_ref[...], far_ref[:, lanes]).astype(jnp.bfloat16)
        far_k, far_v = both[:count], both[count:]
        span = seg[head] * blocks
        p_far, d_far, q_all, g_all = [], [], [], []
        for k in range(blocks):
            rows = pl.ds(pl.multiple_of(info[k] * BLOCK, BLOCK), BLOCK)
            block = info[blocks + k]
            low = block & (-span)
            cq, sq, ck, sk = cq_ref[rows, :], sq_ref[rows, :], ck_ref[rows, :], sk_ref[rows, :]
            raw_q = q_ref[rows, lanes].astype(jnp.float32)
            raw_k = k_ref[rows, lanes].astype(jnp.float32)
            tq = (raw_q * cq + pltpu.roll(raw_q, half, 1) * sq).astype(jnp.bfloat16)
            tk = (raw_k * ck + pltpu.roll(raw_k, half, 1) * sk).astype(jnp.bfloat16)
            grad = g_ref[rows, lanes]
            keys = jnp.concatenate([tk, far_k], axis=0)
            vals = jnp.concatenate([v_ref[rows, lanes], far_v], axis=0)
            score = dot(keys, tq, NT)
            allowed = (far_at >= low) & (far_at < block)
            score = jnp.concatenate(
                [
                    jnp.where(causal, score[:BLOCK], -jnp.inf),
                    jnp.where(allowed, score[BLOCK:], -jnp.inf),
                ],
                axis=0,
            )
            top = jnp.max(score, axis=0, keepdims=True)
            weight = jnp.exp2((score - top) * (scale * LOG2E))
            prob = weight * (1.0 / jnp.sum(weight, axis=0, keepdims=True))
            p16 = prob.astype(jnp.bfloat16)
            dprob = dot(vals, grad, NT)
            delta = jnp.sum(p16.astype(jnp.float32) * dprob, axis=0, keepdims=True)
            d16 = (prob * (dprob - delta)).astype(jnp.bfloat16)
            out = dot(p16, vals, TN)
            dq = dot(d16, keys, TN) * scale
            dk = dot(d16[:BLOCK], tq) * scale
            dv = dot(p16[:BLOCK], grad)
            near_k[k] = dk
            near_v[k] = dv
            o_ref = outs[k]
            o_ref[0, :, lanes] = out.astype(jnp.bfloat16)
            o_ref[1, :, lanes] = (dq * cq - pltpu.roll(dq, half, 1) * sq).astype(jnp.bfloat16)
            o_ref[2, :, lanes] = (dk * ck - pltpu.roll(dk, half, 1) * sk).astype(jnp.bfloat16)
            o_ref[3, :, lanes] = dv.astype(jnp.bfloat16)
            p_far.append(p16[BLOCK:])
            d_far.append(d16[BLOCK:])
            q_all.append(tq)
            g_all.append(grad)
        far_sum[:count] = (
            dot(jnp.concatenate(d_far, axis=1), jnp.concatenate(q_all, axis=0)) * scale
        )
        far_sum[count:] = dot(jnp.concatenate(p_far, axis=1), jnp.concatenate(g_all, axis=0))
        at = phase[head]
        for k in range(blocks):
            block = info[blocks + k]
            far_sum[pl.ds(block, 1), :] = far_sum[pl.ds(block, 1), :] + near_k[k, pl.ds(at, 1), :]
            far_sum[pl.ds(count + block, 1), :] = (
                far_sum[pl.ds(count + block, 1), :] + near_v[k, pl.ds(at, 1), :]
            )
        pay_ref[:, lanes] = dot(push_ref[...], far_sum[...].astype(jnp.bfloat16)).astype(
            jnp.bfloat16
        )


def finish_kernel(heads, blocks, phase, slot, got_ref, cos_ref, sin_ref, *rest):
    parts = rest[:blocks]
    finals = rest[blocks : blocks + 4]
    room, load, save = rest[blocks + 4 :]
    for k in range(blocks):
        pltpu.make_async_copy(parts[k], room.at[slot[k]], load.at[k]).start()
    senders = got_ref.shape[0]
    total = got_ref[0].astype(jnp.float32)
    for sender in range(1, senders):
        total = total + got_ref[sender].astype(jnp.float32)
    far_k, far_v = total[:blocks], total[blocks:]
    for k in range(blocks):
        pltpu.make_async_copy(parts[k], room.at[slot[k]], load.at[k]).wait()
    for k in range(blocks):
        for t in range(2):
            rows = pl.ds(k * BLOCK, BLOCK)
            pltpu.make_async_copy(room.at[k, t], finals[t].at[rows, :], save.at[t, k]).start()
    spot = lax.broadcasted_iota(jnp.int32, (16, HEAD), 0)
    for head in range(heads):
        at = phase[head]
        start = pl.multiple_of(at // 16 * 16, 16)
        lanes = slice(head * HEAD, (head + 1) * HEAD)
        turned = far_k[:, lanes] * cos_ref[:, lanes] - pltpu.roll(
            far_k[:, lanes], HEAD // 2, 1
        ) * sin_ref[:, lanes]
        for k in range(blocks):
            for t, row in ((2, turned[k : k + 1]), (3, far_v[k : k + 1, lanes])):
                tile = room[k, t, pl.ds(start, 16), lanes].astype(jnp.float32)
                room[k, t, pl.ds(start, 16), lanes] = jnp.where(
                    spot == at - start, row, tile
                ).astype(jnp.bfloat16)
    for k in range(blocks):
        for t in range(2, 4):
            rows = pl.ds(k * BLOCK, BLOCK)
            pltpu.make_async_copy(room.at[k, t], finals[t].at[rows, :], save.at[t, k]).start()
    for k in range(blocks):
        for t in range(4):
            rows = pl.ds(k * BLOCK, BLOCK)
            pltpu.make_async_copy(room.at[k, t], finals[t].at[rows, :], save.at[t, k]).wait()


def local(queries, keys, values, output_gradient, dilation_phase, segment_device_count, owner):
    rows, width = queries.shape
    heads = width // HEAD
    blocks = rows // BLOCK
    bal_size = lax.axis_size("bal")
    devices = lax.axis_size("ctx") * bal_size
    total = rows * devices
    count = owner.shape[0]
    assert blocks == bal_size and bal_size & (bal_size - 1) == 0
    bal = lax.axis_index("bal")
    device = lax.axis_index("ctx") * bal_size + bal
    big = pltpu.CompilerParams(vmem_limit_bytes=50 * 1024 * 1024)
    smem = pl.BlockSpec(memory_space=pltpu.SMEM)

    steps = jnp.arange(blocks, dtype=jnp.int32)
    held = device * blocks + steps
    goes_to = lax.dynamic_slice_in_dim(owner, device * blocks, blocks) // blocks % bal_size
    partner = steps ^ bal
    which = jnp.sum(jnp.where(goes_to[None, :] == partner[:, None], steps[None, :], 0), axis=1)
    info = jnp.concatenate([which, device * blocks + which]).astype(jnp.int32)
    comes_from = jnp.sum(
        jnp.where(
            owner[None, :] == held[:, None], jnp.arange(count, dtype=jnp.int32)[None, :], 0
        ),
        axis=1,
    )

    positions = (held[:, None] * BLOCK + jnp.arange(BLOCK, dtype=jnp.int32)[None, :]).reshape(rows)
    cq, sq, ck, sk = tables(positions, total)

    picked = pl.pallas_call(
        functools.partial(pick_kernel, heads, blocks),
        grid=(blocks,),
        in_specs=[
            smem,
            pl.BlockSpec((BLOCK, width), lambda i: (i, 0)),
            pl.BlockSpec((BLOCK, width), lambda i: (i, 0)),
        ],
        out_specs=pl.BlockSpec((2 * blocks, width), lambda i: (0, 0)),
        out_shape=jax.ShapeDtypeStruct((2 * blocks, width), jnp.float32),
        compiler_params=big,
    )(dilation_phase, keys, values)
    own_phase = (held[:, None] * BLOCK + dilation_phase[None, :]).astype(jnp.int32)
    _, _, pick_cos, pick_sin = tables(own_phase, total)
    raw = picked[:blocks].reshape(blocks, heads, HEAD)
    raw = raw * pick_cos + jnp.roll(raw, HEAD // 2, axis=-1) * pick_sin
    own_far = jnp.concatenate([raw.reshape(blocks, width), picked[blocks:]], axis=0)
    own_far = own_far.astype(jnp.bfloat16)
    far = lax.all_gather(own_far, ("ctx", "bal"), axis=0, tiled=True)

    side = 2 * count
    wide = jnp.arange(side, dtype=jnp.int32)
    tall = wide[:, None]
    wide = wide[None, :]
    source = tall % count
    pull = (
        wide == source // blocks * (2 * blocks) + tall // count * blocks + source % blocks
    ).astype(jnp.bfloat16)
    lands = owner // blocks * (2 * blocks) + owner % blocks
    push = (jnp.concatenate([lands, lands + blocks])[None, :] == tall).astype(jnp.bfloat16)

    per_step = 2 if heads % 2 == 0 else 1
    columns = per_step * HEAD
    column = lambda h: (0, h)
    fixed = lambda h: (0, 0)
    tensor = pl.BlockSpec((rows, columns), column)
    square = pl.BlockSpec((side, side), fixed)
    table = pl.BlockSpec((rows, HEAD), fixed)
    part = pl.BlockSpec((4, BLOCK, columns), lambda h: (0, 0, h))
    results = pl.pallas_call(
        functools.partial(attend_kernel, per_step, blocks, count),
        grid=(heads // per_step,),
        in_specs=[smem] * 3
        + [tensor] * 4
        + [pl.BlockSpec((side, columns), column), square, square]
        + [table] * 4,
        out_specs=[part] * blocks + [pl.BlockSpec((side, columns), column)],
        out_shape=[jax.ShapeDtypeStruct((4, BLOCK, width), jnp.bfloat16)] * blocks
        + [jax.ShapeDtypeStruct((side, width), jnp.bfloat16)],
        scratch_shapes=[
            pltpu.VMEM((blocks, BLOCK, HEAD), jnp.float32),
            pltpu.VMEM((blocks, BLOCK, HEAD), jnp.float32),
            pltpu.VMEM((side, HEAD), jnp.float32),
        ],
        compiler_params=big,
    )(
        info,
        dilation_phase,
        segment_device_count,
        queries,
        keys,
        values,
        output_gradient,
        far,
        pull,
        push,
        cq,
        sq,
        ck,
        sk,
    )
    parts, payload = list(results[:blocks]), results[blocks]
    got = lax.all_to_all(
        payload.reshape(devices, 2 * blocks, width),
        ("ctx", "bal"),
        split_axis=0,
        concat_axis=0,
        tiled=True,
    )
    for k in range(1, blocks):
        parts[k] = lax.ppermute(parts[k], "bal", [(i, i ^ k) for i in range(bal_size)])

    new_phase = (comes_from[:, None] * BLOCK + dilation_phase[None, :]).astype(jnp.int32)
    _, _, new_cos, new_sin = tables(new_phase, total)
    vmem = pl.BlockSpec(memory_space=pltpu.VMEM)
    anywhere = pl.BlockSpec(memory_space=pl.ANY)
    return tuple(
        pl.pallas_call(
            functools.partial(finish_kernel, heads, blocks),
            in_specs=[smem, smem, vmem, vmem, vmem] + [anywhere] * blocks,
            out_specs=[anywhere] * 4,
            out_shape=[jax.ShapeDtypeStruct((rows, width), jnp.bfloat16)] * 4,
            scratch_shapes=[
                pltpu.VMEM((blocks, 4, BLOCK, width), jnp.bfloat16),
                pltpu.SemaphoreType.DMA((blocks,)),
                pltpu.SemaphoreType.DMA((4, blocks)),
            ],
            compiler_params=big,
        )(
            dilation_phase,
            partner.astype(jnp.int32),
            got,
            new_cos.reshape(blocks, width),
            new_sin.reshape(blocks, width),
            *parts,
        )
    )


def solution(mesh):
    token = P(("groups", "ctx", "bal"), "head")
    return jax.shard_map(
        local,
        mesh=mesh,
        in_specs=(token, token, token, token, P("head"), P("head"), P("groups")),
        out_specs=(token, token, token, token),
        check_vma=False,
    )
```

```python
import functools
import math

import jax
import jax.numpy as jnp
from jax import lax
from jax.experimental import pallas as pl
from jax.experimental.pallas import tpu as pltpu
from jax.sharding import PartitionSpec as P

BLOCK = 128
HEAD = 128
LOG2E = 1.4426950408889634
NT = (((1,), (1,)), ((), ()))
TN = (((0,), (0,)), ((), ()))


def tables(positions, total):
    half = HEAD // 2
    pair = jnp.arange(half, dtype=jnp.float32)
    inverse = jnp.exp(pair * (-2.0 * math.log(10000.0) / HEAD))
    where = positions.astype(jnp.float32)[..., None]
    angles = where * inverse
    base = (2.0 * pair / HEAD + 0.4) / 1.4
    growth = jnp.exp((2.0 * where - total) / total * jnp.log(base))
    cosine, sine = jnp.cos(angles), jnp.sin(angles)

    def pack(scale):
        first, second = cosine * scale, sine * scale
        return (
            jnp.concatenate([first, first], axis=-1),
            jnp.concatenate([-second, second], axis=-1),
        )

    return pack(growth) + pack(1.0 / growth)


def dot(left, right, dims=None):
    if dims is None:
        dims = (((1,), (0,)), ((), ()))
    return lax.dot_general(left, right, dims, preferred_element_type=jnp.float32)


def attend_kernel(
    per_step, blocks, count, first, relaid, info, phase, seg, far_ref, pull_ref, push_ref, *rest
):
    cq_ref, sq_ref, ck_ref, sk_ref = rest[:4]
    own = rest[4:8]
    rest = rest[8:]
    if relaid:
        come, rest = rest[: blocks - 1], rest[blocks:]
        finals, rest = rest[:4], rest[4:]
    else:
        finals, rest = rest[:blocks], rest[blocks:]
    pay_ref, near_k, near_v, far_sum = rest
    scale = 1.0 / math.sqrt(HEAD)
    key_at = lax.broadcasted_iota(jnp.int32, (BLOCK, BLOCK), 0)
    query_at = lax.broadcasted_iota(jnp.int32, (BLOCK, BLOCK), 1)
    causal = key_at <= query_at
    far_at = lax.broadcasted_iota(jnp.int32, (count, BLOCK), 0)
    half = HEAD // 2
    for sub in range(per_step):
        head = first + pl.program_id(0) * per_step + sub
        lanes = slice(sub * HEAD, (sub + 1) * HEAD)
        both = dot(pull_ref[...], far_ref[:, lanes]).astype(jnp.bfloat16)
        far_k, far_v = both[:count], both[count:]
        span = seg[head] * blocks
        p_far, d_far, q_all, g_all = [], [], [], []
        for k in range(blocks):
            if relaid:
                rows = slice(k * BLOCK, (k + 1) * BLOCK)
                source = [ref[:, lanes] for ref in own]
                if k:
                    source = [come[k - 1][t, :, lanes] for t in range(4)]
            else:
                rows = pl.ds(pl.multiple_of(info[k] * BLOCK, BLOCK), BLOCK)
                source = [ref[rows, lanes] for ref in own]
            block = info[blocks + k]
            low = block & (-span)
            cq, sq, ck, sk = cq_ref[rows, :], sq_ref[rows, :], ck_ref[rows, :], sk_ref[rows, :]
            raw_q, raw_k, value, grad = source
            raw_q = raw_q.astype(jnp.float32)
            raw_k = raw_k.astype(jnp.float32)
            tq = (raw_q * cq + pltpu.roll(raw_q, half, 1) * sq).astype(jnp.bfloat16)
            tk = (raw_k * ck + pltpu.roll(raw_k, half, 1) * sk).astype(jnp.bfloat16)
            keys = jnp.concatenate([tk, far_k], axis=0)
            vals = jnp.concatenate([value, far_v], axis=0)
            score = dot(keys, tq, NT)
            allowed = (far_at >= low) & (far_at < block)
            score = jnp.concatenate(
                [
                    jnp.where(causal, score[:BLOCK], -jnp.inf),
                    jnp.where(allowed, score[BLOCK:], -jnp.inf),
                ],
                axis=0,
            )
            top = jnp.max(score, axis=0, keepdims=True)
            weight = jnp.exp2((score - top) * (scale * LOG2E))
            prob = weight * (1.0 / jnp.sum(weight, axis=0, keepdims=True))
            p16 = prob.astype(jnp.bfloat16)
            dprob = dot(vals, grad, NT)
            delta = jnp.sum(p16.astype(jnp.float32) * dprob, axis=0, keepdims=True)
            d16 = (prob * (dprob - delta)).astype(jnp.bfloat16)
            out = dot(p16, vals, TN)
            dq = dot(d16, keys, TN) * scale
            dk = dot(d16[:BLOCK], tq) * scale
            dv = dot(p16[:BLOCK], grad)
            near_k[k] = dk
            near_v[k] = dv
            made = (
                out,
                dq * cq - pltpu.roll(dq, half, 1) * sq,
                dk * ck - pltpu.roll(dk, half, 1) * sk,
                dv,
            )
            for t in range(4):
                if relaid:
                    finals[t][info[2 * blocks + k], :, lanes] = made[t].astype(jnp.bfloat16)
                else:
                    finals[k][t, :, lanes] = made[t].astype(jnp.bfloat16)
            p_far.append(p16[BLOCK:])
            d_far.append(d16[BLOCK:])
            q_all.append(tq)
            g_all.append(grad)
        far_sum[:count] = (
            dot(jnp.concatenate(d_far, axis=1), jnp.concatenate(q_all, axis=0)) * scale
        )
        far_sum[count:] = dot(jnp.concatenate(p_far, axis=1), jnp.concatenate(g_all, axis=0))
        at = phase[head]
        for k in range(blocks):
            block = info[blocks + k]
            far_sum[pl.ds(block, 1), :] = far_sum[pl.ds(block, 1), :] + near_k[k, pl.ds(at, 1), :]
            far_sum[pl.ds(count + block, 1), :] = (
                far_sum[pl.ds(count + block, 1), :] + near_v[k, pl.ds(at, 1), :]
            )
        pay_ref[:, lanes] = dot(push_ref[...], far_sum[...].astype(jnp.bfloat16)).astype(
            jnp.bfloat16
        )


def pick_kernel(heads, blocks, phase, k_hbm, v_hbm, cos_ref, sin_ref, out_ref, k_ref, v_ref, load):
    moves = [
        pltpu.make_async_copy(k_hbm, k_ref, load.at[0]),
        pltpu.make_async_copy(v_hbm, v_ref, load.at[1]),
    ]
    for move in moves:
        move.start()
    spot = lax.broadcasted_iota(jnp.int32, (16, HEAD), 0)
    for t in range(2):
        moves[t].wait()
        ref = (k_ref, v_ref)[t]
        for head in range(heads):
            at = phase[head]
            start = pl.multiple_of(at // 16 * 16, 16)
            lanes = slice(head * HEAD, (head + 1) * HEAD)
            rows = []
            for k in range(blocks):
                tile = ref[pl.ds(pl.multiple_of(k * BLOCK + start, 16), 16), lanes]
                tile = jnp.where(spot == at - start, tile.astype(jnp.float32), 0.0)
                rows.append(jnp.sum(tile, axis=0, keepdims=True))
            row = jnp.concatenate(rows, axis=0)
            if t == 0:
                row = row * cos_ref[:, lanes] + pltpu.roll(row, HEAD // 2, 1) * sin_ref[:, lanes]
            out_ref[t * blocks : (t + 1) * blocks, lanes] = row


def pack_kernel(blocks, width, info, far_ref, *rest):
    inputs = rest[:4]
    outs = rest[4 : 4 + blocks - 1]
    sems = rest[4 + blocks - 1]
    for wait in (False, True):
        for k in reversed(range(1, blocks)):
            rows = pl.ds(pl.multiple_of(info[k] * BLOCK, BLOCK), BLOCK)
            for t in range(4):
                move = pltpu.make_async_copy(
                    inputs[t].at[rows, pl.ds(0, width)], outs[k - 1].at[t], sems.at[k - 1, t]
                )
                if wait:
                    move.wait()
                else:
                    move.start()


def finish_kernel(heads, blocks, first, phase, slot, got_ref, cos_ref, sin_ref, *rest):
    parts = rest[:blocks]
    finals = rest[blocks + 4 : blocks + 8]
    room, left, load, save, take, give = rest[blocks + 8 :]
    edge = first * HEAD

    def rows(k):
        return pl.ds(k * BLOCK, BLOCK)

    loads = [pltpu.make_async_copy(parts[k], room.at[slot[k]], load.at[k]) for k in range(blocks)]
    takes = [
        pltpu.make_async_copy(finals[2 + t].at[:, pl.ds(0, edge)], left.at[t], take.at[t])
        for t in range(2)
    ]
    gives = [
        pltpu.make_async_copy(left.at[t], finals[2 + t].at[:, pl.ds(0, edge)], give.at[t])
        for t in range(2)
    ]
    saves = [
        [
            pltpu.make_async_copy(
                room.at[k, t], finals[t].at[rows(k), pl.ds(edge, room.shape[-1])], save.at[t, k]
            )
            for k in range(blocks)
        ]
        for t in range(4)
    ]
    for move in loads + takes:
        move.start()
    senders = got_ref.shape[0]
    total = got_ref[0].astype(jnp.float32)
    for sender in range(1, senders):
        total = total + got_ref[sender].astype(jnp.float32)
    far_k, far_v = total[:blocks], total[blocks:]
    for move in loads:
        move.wait()
    for t in range(2):
        for move in saves[t]:
            move.start()
    for move in takes:
        move.wait()
    spot = lax.broadcasted_iota(jnp.int32, (16, HEAD), 0)
    for head in range(heads):
        at = phase[head]
        start = pl.multiple_of(at // 16 * 16, 16)
        lanes = slice(head * HEAD, (head + 1) * HEAD)
        turned = far_k[:, lanes] * cos_ref[:, lanes] - pltpu.roll(
            far_k[:, lanes], HEAD // 2, 1
        ) * sin_ref[:, lanes]
        for k in range(blocks):
            for t, row in ((0, turned[k : k + 1]), (1, far_v[k : k + 1, lanes])):
                if head < first:
                    spots = pl.ds(pl.multiple_of(k * BLOCK + start, 16), 16)
                    old = left[t, spots, lanes]
                else:
                    here = slice((head - first) * HEAD, (head - first + 1) * HEAD)
                    old = room[k, t + 2, pl.ds(start, 16), here]
                new = jnp.where(spot == at - start, row, old.astype(jnp.float32)).astype(
                    jnp.bfloat16
                )
                if head < first:
                    left[t, spots, lanes] = new
                else:
                    room[k, t + 2, pl.ds(start, 16), here] = new
    for t in range(2, 4):
        for move in saves[t]:
            move.start()
    for move in gives:
        move.start()
    for t in range(4):
        for move in saves[t]:
            move.wait()
    for move in gives:
        move.wait()


def local(queries, keys, values, output_gradient, dilation_phase, segment_device_count, owner):
    rows, width = queries.shape
    heads = width // HEAD
    blocks = rows // BLOCK
    bal_size = lax.axis_size("bal")
    devices = lax.axis_size("ctx") * bal_size
    total = rows * devices
    count = owner.shape[0]
    assert blocks == bal_size and bal_size & (bal_size - 1) == 0
    bal = lax.axis_index("bal")
    device = lax.axis_index("ctx") * bal_size + bal
    big = pltpu.CompilerParams(vmem_limit_bytes=50 * 1024 * 1024)
    smem = pl.BlockSpec(memory_space=pltpu.SMEM)
    vmem = pl.BlockSpec(memory_space=pltpu.VMEM)
    anywhere = pl.BlockSpec(memory_space=pl.ANY)

    def tokens_of(ids):
        return (ids[:, None] * BLOCK + jnp.arange(BLOCK, dtype=jnp.int32)[None, :]).reshape(rows)

    def swap(array, k):
        return lax.ppermute(array, "bal", [(i, i ^ k) for i in range(bal_size)])

    steps = jnp.arange(blocks, dtype=jnp.int32)
    held = device * blocks + steps
    goes_to = lax.dynamic_slice_in_dim(owner, device * blocks, blocks) // blocks % bal_size
    partner = steps ^ bal
    which = jnp.sum(jnp.where(goes_to[None, :] == partner[:, None], steps[None, :], 0), axis=1)
    info = jnp.concatenate([which, device * blocks + which]).astype(jnp.int32)
    comes_from = jnp.sum(
        jnp.where(
            owner[None, :] == held[:, None], jnp.arange(count, dtype=jnp.int32)[None, :], 0
        ),
        axis=1,
    )

    cq, sq, ck, sk = tables(tokens_of(held), total)
    own_phase = (held[:, None] * BLOCK + dilation_phase[None, :]).astype(jnp.int32)
    _, _, pick_cos, pick_sin = tables(own_phase, total)
    own_far = pl.pallas_call(
        functools.partial(pick_kernel, heads, blocks),
        in_specs=[smem, anywhere, anywhere, vmem, vmem],
        out_specs=vmem,
        out_shape=jax.ShapeDtypeStruct((2 * blocks, width), jnp.float32),
        scratch_shapes=[
            pltpu.VMEM((rows, width), jnp.bfloat16),
            pltpu.VMEM((rows, width), jnp.bfloat16),
            pltpu.SemaphoreType.DMA((2,)),
        ],
        compiler_params=big,
    )(
        dilation_phase,
        keys,
        values,
        pick_cos.reshape(blocks, width),
        pick_sin.reshape(blocks, width),
    ).astype(jnp.bfloat16)
    far = lax.all_to_all(
        jnp.broadcast_to(own_far[None], (devices, 2 * blocks, width)),
        ("ctx", "bal"),
        split_axis=0,
        concat_axis=0,
        tiled=True,
    ).reshape(devices * 2 * blocks, width)

    first = heads // 4 * 2
    last = heads - first
    edge = first * HEAD
    sent = pl.pallas_call(
        functools.partial(pack_kernel, blocks, edge),
        in_specs=[smem] + [anywhere] * 5,
        out_specs=[anywhere] * (blocks - 1),
        out_shape=[jax.ShapeDtypeStruct((4, BLOCK, edge), jnp.bfloat16)] * (blocks - 1),
        scratch_shapes=[pltpu.SemaphoreType.DMA((blocks - 1, 4))],
        compiler_params=big,
    )(info, own_far, queries, keys, values, output_gradient)
    come = [swap(sent[k - 1], k) for k in range(1, blocks)]

    side = 2 * count
    wide = jnp.arange(side, dtype=jnp.int32)
    tall = wide[:, None]
    wide = wide[None, :]
    source = tall % count
    pull = (
        wide == source // blocks * (2 * blocks) + tall // count * blocks + source % blocks
    ).astype(jnp.bfloat16)
    lands = owner // blocks * (2 * blocks) + owner % blocks
    push = (jnp.concatenate([lands, lands + blocks])[None, :] == tall).astype(jnp.bfloat16)

    per_step = 2
    columns = per_step * HEAD
    fixed = lambda h, *_: (0, 0)
    square = pl.BlockSpec((side, side), fixed)
    table = pl.BlockSpec((rows, HEAD), fixed)
    part = pl.BlockSpec((4, BLOCK, columns), lambda h, *_: (0, 0, h))
    scratch = [
        pltpu.VMEM((blocks, BLOCK, HEAD), jnp.float32),
        pltpu.VMEM((blocks, BLOCK, HEAD), jnp.float32),
        pltpu.VMEM((side, HEAD), jnp.float32),
    ]
    originals = (queries, keys, values, output_gradient)

    skip = first // per_step
    tensor = pl.BlockSpec((rows, columns), lambda h, *_: (0, h + skip))
    lane = pl.BlockSpec((side, columns), lambda h, *_: (0, h + skip))
    results = pl.pallas_call(
        functools.partial(attend_kernel, per_step, blocks, count, first, False),
        grid_spec=pltpu.PrefetchScalarGridSpec(
            num_scalar_prefetch=3,
            grid=(last // per_step,),
            in_specs=[lane, square, square] + [table] * 4 + [tensor] * 4,
            out_specs=[part] * blocks + [lane],
            scratch_shapes=scratch,
        ),
        out_shape=[jax.ShapeDtypeStruct((4, BLOCK, last * HEAD), jnp.bfloat16)] * blocks
        + [jax.ShapeDtypeStruct((side, width), jnp.bfloat16)],
        compiler_params=big,
    )(info, dilation_phase, segment_device_count, far, pull, push, cq, sq, ck, sk, *originals)
    parts, payload = list(results[:blocks]), results[blocks]
    for k in range(1, blocks):
        parts[k] = swap(parts[k], k)

    ids = (device ^ steps) * blocks
    came = jnp.sum(
        jnp.where(comes_from[None, :] // blocks * blocks == ids[:, None], comes_from[None, :], 0),
        axis=1,
    )
    moved = jnp.concatenate([which, came, partner]).astype(jnp.int32)
    cq, sq, ck, sk = tables(tokens_of(came), total)
    tensor = pl.BlockSpec((BLOCK, columns), lambda h, info, *_: (info[0], h))
    lane = pl.BlockSpec((side, columns), lambda h, *_: (0, h))
    whole = pl.BlockSpec((blocks, BLOCK, columns), lambda h, *_: (0, 0, h))
    results = pl.pallas_call(
        functools.partial(attend_kernel, per_step, blocks, count, 0, True),
        grid_spec=pltpu.PrefetchScalarGridSpec(
            num_scalar_prefetch=3,
            grid=(first // per_step,),
            in_specs=[lane, square, square]
            + [table] * 4
            + [tensor] * 4
            + [part] * (blocks - 1)
            + [anywhere],
            out_specs=[whole] * 4 + [lane],
            scratch_shapes=scratch,
        ),
        out_shape=[jax.ShapeDtypeStruct((blocks, BLOCK, width), jnp.bfloat16)] * 4
        + [jax.ShapeDtypeStruct((side, width), jnp.bfloat16)],
        input_output_aliases={3 + 3 + 4 + 4 + blocks - 1: 4},
        compiler_params=big,
    )(
        moved,
        dilation_phase,
        segment_device_count,
        far,
        pull,
        push,
        cq,
        sq,
        ck,
        sk,
        *originals,
        *come,
        payload,
    )
    finals, payload = [one.reshape(rows, width) for one in results[:4]], results[4]
    got = lax.all_to_all(
        payload.reshape(devices, 2 * blocks, width),
        ("ctx", "bal"),
        split_axis=0,
        concat_axis=0,
        tiled=True,
    )

    new_phase = (comes_from[:, None] * BLOCK + dilation_phase[None, :]).astype(jnp.int32)
    _, _, new_cos, new_sin = tables(new_phase, total)
    return tuple(
        pl.pallas_call(
            functools.partial(finish_kernel, heads, blocks, first),
            in_specs=[smem, smem, vmem, vmem, vmem] + [anywhere] * (blocks + 4),
            out_specs=[anywhere] * 4,
            out_shape=[jax.ShapeDtypeStruct((rows, width), jnp.bfloat16)] * 4,
            input_output_aliases={5 + blocks + t: t for t in range(4)},
            scratch_shapes=[
                pltpu.VMEM((blocks, 4, BLOCK, last * HEAD), jnp.bfloat16),
                pltpu.VMEM((2, rows, edge), jnp.bfloat16),
                pltpu.SemaphoreType.DMA((blocks,)),
                pltpu.SemaphoreType.DMA((4, blocks)),
                pltpu.SemaphoreType.DMA((2,)),
                pltpu.SemaphoreType.DMA((2,)),
            ],
            compiler_params=big,
        )(
            dilation_phase,
            partner.astype(jnp.int32),
            got,
            new_cos.reshape(blocks, width),
            new_sin.reshape(blocks, width),
            *parts,
            *finals,
        )
    )


def solution(mesh):
    token = P(("groups", "ctx", "bal"), "head")
    return jax.shard_map(
        local,
        mesh=mesh,
        in_specs=(token, token, token, token, P("head"), P("head"), P("groups")),
        out_specs=(token, token, token, token),
        check_vma=False,
    )
```

```python
import functools
import math

import jax
import jax.numpy as jnp
from jax import lax
from jax.experimental import pallas as pl
from jax.experimental.pallas import tpu as pltpu
from jax.sharding import PartitionSpec as P

BLOCK = 128
HEAD = 128
LOG2E = 1.4426950408889634
NT = (((1,), (1,)), ((), ()))
TN = (((0,), (0,)), ((), ()))


def tables(positions, total):
    half = HEAD // 2
    pair = jnp.arange(half, dtype=jnp.float32)
    inverse = jnp.exp(pair * (-2.0 * math.log(10000.0) / HEAD))
    where = positions.astype(jnp.float32)[..., None]
    angles = where * inverse
    base = (2.0 * pair / HEAD + 0.4) / 1.4
    growth = jnp.exp((2.0 * where - total) / total * jnp.log(base))
    cosine, sine = jnp.cos(angles), jnp.sin(angles)

    def pack(scale):
        first, second = cosine * scale, sine * scale
        return (
            jnp.concatenate([first, first], axis=-1),
            jnp.concatenate([-second, second], axis=-1),
        )

    return pack(growth) + pack(1.0 / growth)


def dot(left, right, dims=None):
    if dims is None:
        dims = (((1,), (0,)), ((), ()))
    return lax.dot_general(left, right, dims, preferred_element_type=jnp.float32)


def attend_kernel(
    per_step, blocks, count, first, relaid, info, phase, seg, far_ref, pull_ref, push_ref, *rest
):
    cq_ref, sq_ref, ck_ref, sk_ref = rest[:4]
    own = rest[4:8]
    rest = rest[8:]
    if relaid:
        come, rest = rest[: blocks - 1], rest[blocks:]
        finals, rest = rest[:4], rest[4:]
    else:
        finals, rest = rest[:blocks], rest[blocks:]
    pay_ref, near_k, near_v, far_sum = rest
    scale = 1.0 / math.sqrt(HEAD)
    key_at = lax.broadcasted_iota(jnp.int32, (BLOCK, BLOCK), 0)
    query_at = lax.broadcasted_iota(jnp.int32, (BLOCK, BLOCK), 1)
    causal = key_at <= query_at
    far_at = lax.broadcasted_iota(jnp.int32, (count, BLOCK), 0)
    half = HEAD // 2
    for sub in range(per_step):
        head = first + pl.program_id(0) * per_step + sub
        lanes = slice(sub * HEAD, (sub + 1) * HEAD)
        both = dot(pull_ref[...], far_ref[:, lanes]).astype(jnp.bfloat16)
        far_k, far_v = both[:count], both[count:]
        span = seg[head] * blocks
        p_far, d_far, q_all, g_all = [], [], [], []
        for k in range(blocks):
            if relaid:
                rows = slice(k * BLOCK, (k + 1) * BLOCK)
                source = [ref[:, lanes] for ref in own]
                if k:
                    source = [come[k - 1][t, :, lanes] for t in range(4)]
            else:
                rows = pl.ds(pl.multiple_of(info[k] * BLOCK, BLOCK), BLOCK)
                source = [ref[rows, lanes] for ref in own]
            block = info[blocks + k]
            low = block & (-span)
            cq, sq, ck, sk = cq_ref[rows, :], sq_ref[rows, :], ck_ref[rows, :], sk_ref[rows, :]
            raw_q, raw_k, value, grad = source
            raw_q = raw_q.astype(jnp.float32)
            raw_k = raw_k.astype(jnp.float32)
            tq = (raw_q * cq + pltpu.roll(raw_q, half, 1) * sq).astype(jnp.bfloat16)
            tk = (raw_k * ck + pltpu.roll(raw_k, half, 1) * sk).astype(jnp.bfloat16)
            keys = jnp.concatenate([tk, far_k], axis=0)
            vals = jnp.concatenate([value, far_v], axis=0)
            score = dot(keys, tq, NT)
            allowed = (far_at >= low) & (far_at < block)
            score = jnp.concatenate(
                [
                    jnp.where(causal, score[:BLOCK], -jnp.inf),
                    jnp.where(allowed, score[BLOCK:], -jnp.inf),
                ],
                axis=0,
            )
            top = jnp.max(score, axis=0, keepdims=True)
            weight = jnp.exp2((score - top) * (scale * LOG2E))
            prob = weight * (1.0 / jnp.sum(weight, axis=0, keepdims=True))
            p16 = prob.astype(jnp.bfloat16)
            dprob = dot(vals, grad, NT)
            delta = jnp.sum(p16.astype(jnp.float32) * dprob, axis=0, keepdims=True)
            d16 = (prob * (dprob - delta)).astype(jnp.bfloat16)
            out = dot(p16, vals, TN)
            dq = dot(d16, keys, TN) * scale
            dk = dot(d16[:BLOCK], tq) * scale
            dv = dot(p16[:BLOCK], grad)
            near_k[k] = dk
            near_v[k] = dv
            made = (
                out,
                dq * cq - pltpu.roll(dq, half, 1) * sq,
                dk * ck - pltpu.roll(dk, half, 1) * sk,
                dv,
            )
            for t in range(4):
                if relaid:
                    finals[t][info[2 * blocks + k], :, lanes] = made[t].astype(jnp.bfloat16)
                else:
                    finals[k][t, :, lanes] = made[t].astype(jnp.bfloat16)
            p_far.append(p16[BLOCK:])
            d_far.append(d16[BLOCK:])
            q_all.append(tq)
            g_all.append(grad)
        far_sum[:count] = (
            dot(jnp.concatenate(d_far, axis=1), jnp.concatenate(q_all, axis=0)) * scale
        )
        far_sum[count:] = dot(jnp.concatenate(p_far, axis=1), jnp.concatenate(g_all, axis=0))
        at = phase[head]
        for k in range(blocks):
            block = info[blocks + k]
            far_sum[pl.ds(block, 1), :] = far_sum[pl.ds(block, 1), :] + near_k[k, pl.ds(at, 1), :]
            far_sum[pl.ds(count + block, 1), :] = (
                far_sum[pl.ds(count + block, 1), :] + near_v[k, pl.ds(at, 1), :]
            )
        pay_ref[:, lanes] = dot(push_ref[...], far_sum[...].astype(jnp.bfloat16)).astype(
            jnp.bfloat16
        )


def pick_kernel(heads, blocks, phase, k_hbm, v_hbm, cos_ref, sin_ref, out_ref, k_ref, v_ref, load):
    moves = [
        pltpu.make_async_copy(k_hbm, k_ref, load.at[0]),
        pltpu.make_async_copy(v_hbm, v_ref, load.at[1]),
    ]
    for move in moves:
        move.start()
    spot = lax.broadcasted_iota(jnp.int32, (16, HEAD), 0)
    for t in range(2):
        moves[t].wait()
        ref = (k_ref, v_ref)[t]
        for head in range(heads):
            at = phase[head]
            start = pl.multiple_of(at // 16 * 16, 16)
            lanes = slice(head * HEAD, (head + 1) * HEAD)
            rows = []
            for k in range(blocks):
                tile = ref[pl.ds(pl.multiple_of(k * BLOCK + start, 16), 16), lanes]
                tile = jnp.where(spot == at - start, tile.astype(jnp.float32), 0.0)
                rows.append(jnp.sum(tile, axis=0, keepdims=True))
            row = jnp.concatenate(rows, axis=0)
            if t == 0:
                row = row * cos_ref[:, lanes] + pltpu.roll(row, HEAD // 2, 1) * sin_ref[:, lanes]
            out_ref[t * blocks : (t + 1) * blocks, lanes] = row


def pack_kernel(blocks, width, info, far_ref, *rest):
    inputs = rest[:4]
    outs = rest[4 : 3 + blocks]
    room, load, save = rest[3 + blocks :]
    order = [(k, t) for k in reversed(range(1, blocks)) for t in range(4)]

    def pull(k, t):
        rows = pl.ds(pl.multiple_of(info[k] * BLOCK, BLOCK), BLOCK)
        source = inputs[t].at[rows, pl.ds(0, width)]
        return pltpu.make_async_copy(source, room.at[k - 1, t], load.at[k - 1, t])

    def push(k, t):
        return pltpu.make_async_copy(room.at[k - 1, t], outs[k - 1].at[t], save.at[k - 1, t])

    for k, t in order:
        pull(k, t).start()
    for k, t in order:
        pull(k, t).wait()
        push(k, t).start()
    for k, t in order:
        push(k, t).wait()


def finish_kernel(heads, blocks, first, phase, slot, got_ref, cos_ref, sin_ref, *rest):
    parts = rest[:blocks]
    finals = rest[blocks + 4 : blocks + 8]
    room, left, load, save, take, give = rest[blocks + 8 :]
    edge = first * HEAD

    def rows(k):
        return pl.ds(k * BLOCK, BLOCK)

    loads = [pltpu.make_async_copy(parts[k], room.at[slot[k]], load.at[k]) for k in range(blocks)]
    takes = [
        pltpu.make_async_copy(finals[2 + t].at[:, pl.ds(0, edge)], left.at[t], take.at[t])
        for t in range(2)
    ]
    gives = [
        pltpu.make_async_copy(left.at[t], finals[2 + t].at[:, pl.ds(0, edge)], give.at[t])
        for t in range(2)
    ]
    saves = [
        [
            pltpu.make_async_copy(
                room.at[k, t], finals[t].at[rows(k), pl.ds(edge, room.shape[-1])], save.at[t, k]
            )
            for k in range(blocks)
        ]
        for t in range(4)
    ]
    for move in loads + takes:
        move.start()
    senders = got_ref.shape[0]
    total = got_ref[0].astype(jnp.float32)
    for sender in range(1, senders):
        total = total + got_ref[sender].astype(jnp.float32)
    far_k, far_v = total[:blocks], total[blocks:]
    for move in loads:
        move.wait()
    for t in range(2):
        for move in saves[t]:
            move.start()
    for move in takes:
        move.wait()
    spot = lax.broadcasted_iota(jnp.int32, (16, HEAD), 0)
    for head in range(heads):
        at = phase[head]
        start = pl.multiple_of(at // 16 * 16, 16)
        lanes = slice(head * HEAD, (head + 1) * HEAD)
        turned = far_k[:, lanes] * cos_ref[:, lanes] - pltpu.roll(
            far_k[:, lanes], HEAD // 2, 1
        ) * sin_ref[:, lanes]
        for k in range(blocks):
            for t, row in ((0, turned[k : k + 1]), (1, far_v[k : k + 1, lanes])):
                if head < first:
                    spots = pl.ds(pl.multiple_of(k * BLOCK + start, 16), 16)
                    old = left[t, spots, lanes]
                else:
                    here = slice((head - first) * HEAD, (head - first + 1) * HEAD)
                    old = room[k, t + 2, pl.ds(start, 16), here]
                new = jnp.where(spot == at - start, row, old.astype(jnp.float32)).astype(
                    jnp.bfloat16
                )
                if head < first:
                    left[t, spots, lanes] = new
                else:
                    room[k, t + 2, pl.ds(start, 16), here] = new
    for t in range(2, 4):
        for move in saves[t]:
            move.start()
    for move in gives:
        move.start()
    for t in range(4):
        for move in saves[t]:
            move.wait()
    for move in gives:
        move.wait()


def local(queries, keys, values, output_gradient, dilation_phase, segment_device_count, owner):
    rows, width = queries.shape
    heads = width // HEAD
    blocks = rows // BLOCK
    bal_size = lax.axis_size("bal")
    devices = lax.axis_size("ctx") * bal_size
    total = rows * devices
    count = owner.shape[0]
    assert blocks == bal_size and bal_size & (bal_size - 1) == 0
    bal = lax.axis_index("bal")
    device = lax.axis_index("ctx") * bal_size + bal
    big = pltpu.CompilerParams(vmem_limit_bytes=60 * 1024 * 1024)
    smem = pl.BlockSpec(memory_space=pltpu.SMEM)
    vmem = pl.BlockSpec(memory_space=pltpu.VMEM)
    anywhere = pl.BlockSpec(memory_space=pl.ANY)
    heavy = pl.CostEstimate(flops=20_000_000_000, bytes_accessed=60_000_000, transcendentals=0)

    def tokens_of(ids):
        return (ids[:, None] * BLOCK + jnp.arange(BLOCK, dtype=jnp.int32)[None, :]).reshape(rows)

    def swap(array, k):
        return lax.ppermute(array, "bal", [(i, i ^ k) for i in range(bal_size)])

    steps = jnp.arange(blocks, dtype=jnp.int32)
    held = device * blocks + steps
    goes_to = lax.dynamic_slice_in_dim(owner, device * blocks, blocks) // blocks % bal_size
    partner = steps ^ bal
    which = jnp.sum(jnp.where(goes_to[None, :] == partner[:, None], steps[None, :], 0), axis=1)
    info = jnp.concatenate([which, device * blocks + which]).astype(jnp.int32)
    comes_from = jnp.sum(
        jnp.where(
            owner[None, :] == held[:, None], jnp.arange(count, dtype=jnp.int32)[None, :], 0
        ),
        axis=1,
    )

    cq, sq, ck, sk = tables(tokens_of(held), total)
    own_phase = (held[:, None] * BLOCK + dilation_phase[None, :]).astype(jnp.int32)
    _, _, pick_cos, pick_sin = tables(own_phase, total)
    own_far = pl.pallas_call(
        functools.partial(pick_kernel, heads, blocks),
        in_specs=[smem, anywhere, anywhere, vmem, vmem],
        out_specs=vmem,
        out_shape=jax.ShapeDtypeStruct((2 * blocks, width), jnp.float32),
        scratch_shapes=[
            pltpu.VMEM((rows, width), jnp.bfloat16),
            pltpu.VMEM((rows, width), jnp.bfloat16),
            pltpu.SemaphoreType.DMA((2,)),
        ],
        compiler_params=big,
    )(
        dilation_phase,
        keys,
        values,
        pick_cos.reshape(blocks, width),
        pick_sin.reshape(blocks, width),
    ).astype(jnp.bfloat16)
    far = lax.all_to_all(
        jnp.broadcast_to(own_far[None], (devices, 2 * blocks, width)),
        ("ctx", "bal"),
        split_axis=0,
        concat_axis=0,
        tiled=True,
    ).reshape(devices * 2 * blocks, width)

    first = heads // 4 * 2
    last = heads - first
    edge = first * HEAD
    sent = pl.pallas_call(
        functools.partial(pack_kernel, blocks, edge),
        in_specs=[smem] + [anywhere] * 5,
        out_specs=[anywhere] * (blocks - 1),
        out_shape=[jax.ShapeDtypeStruct((4, BLOCK, edge), jnp.bfloat16)] * (blocks - 1),
        scratch_shapes=[
            pltpu.VMEM((blocks - 1, 4, BLOCK, edge), jnp.bfloat16),
            pltpu.SemaphoreType.DMA((blocks - 1, 4)),
            pltpu.SemaphoreType.DMA((blocks - 1, 4)),
        ],
        compiler_params=big,
    )(info, own_far, queries, keys, values, output_gradient)
    come = [swap(sent[k - 1], k) for k in range(1, blocks)]

    side = 2 * count
    wide = jnp.arange(side, dtype=jnp.int32)
    tall = wide[:, None]
    wide = wide[None, :]
    source = tall % count
    pull = (
        wide == source // blocks * (2 * blocks) + tall // count * blocks + source % blocks
    ).astype(jnp.bfloat16)
    lands = owner // blocks * (2 * blocks) + owner % blocks
    push = (jnp.concatenate([lands, lands + blocks])[None, :] == tall).astype(jnp.bfloat16)

    per_step = 2
    columns = per_step * HEAD
    fixed = lambda h, *_: (0, 0)
    square = pl.BlockSpec((side, side), fixed)
    table = pl.BlockSpec((rows, HEAD), fixed)
    part = pl.BlockSpec((4, BLOCK, columns), lambda h, *_: (0, 0, h))
    scratch = [
        pltpu.VMEM((blocks, BLOCK, HEAD), jnp.float32),
        pltpu.VMEM((blocks, BLOCK, HEAD), jnp.float32),
        pltpu.VMEM((side, HEAD), jnp.float32),
    ]
    originals = (queries, keys, values, output_gradient)

    skip = first // per_step
    tensor = pl.BlockSpec((rows, columns), lambda h, *_: (0, h + skip))
    lane = pl.BlockSpec((side, columns), lambda h, *_: (0, h + skip))
    results = pl.pallas_call(
        functools.partial(attend_kernel, per_step, blocks, count, first, False),
        grid_spec=pltpu.PrefetchScalarGridSpec(
            num_scalar_prefetch=3,
            grid=(last // per_step,),
            in_specs=[lane, square, square] + [table] * 4 + [tensor] * 4,
            out_specs=[part] * blocks + [lane],
            scratch_shapes=scratch,
        ),
        out_shape=[jax.ShapeDtypeStruct((4, BLOCK, last * HEAD), jnp.bfloat16)] * blocks
        + [jax.ShapeDtypeStruct((side, width), jnp.bfloat16)],
        compiler_params=big,
        cost_estimate=heavy,
    )(info, dilation_phase, segment_device_count, far, pull, push, cq, sq, ck, sk, *originals)
    parts, payload = list(results[:blocks]), results[blocks]
    for k in range(1, blocks):
        parts[k] = swap(parts[k], k)

    ids = (device ^ steps) * blocks
    came = jnp.sum(
        jnp.where(comes_from[None, :] // blocks * blocks == ids[:, None], comes_from[None, :], 0),
        axis=1,
    )
    moved = jnp.concatenate([which, came, partner]).astype(jnp.int32)
    cq, sq, ck, sk = tables(tokens_of(came), total)
    tensor = pl.BlockSpec((BLOCK, columns), lambda h, info, *_: (info[0], h))
    lane = pl.BlockSpec((side, columns), lambda h, *_: (0, h))
    whole = pl.BlockSpec((blocks, BLOCK, columns), lambda h, *_: (0, 0, h))
    results = pl.pallas_call(
        functools.partial(attend_kernel, per_step, blocks, count, 0, True),
        grid_spec=pltpu.PrefetchScalarGridSpec(
            num_scalar_prefetch=3,
            grid=(first // per_step,),
            in_specs=[lane, square, square]
            + [table] * 4
            + [tensor] * 4
            + [part] * (blocks - 1)
            + [anywhere],
            out_specs=[whole] * 4 + [lane],
            scratch_shapes=scratch,
        ),
        out_shape=[jax.ShapeDtypeStruct((blocks, BLOCK, width), jnp.bfloat16)] * 4
        + [jax.ShapeDtypeStruct((side, width), jnp.bfloat16)],
        input_output_aliases={3 + 3 + 4 + 4 + blocks - 1: 4},
        compiler_params=big,
        cost_estimate=heavy,
    )(
        moved,
        dilation_phase,
        segment_device_count,
        far,
        pull,
        push,
        cq,
        sq,
        ck,
        sk,
        *originals,
        *come,
        payload,
    )
    finals, payload = [one.reshape(rows, width) for one in results[:4]], results[4]
    got = lax.all_to_all(
        payload.reshape(devices, 2 * blocks, width),
        ("ctx", "bal"),
        split_axis=0,
        concat_axis=0,
        tiled=True,
    )

    new_phase = (comes_from[:, None] * BLOCK + dilation_phase[None, :]).astype(jnp.int32)
    _, _, new_cos, new_sin = tables(new_phase, total)
    return tuple(
        pl.pallas_call(
            functools.partial(finish_kernel, heads, blocks, first),
            in_specs=[smem, smem, vmem, vmem, vmem] + [anywhere] * (blocks + 4),
            out_specs=[anywhere] * 4,
            out_shape=[jax.ShapeDtypeStruct((rows, width), jnp.bfloat16)] * 4,
            input_output_aliases={5 + blocks + t: t for t in range(4)},
            scratch_shapes=[
                pltpu.VMEM((blocks, 4, BLOCK, last * HEAD), jnp.bfloat16),
                pltpu.VMEM((2, rows, edge), jnp.bfloat16),
                pltpu.SemaphoreType.DMA((blocks,)),
                pltpu.SemaphoreType.DMA((4, blocks)),
                pltpu.SemaphoreType.DMA((2,)),
                pltpu.SemaphoreType.DMA((2,)),
            ],
            compiler_params=big,
        )(
            dilation_phase,
            partner.astype(jnp.int32),
            got,
            new_cos.reshape(blocks, width),
            new_sin.reshape(blocks, width),
            *parts,
            *finals,
        )
    )


def solution(mesh):
    token = P(("groups", "ctx", "bal"), "head")
    return jax.shard_map(
        local,
        mesh=mesh,
        in_specs=(token, token, token, token, P("head"), P("head"), P("groups")),
        out_specs=(token, token, token, token),
        check_vma=False,
    )
```

```python
import functools
import math

import jax
import jax.numpy as jnp
from jax import lax
from jax.experimental import pallas as pl
from jax.experimental.pallas import tpu as pltpu
from jax.sharding import PartitionSpec as P

BLOCK = 128
HEAD = 128
LOG2E = 1.4426950408889634
NT = (((1,), (1,)), ((), ()))
TN = (((0,), (0,)), ((), ()))


def tables(positions, total):
    half = HEAD // 2
    pair = jnp.arange(half, dtype=jnp.float32)
    inverse = jnp.exp(pair * (-2.0 * math.log(10000.0) / HEAD))
    where = positions.astype(jnp.float32)[..., None]
    angles = where * inverse
    base = (2.0 * pair / HEAD + 0.4) / 1.4
    growth = jnp.exp((2.0 * where - total) / total * jnp.log(base))
    cosine, sine = jnp.cos(angles), jnp.sin(angles)

    def pack(scale):
        first, second = cosine * scale, sine * scale
        return (
            jnp.concatenate([first, first], axis=-1),
            jnp.concatenate([-second, second], axis=-1),
        )

    return pack(growth) + pack(1.0 / growth)


def dot(left, right, dims=None):
    if dims is None:
        dims = (((1,), (0,)), ((), ()))
    return lax.dot_general(left, right, dims, preferred_element_type=jnp.float32)


def attend_kernel(
    per_step, blocks, count, first, relaid, info, phase, seg, far_ref, pull_ref, push_ref, *rest
):
    cq_ref, sq_ref, ck_ref, sk_ref = rest[:4]
    own = rest[4:8]
    rest = rest[8:]
    if relaid:
        come, rest = rest[: blocks - 1], rest[blocks - 1 + relaid :]
        finals, rest = rest[:4], rest[4:]
    else:
        finals, rest = rest[:blocks], rest[blocks:]
    pay_ref, near_k, near_v, far_sum = rest
    scale = 1.0 / math.sqrt(HEAD)
    key_at = lax.broadcasted_iota(jnp.int32, (BLOCK, BLOCK), 0)
    query_at = lax.broadcasted_iota(jnp.int32, (BLOCK, BLOCK), 1)
    causal = key_at <= query_at
    far_at = lax.broadcasted_iota(jnp.int32, (count, BLOCK), 0)
    half = HEAD // 2
    for sub in range(per_step):
        head = first + pl.program_id(0) * per_step + sub
        lanes = slice(sub * HEAD, (sub + 1) * HEAD)
        both = dot(pull_ref[...], far_ref[:, lanes]).astype(jnp.bfloat16)
        far_k, far_v = both[:count], both[count:]
        span = seg[head] * blocks
        p_far, d_far, q_all, g_all = [], [], [], []
        for k in range(blocks):
            if relaid:
                rows = slice(k * BLOCK, (k + 1) * BLOCK)
                source = [ref[:, lanes] for ref in own]
                if k:
                    source = [come[k - 1][t, :, lanes] for t in range(4)]
            else:
                rows = pl.ds(pl.multiple_of(info[k] * BLOCK, BLOCK), BLOCK)
                source = [ref[rows, lanes] for ref in own]
            block = info[blocks + k]
            low = block & (-span)
            cq, sq, ck, sk = cq_ref[rows, :], sq_ref[rows, :], ck_ref[rows, :], sk_ref[rows, :]
            raw_q, raw_k, value, grad = source
            raw_q = raw_q.astype(jnp.float32)
            raw_k = raw_k.astype(jnp.float32)
            tq = (raw_q * cq + pltpu.roll(raw_q, half, 1) * sq).astype(jnp.bfloat16)
            tk = (raw_k * ck + pltpu.roll(raw_k, half, 1) * sk).astype(jnp.bfloat16)
            keys = jnp.concatenate([tk, far_k], axis=0)
            vals = jnp.concatenate([value, far_v], axis=0)
            score = dot(keys, tq, NT)
            allowed = (far_at >= low) & (far_at < block)
            score = jnp.concatenate(
                [
                    jnp.where(causal, score[:BLOCK], -jnp.inf),
                    jnp.where(allowed, score[BLOCK:], -jnp.inf),
                ],
                axis=0,
            )
            top = jnp.max(score, axis=0, keepdims=True)
            weight = jnp.exp2((score - top) * (scale * LOG2E))
            prob = weight * (1.0 / jnp.sum(weight, axis=0, keepdims=True))
            p16 = prob.astype(jnp.bfloat16)
            dprob = dot(vals, grad, NT)
            delta = jnp.sum(p16.astype(jnp.float32) * dprob, axis=0, keepdims=True)
            d16 = (prob * (dprob - delta)).astype(jnp.bfloat16)
            out = dot(p16, vals, TN)
            dq = dot(d16, keys, TN) * scale
            dk = dot(d16[:BLOCK], tq) * scale
            dv = dot(p16[:BLOCK], grad)
            near_k[k] = dk
            near_v[k] = dv
            made = (
                out,
                dq * cq - pltpu.roll(dq, half, 1) * sq,
                dk * ck - pltpu.roll(dk, half, 1) * sk,
                dv,
            )
            for t in range(4):
                if relaid:
                    finals[t][info[2 * blocks + k], :, lanes] = made[t].astype(jnp.bfloat16)
                else:
                    finals[k][t, :, lanes] = made[t].astype(jnp.bfloat16)
            p_far.append(p16[BLOCK:])
            d_far.append(d16[BLOCK:])
            q_all.append(tq)
            g_all.append(grad)
        far_sum[:count] = (
            dot(jnp.concatenate(d_far, axis=1), jnp.concatenate(q_all, axis=0)) * scale
        )
        far_sum[count:] = dot(jnp.concatenate(p_far, axis=1), jnp.concatenate(g_all, axis=0))
        at = phase[head]
        for k in range(blocks):
            block = info[blocks + k]
            far_sum[pl.ds(block, 1), :] = far_sum[pl.ds(block, 1), :] + near_k[k, pl.ds(at, 1), :]
            far_sum[pl.ds(count + block, 1), :] = (
                far_sum[pl.ds(count + block, 1), :] + near_v[k, pl.ds(at, 1), :]
            )
        pay_ref[:, lanes] = dot(push_ref[...], far_sum[...].astype(jnp.bfloat16)).astype(
            jnp.bfloat16
        )


def pick_kernel(
    heads, blocks, phase, k_hbm, v_hbm, cos_ref, sin_ref, after, out_ref, k_ref, v_ref, row_ref,
    load, save
):
    moves = [
        pltpu.make_async_copy(k_hbm, k_ref, load.at[0]),
        pltpu.make_async_copy(v_hbm, v_ref, load.at[1]),
    ]
    for move in moves:
        move.start()
    for move in moves:
        move.wait()
    spot = lax.broadcasted_iota(jnp.int32, (16, HEAD), 0)
    for head in range(heads):
        at = phase[head]
        start = pl.multiple_of(at // 16 * 16, 16)
        lanes = slice(head * HEAD, (head + 1) * HEAD)
        both = []
        for ref in (k_ref, v_ref):
            rows = []
            for k in range(blocks):
                tile = ref[pl.ds(pl.multiple_of(k * BLOCK + start, 16), 16), lanes]
                tile = jnp.where(spot == at - start, tile.astype(jnp.float32), 0.0)
                rows.append(jnp.sum(tile, axis=0, keepdims=True))
            both.append(jnp.concatenate(rows, axis=0))
        key, value = both
        key = key * cos_ref[:, lanes] + pltpu.roll(key, HEAD // 2, 1) * sin_ref[:, lanes]
        row_ref[:, lanes] = jnp.concatenate([key, value], axis=0).astype(jnp.bfloat16)
    copies = [
        pltpu.make_async_copy(row_ref, out_ref.at[d], save.at[d]) for d in range(out_ref.shape[0])
    ]
    for copy in copies:
        copy.start()
    for copy in copies:
        copy.wait()


def pack_kernel(jobs, info, after, *rest):
    number = len(jobs)
    inputs, rest = rest[:4], rest[4:]
    outs, rooms, (load, save) = rest[:number], rest[number : 2 * number], rest[2 * number :]
    order = [(job, t) for job in range(number) for t in range(4)]

    def fetch(job, t):
        k, start, width = jobs[job]
        rows = pl.ds(pl.multiple_of(info[k] * BLOCK, BLOCK), BLOCK)
        source = inputs[t].at[rows, pl.ds(start, width)]
        return pltpu.make_async_copy(source, rooms[job].at[t], load.at[job, t])

    def store(job, t):
        return pltpu.make_async_copy(rooms[job].at[t], outs[job].at[t], save.at[job, t])

    for job, t in order:
        fetch(job, t).start()
    for job, t in order:
        fetch(job, t).wait()
        store(job, t).start()
    for job, t in order:
        store(job, t).wait()


def place_kernel(blocks, edge, slot, *rest):
    parts = rest[:blocks]
    finals = rest[blocks + 4 : blocks + 8]
    room, load, save = rest[blocks + 8 :]
    width = room.shape[-1]

    def save_of(k, t):
        where = finals[t].at[pl.ds(k * BLOCK, BLOCK), pl.ds(edge, width)]
        return pltpu.make_async_copy(room.at[k, t], where, save.at[k, t])

    loads = [pltpu.make_async_copy(parts[k], room.at[slot[k]], load.at[k]) for k in range(blocks)]
    for move in loads:
        move.start()
    for move in loads:
        move.wait()
    for k in range(blocks):
        for t in range(4):
            save_of(k, t).start()
    for k in range(blocks):
        for t in range(4):
            save_of(k, t).wait()


def patch_kernel(
    heads, blocks, phase, got_hbm, cos_ref, sin_ref, dk_in, dv_in, dk_out, dv_out, got, room, get,
    load, save
):
    def rows(k):
        return pl.ds(k * BLOCK, BLOCK)

    outs = (dk_out, dv_out)
    order = [(k, t) for k in range(blocks) for t in range(2)]
    fetch = pltpu.make_async_copy(got_hbm, got, get)
    loads = [pltpu.make_async_copy(outs[t].at[rows(k)], room.at[t, k], load.at[t, k]) for k, t in order]
    saves = [pltpu.make_async_copy(room.at[t, k], outs[t].at[rows(k)], save.at[t, k]) for k, t in order]
    fetch.start()
    for move in loads:
        move.start()
    fetch.wait()
    total = got[0].astype(jnp.float32)
    for sender in range(1, got.shape[0]):
        total = total + got[sender].astype(jnp.float32)
    far_k, far_v = total[:blocks], total[blocks:]
    spot = lax.broadcasted_iota(jnp.int32, (16, HEAD), 0)
    fresh = []
    for head in range(heads):
        lanes = slice(head * HEAD, (head + 1) * HEAD)
        turned = far_k[:, lanes] * cos_ref[:, lanes] - pltpu.roll(
            far_k[:, lanes], HEAD // 2, 1
        ) * sin_ref[:, lanes]
        fresh.append((turned, far_v[:, lanes]))
    for index, (k, t) in enumerate(order):
        loads[index].wait()
        for head in range(heads):
            at = phase[head]
            start = pl.multiple_of(at // 16 * 16, 16)
            lanes = slice(head * HEAD, (head + 1) * HEAD)
            old = room[t, k, pl.ds(start, 16), lanes].astype(jnp.float32)
            row = fresh[head][t][k : k + 1]
            room[t, k, pl.ds(start, 16), lanes] = jnp.where(spot == at - start, row, old).astype(
                jnp.bfloat16
            )
        saves[index].start()
    for move in saves:
        move.wait()


def local(queries, keys, values, output_gradient, dilation_phase, segment_device_count, owner):
    rows, width = queries.shape
    heads = width // HEAD
    blocks = rows // BLOCK
    bal_size = lax.axis_size("bal")
    devices = lax.axis_size("ctx") * bal_size
    total = rows * devices
    count = owner.shape[0]
    assert blocks == bal_size and bal_size & (bal_size - 1) == 0
    bal = lax.axis_index("bal")
    device = lax.axis_index("ctx") * bal_size + bal
    big = pltpu.CompilerParams(vmem_limit_bytes=60 * 1024 * 1024)
    smem = pl.BlockSpec(memory_space=pltpu.SMEM)
    vmem = pl.BlockSpec(memory_space=pltpu.VMEM)
    anywhere = pl.BlockSpec(memory_space=pl.ANY)
    light = pl.CostEstimate(flops=2_000_000_000, bytes_accessed=5_000_000, transcendentals=0)
    heavy = pl.CostEstimate(flops=20_000_000_000, bytes_accessed=60_000_000, transcendentals=0)
    huge = pl.CostEstimate(flops=1000, bytes_accessed=400_000_000, transcendentals=0)

    def tokens_of(ids):
        return (ids[:, None] * BLOCK + jnp.arange(BLOCK, dtype=jnp.int32)[None, :]).reshape(rows)

    def swap(array, k):
        return lax.ppermute(array, "bal", [(i, i ^ k) for i in range(bal_size)])

    steps = jnp.arange(blocks, dtype=jnp.int32)
    held = device * blocks + steps
    goes_to = lax.dynamic_slice_in_dim(owner, device * blocks, blocks) // blocks % bal_size
    partner = steps ^ bal
    which = jnp.sum(jnp.where(goes_to[None, :] == partner[:, None], steps[None, :], 0), axis=1)
    info = jnp.concatenate([which, device * blocks + which]).astype(jnp.int32)
    comes_from = jnp.sum(
        jnp.where(
            owner[None, :] == held[:, None], jnp.arange(count, dtype=jnp.int32)[None, :], 0
        ),
        axis=1,
    )

    first = heads // 4 * 2
    early = first // 4 * 2
    last = heads - first
    edge = first * HEAD
    originals = (queries, keys, values, output_gradient)

    def send_inputs(jobs, after):
        sizes = [(4, BLOCK, width) for _, _, width in jobs]
        sent = pl.pallas_call(
            functools.partial(pack_kernel, jobs),
            in_specs=[smem] + [anywhere] * 5,
            out_specs=[anywhere] * len(jobs),
            out_shape=[jax.ShapeDtypeStruct(size, jnp.bfloat16) for size in sizes],
            scratch_shapes=[pltpu.VMEM(size, jnp.bfloat16) for size in sizes]
            + [pltpu.SemaphoreType.DMA((len(jobs), 4))] * 2,
            compiler_params=big,
        )(info, after, *originals)
        return sent, [swap(one, job[0]) for one, job in zip(sent, jobs)]

    cut = early * HEAD
    across = range(2, blocks)
    sent, come_early = send_inputs([(k, 0, cut) for k in across], owner)

    cq, sq, ck, sk = tables(tokens_of(held), total)
    own_phase = (held[:, None] * BLOCK + dilation_phase[None, :]).astype(jnp.int32)
    _, _, pick_cos, pick_sin = tables(own_phase, total)
    own_far = pl.pallas_call(
        functools.partial(pick_kernel, heads, blocks),
        in_specs=[smem, anywhere, anywhere, vmem, vmem, anywhere],
        out_specs=anywhere,
        out_shape=jax.ShapeDtypeStruct((devices, 2 * blocks, width), jnp.bfloat16),
        scratch_shapes=[
            pltpu.VMEM((rows, width), jnp.bfloat16),
            pltpu.VMEM((rows, width), jnp.bfloat16),
            pltpu.VMEM((2 * blocks, width), jnp.bfloat16),
            pltpu.SemaphoreType.DMA((2,)),
            pltpu.SemaphoreType.DMA((devices,)),
        ],
        compiler_params=big,
    )(
        dilation_phase,
        keys,
        values,
        pick_cos.reshape(blocks, width),
        pick_sin.reshape(blocks, width),
        sent[0],
    )
    far = lax.all_to_all(
        own_far, ("ctx", "bal"), split_axis=0, concat_axis=0, tiled=True
    ).reshape(devices * 2 * blocks, width)
    _, come_late = send_inputs([(k, cut, edge - cut) for k in across] + [(1, 0, edge)], own_far)
    come_early = [come_late[-1]] + come_early
    come_late = [come_late[-1]] + come_late[:-1]

    side = 2 * count
    wide = jnp.arange(side, dtype=jnp.int32)
    tall = wide[:, None]
    wide = wide[None, :]
    source = tall % count
    pull = (
        wide == source // blocks * (2 * blocks) + tall // count * blocks + source % blocks
    ).astype(jnp.bfloat16)
    lands = owner // blocks * (2 * blocks) + owner % blocks
    push = (jnp.concatenate([lands, lands + blocks])[None, :] == tall).astype(jnp.bfloat16)

    per_step = 2
    columns = per_step * HEAD
    fixed = lambda h, *_: (0, 0)
    square = pl.BlockSpec((side, side), fixed)
    table = pl.BlockSpec((rows, HEAD), fixed)
    part = pl.BlockSpec((4, BLOCK, columns), lambda h, *_: (0, 0, h))
    scratch = [
        pltpu.VMEM((blocks, BLOCK, HEAD), jnp.float32),
        pltpu.VMEM((blocks, BLOCK, HEAD), jnp.float32),
        pltpu.VMEM((side, HEAD), jnp.float32),
    ]
    skip = first // per_step
    tensor = pl.BlockSpec((rows, columns), lambda h, *_: (0, h + skip))
    lane = pl.BlockSpec((side, columns), lambda h, *_: (0, h + skip))
    results = pl.pallas_call(
        functools.partial(attend_kernel, per_step, blocks, count, first, 0),
        grid_spec=pltpu.PrefetchScalarGridSpec(
            num_scalar_prefetch=3,
            grid=(last // per_step,),
            in_specs=[lane, square, square] + [table] * 4 + [tensor] * 4,
            out_specs=[part] * blocks + [lane],
            scratch_shapes=scratch,
        ),
        out_shape=[jax.ShapeDtypeStruct((4, BLOCK, last * HEAD), jnp.bfloat16)] * blocks
        + [jax.ShapeDtypeStruct((side, width), jnp.bfloat16)],
        compiler_params=big,
        cost_estimate=heavy,
    )(info, dilation_phase, segment_device_count, far, pull, push, cq, sq, ck, sk, *originals)
    parts, payload = list(results[:blocks]), results[blocks]
    for k in range(1, blocks):
        parts[k] = swap(parts[k], k)

    ids = (device ^ steps) * blocks
    came = jnp.sum(
        jnp.where(comes_from[None, :] // blocks * blocks == ids[:, None], comes_from[None, :], 0),
        axis=1,
    )
    moved = jnp.concatenate([which, came, partner]).astype(jnp.int32)
    cq, sq, ck, sk = tables(tokens_of(came), total)
    shapes = [jax.ShapeDtypeStruct((blocks, BLOCK, width), jnp.bfloat16)] * 4
    shapes = shapes + [jax.ShapeDtypeStruct((side, width), jnp.bfloat16)]

    def attend_relaid(begin, end, come, carried):
        skip = begin // per_step
        tensor = pl.BlockSpec((BLOCK, columns), lambda h, info, *_: (info[0], h + skip))
        lane = pl.BlockSpec((side, columns), lambda h, *_: (0, h + skip))
        whole = pl.BlockSpec((blocks, BLOCK, columns), lambda h, *_: (0, 0, h + skip))
        operands = 3 + 3 + 4 + 4 + blocks - 1
        return pl.pallas_call(
            functools.partial(attend_kernel, per_step, blocks, count, begin, len(carried)),
            grid_spec=pltpu.PrefetchScalarGridSpec(
                num_scalar_prefetch=3,
                grid=((end - begin) // per_step,),
                in_specs=[lane, square, square]
                + [table] * 4
                + [tensor] * 4
                + [pl.BlockSpec((4, BLOCK, columns), lambda h, *_: (0, 0, h + skip))]
                + [part] * (blocks - 2)
                + [anywhere] * len(carried),
                out_specs=[whole] * 4 + [lane],
                scratch_shapes=scratch,
            ),
            out_shape=shapes,
            input_output_aliases={
                operands + i: 5 - len(carried) + i for i in range(len(carried))
            },
            compiler_params=big,
            cost_estimate=light,
        )(
            moved,
            dilation_phase,
            segment_device_count,
            far,
            pull,
            push,
            cq,
            sq,
            ck,
            sk,
            *originals,
            *come,
            *carried,
        )

    results = attend_relaid(0, early, come_early, [payload])
    results = attend_relaid(early, first, come_late, results)
    finals, payload = [one.reshape(rows, width) for one in results[:4]], results[4]
    got = lax.all_to_all(
        payload.reshape(devices, 2 * blocks, width),
        ("ctx", "bal"),
        split_axis=0,
        concat_axis=0,
        tiled=True,
    )

    new_phase = (comes_from[:, None] * BLOCK + dilation_phase[None, :]).astype(jnp.int32)
    _, _, new_cos, new_sin = tables(new_phase, total)
    out = jax.ShapeDtypeStruct((rows, width), jnp.bfloat16)
    finals = pl.pallas_call(
        functools.partial(place_kernel, blocks, edge),
        in_specs=[smem] + [anywhere] * (blocks + 4),
        out_specs=[anywhere] * 4,
        out_shape=[out] * 4,
        input_output_aliases={1 + blocks + t: t for t in range(4)},
        scratch_shapes=[
            pltpu.VMEM((blocks, 4, BLOCK, last * HEAD), jnp.bfloat16),
            pltpu.SemaphoreType.DMA((blocks,)),
            pltpu.SemaphoreType.DMA((blocks, 4)),
        ],
        compiler_params=big,
        cost_estimate=huge,
    )(partner.astype(jnp.int32), *parts, *finals)
    patched = pl.pallas_call(
        functools.partial(patch_kernel, heads, blocks),
        in_specs=[smem, anywhere, vmem, vmem, anywhere, anywhere],
        out_specs=[anywhere] * 2,
        out_shape=[out] * 2,
        input_output_aliases={4: 0, 5: 1},
        scratch_shapes=[
            pltpu.VMEM((devices, 2 * blocks, width), jnp.bfloat16),
            pltpu.VMEM((2, blocks, BLOCK, width), jnp.bfloat16),
            pltpu.SemaphoreType.DMA(()),
            pltpu.SemaphoreType.DMA((2, blocks)),
            pltpu.SemaphoreType.DMA((2, blocks)),
        ],
        compiler_params=big,
    )(
        dilation_phase,
        got,
        new_cos.reshape(blocks, width),
        new_sin.reshape(blocks, width),
        finals[2],
        finals[3],
    )
    return finals[0], finals[1], patched[0], patched[1]


def solution(mesh):
    token = P(("groups", "ctx", "bal"), "head")
    return jax.shard_map(
        local,
        mesh=mesh,
        in_specs=(token, token, token, token, P("head"), P("head"), P("groups")),
        out_specs=(token, token, token, token),
        check_vma=False,
    )
```

```python
import functools
import math

import jax
import jax.numpy as jnp
from jax import lax
from jax.experimental import pallas as pl
from jax.experimental.pallas import tpu as pltpu
from jax.sharding import PartitionSpec as P

BLOCK = 128
HEAD = 128
LOG2E = 1.4426950408889634
NT = (((1,), (1,)), ((), ()))
TN = (((0,), (0,)), ((), ()))


def tables(positions, total):
    half = HEAD // 2
    pair = jnp.arange(half, dtype=jnp.float32)
    inverse = jnp.exp(pair * (-2.0 * math.log(10000.0) / HEAD))
    where = positions.astype(jnp.float32)[..., None]
    angles = where * inverse
    base = (2.0 * pair / HEAD + 0.4) / 1.4
    growth = jnp.exp((2.0 * where - total) / total * jnp.log(base))
    cosine, sine = jnp.cos(angles), jnp.sin(angles)

    def pack(scale):
        first, second = cosine * scale, sine * scale
        return (
            jnp.concatenate([first, first], axis=-1),
            jnp.concatenate([-second, second], axis=-1),
        )

    return pack(growth) + pack(1.0 / growth)


def dot(left, right, dims=None):
    if dims is None:
        dims = (((1,), (0,)), ((), ()))
    return lax.dot_general(left, right, dims, preferred_element_type=jnp.float32)


def attend_kernel(
    per_step, blocks, count, first, relaid, info, phase, seg, far_ref, pull_ref, push_ref, *rest
):
    cq_ref, sq_ref, ck_ref, sk_ref = rest[:4]
    own = rest[4:8]
    rest = rest[8:]
    if relaid:
        come, rest = rest[: blocks - 1], rest[blocks - 1 + relaid :]
        finals, rest = rest[:4], rest[4:]
    else:
        finals, rest = rest[:blocks], rest[blocks:]
    pay_ref, near_k, near_v, far_sum = rest
    scale = 1.0 / math.sqrt(HEAD)
    key_at = lax.broadcasted_iota(jnp.int32, (BLOCK, BLOCK), 0)
    query_at = lax.broadcasted_iota(jnp.int32, (BLOCK, BLOCK), 1)
    causal = key_at <= query_at
    far_at = lax.broadcasted_iota(jnp.int32, (count, BLOCK), 0)
    half = HEAD // 2
    for sub in range(per_step):
        head = first + pl.program_id(0) * per_step + sub
        lanes = slice(sub * HEAD, (sub + 1) * HEAD)
        both = dot(pull_ref[...], far_ref[:, lanes]).astype(jnp.bfloat16)
        far_k, far_v = both[:count], both[count:]
        span = seg[head] * blocks
        p_far, d_far, q_all, g_all = [], [], [], []
        for k in range(blocks):
            if relaid:
                rows = slice(k * BLOCK, (k + 1) * BLOCK)
                source = [ref[:, lanes] for ref in own]
                if k:
                    source = [come[k - 1][t, :, lanes] for t in range(4)]
            else:
                rows = pl.ds(pl.multiple_of(info[k] * BLOCK, BLOCK), BLOCK)
                source = [ref[rows, lanes] for ref in own]
            block = info[blocks + k]
            low = block & (-span)
            cq, sq, ck, sk = cq_ref[rows, :], sq_ref[rows, :], ck_ref[rows, :], sk_ref[rows, :]
            raw_q, raw_k, value, grad = source
            raw_q = raw_q.astype(jnp.float32)
            raw_k = raw_k.astype(jnp.float32)
            tq = (raw_q * cq + pltpu.roll(raw_q, half, 1) * sq).astype(jnp.bfloat16)
            tk = (raw_k * ck + pltpu.roll(raw_k, half, 1) * sk).astype(jnp.bfloat16)
            keys = jnp.concatenate([tk, far_k], axis=0)
            vals = jnp.concatenate([value, far_v], axis=0)
            score = dot(keys, tq, NT)
            allowed = (far_at >= low) & (far_at < block)
            score = jnp.concatenate(
                [
                    jnp.where(causal, score[:BLOCK], -jnp.inf),
                    jnp.where(allowed, score[BLOCK:], -jnp.inf),
                ],
                axis=0,
            )
            top = jnp.max(score, axis=0, keepdims=True)
            weight = jnp.exp2((score - top) * (scale * LOG2E))
            prob = weight * (1.0 / jnp.sum(weight, axis=0, keepdims=True))
            p16 = prob.astype(jnp.bfloat16)
            dprob = dot(vals, grad, NT)
            delta = jnp.sum(p16.astype(jnp.float32) * dprob, axis=0, keepdims=True)
            d16 = (prob * (dprob - delta)).astype(jnp.bfloat16)
            out = dot(p16, vals, TN)
            dq = dot(d16, keys, TN) * scale
            dk = dot(d16[:BLOCK], tq) * scale
            dv = dot(p16[:BLOCK], grad)
            near_k[k] = dk
            near_v[k] = dv
            made = (
                out,
                dq * cq - pltpu.roll(dq, half, 1) * sq,
                dk * ck - pltpu.roll(dk, half, 1) * sk,
                dv,
            )
            for t in range(4):
                if relaid:
                    finals[t][info[2 * blocks + k], :, lanes] = made[t].astype(jnp.bfloat16)
                else:
                    finals[k][t, :, lanes] = made[t].astype(jnp.bfloat16)
            p_far.append(p16[BLOCK:])
            d_far.append(d16[BLOCK:])
            q_all.append(tq)
            g_all.append(grad)
        far_sum[:count] = (
            dot(jnp.concatenate(d_far, axis=1), jnp.concatenate(q_all, axis=0)) * scale
        )
        far_sum[count:] = dot(jnp.concatenate(p_far, axis=1), jnp.concatenate(g_all, axis=0))
        at = phase[head]
        for k in range(blocks):
            block = info[blocks + k]
            far_sum[pl.ds(block, 1), :] = far_sum[pl.ds(block, 1), :] + near_k[k, pl.ds(at, 1), :]
            far_sum[pl.ds(count + block, 1), :] = (
                far_sum[pl.ds(count + block, 1), :] + near_v[k, pl.ds(at, 1), :]
            )
        pay_ref[:, lanes] = dot(push_ref[...], far_sum[...].astype(jnp.bfloat16)).astype(
            jnp.bfloat16
        )


def pick_kernel(
    heads, blocks, phase, k_hbm, v_hbm, cos_ref, sin_ref, after, out_ref, k_ref, v_ref, row_ref,
    load, save
):
    moves = [
        pltpu.make_async_copy(k_hbm, k_ref, load.at[0]),
        pltpu.make_async_copy(v_hbm, v_ref, load.at[1]),
    ]
    for move in moves:
        move.start()
    for move in moves:
        move.wait()
    spot = lax.broadcasted_iota(jnp.int32, (16, HEAD), 0)
    for head in range(heads):
        at = phase[head]
        start = pl.multiple_of(at // 16 * 16, 16)
        lanes = slice(head * HEAD, (head + 1) * HEAD)
        both = []
        for ref in (k_ref, v_ref):
            rows = []
            for k in range(blocks):
                tile = ref[pl.ds(pl.multiple_of(k * BLOCK + start, 16), 16), lanes]
                tile = jnp.where(spot == at - start, tile.astype(jnp.float32), 0.0)
                rows.append(jnp.sum(tile, axis=0, keepdims=True))
            both.append(jnp.concatenate(rows, axis=0))
        key, value = both
        key = key * cos_ref[:, lanes] + pltpu.roll(key, HEAD // 2, 1) * sin_ref[:, lanes]
        row_ref[:, lanes] = jnp.concatenate([key, value], axis=0).astype(jnp.bfloat16)
    copies = [
        pltpu.make_async_copy(row_ref, out_ref.at[d], save.at[d]) for d in range(out_ref.shape[0])
    ]
    for copy in copies:
        copy.start()
    for copy in copies:
        copy.wait()


def pack_kernel(jobs, info, after, *rest):
    number = len(jobs)
    inputs, rest = rest[:4], rest[4:]
    outs, rooms, (load, save) = rest[:number], rest[number : 2 * number], rest[2 * number :]
    order = [(job, t) for job in range(number) for t in range(4)]

    def fetch(job, t):
        k, start, width = jobs[job]
        rows = pl.ds(pl.multiple_of(info[k] * BLOCK, BLOCK), BLOCK)
        source = inputs[t].at[rows, pl.ds(start, width)]
        return pltpu.make_async_copy(source, rooms[job].at[t], load.at[job, t])

    def store(job, t):
        return pltpu.make_async_copy(rooms[job].at[t], outs[job].at[t], save.at[job, t])

    for job, t in order:
        fetch(job, t).start()
    for job, t in order:
        fetch(job, t).wait()
        store(job, t).start()
    for job, t in order:
        store(job, t).wait()


def link_kernel(*refs):
    pass


def place_kernel(number, edge, slot, *rest):
    parts = rest[:number]
    finals = rest[number + 4 : number + 8]
    room, load, save = rest[number + 8 :]
    width = room.shape[-1]

    def save_of(k, t):
        start = pl.multiple_of(slot[k] * BLOCK, BLOCK)
        where = finals[t].at[pl.ds(start, BLOCK), pl.ds(edge, width)]
        return pltpu.make_async_copy(room.at[k, t], where, save.at[k, t])

    loads = [pltpu.make_async_copy(parts[k], room.at[k], load.at[k]) for k in range(number)]
    for move in loads:
        move.start()
    for k in range(number):
        loads[k].wait()
        for t in range(4):
            save_of(k, t).start()
    for k in range(number):
        for t in range(4):
            save_of(k, t).wait()


def patch_kernel(
    heads, blocks, edge, phase, slot, got_hbm, cos_ref, sin_ref, part, *rest
):
    outs = rest[4:8]
    got, room, side, get, load, save, side_load, side_save = rest[8:]
    width = room.shape[-1]
    final = blocks - 1

    def rows(k):
        return pl.ds(pl.multiple_of(slot[k] * BLOCK, BLOCK), BLOCK)

    def left(ref, k):
        return ref.at[:, pl.ds(0, edge if k == final else width)]

    def store(t, k):
        return pltpu.make_async_copy(room.at[t, k], outs[2 + t].at[rows(k)], save.at[t, k])

    order = [(k, t) for k in range(blocks) for t in range(2)]
    fetch = pltpu.make_async_copy(got_hbm, got, get)
    loads = [
        pltpu.make_async_copy(
            left(outs[2 + t].at[rows(k)], k), left(room.at[t, k], k), load.at[t, k]
        )
        for k, t in order
    ]
    right = pl.ds(edge, width - edge)
    side_loads = [pltpu.make_async_copy(part.at[t], side.at[t], side_load.at[t]) for t in range(2)]
    side_loads += [
        pltpu.make_async_copy(part.at[2 + t], room.at[t, final].at[:, right], side_load.at[2 + t])
        for t in range(2)
    ]
    side_saves = [
        pltpu.make_async_copy(side.at[t], outs[t].at[rows(final), right], side_save.at[t])
        for t in range(2)
    ]
    fetch.start()
    for move in loads + side_loads:
        move.start()
    fetch.wait()
    total = got[0].astype(jnp.float32)
    for sender in range(1, got.shape[0]):
        total = total + got[sender].astype(jnp.float32)
    got_sum = total
    spot = lax.broadcasted_iota(jnp.int32, (16, HEAD), 0)
    line = lax.broadcasted_iota(jnp.int32, (2 * blocks, HEAD), 0)
    turned = []
    for head in range(heads):
        lanes = slice(head * HEAD, (head + 1) * HEAD)
        far_k = got_sum[:blocks, lanes]
        turned.append(
            far_k * cos_ref[:, lanes] - pltpu.roll(far_k, HEAD // 2, 1) * sin_ref[:, lanes]
        )
    for t in range(2):
        side_loads[t].wait()
        side_saves[t].start()
    for index, (k, t) in enumerate(order):
        loads[index].wait()
        if k == final:
            side_loads[2 + t].wait()
        for head in range(heads):
            at = phase[head]
            start = pl.multiple_of(at // 16 * 16, 16)
            lanes = slice(head * HEAD, (head + 1) * HEAD)
            old = room[t, k, pl.ds(start, 16), lanes].astype(jnp.float32)
            source = turned[head] if t == 0 else got_sum[blocks:, lanes]
            row = jnp.sum(
                jnp.where(line[:blocks] == slot[k], source, 0.0), axis=0, keepdims=True
            )
            room[t, k, pl.ds(start, 16), lanes] = jnp.where(spot == at - start, row, old).astype(
                jnp.bfloat16
            )
        store(t, k).start()
    for k, t in order:
        store(t, k).wait()
    for move in side_saves:
        move.wait()


def local(queries, keys, values, output_gradient, dilation_phase, segment_device_count, owner):
    rows, width = queries.shape
    heads = width // HEAD
    blocks = rows // BLOCK
    bal_size = lax.axis_size("bal")
    devices = lax.axis_size("ctx") * bal_size
    total = rows * devices
    count = owner.shape[0]
    assert blocks == bal_size and bal_size & (bal_size - 1) == 0
    bal = lax.axis_index("bal")
    device = lax.axis_index("ctx") * bal_size + bal
    big = pltpu.CompilerParams(vmem_limit_bytes=60 * 1024 * 1024)
    smem = pl.BlockSpec(memory_space=pltpu.SMEM)
    vmem = pl.BlockSpec(memory_space=pltpu.VMEM)
    anywhere = pl.BlockSpec(memory_space=pl.ANY)
    light = pl.CostEstimate(flops=2_000_000_000, bytes_accessed=5_000_000, transcendentals=0)
    heavy = pl.CostEstimate(flops=20_000_000_000, bytes_accessed=60_000_000, transcendentals=0)

    def tokens_of(ids):
        return (ids[:, None] * BLOCK + jnp.arange(BLOCK, dtype=jnp.int32)[None, :]).reshape(rows)

    def swap(array, k):
        return lax.ppermute(array, "bal", [(i, i ^ k) for i in range(bal_size)])

    steps = jnp.arange(blocks, dtype=jnp.int32)
    held = device * blocks + steps
    goes_to = lax.dynamic_slice_in_dim(owner, device * blocks, blocks) // blocks % bal_size
    partner = steps ^ bal
    which = jnp.sum(jnp.where(goes_to[None, :] == partner[:, None], steps[None, :], 0), axis=1)
    info = jnp.concatenate([which, device * blocks + which]).astype(jnp.int32)
    comes_from = jnp.sum(
        jnp.where(
            owner[None, :] == held[:, None], jnp.arange(count, dtype=jnp.int32)[None, :], 0
        ),
        axis=1,
    )

    first = heads // 4 * 2
    early = first // 4 * 2
    last = heads - first
    edge = first * HEAD
    originals = (queries, keys, values, output_gradient)

    def send_inputs(jobs, after):
        sizes = [(4, BLOCK, width) for _, _, width in jobs]
        sent = pl.pallas_call(
            functools.partial(pack_kernel, jobs),
            in_specs=[smem] + [anywhere] * 5,
            out_specs=[anywhere] * len(jobs),
            out_shape=[jax.ShapeDtypeStruct(size, jnp.bfloat16) for size in sizes],
            scratch_shapes=[pltpu.VMEM(size, jnp.bfloat16) for size in sizes]
            + [pltpu.SemaphoreType.DMA((len(jobs), 4))] * 2,
            compiler_params=big,
        )(info, after, *originals)
        return sent, [swap(one, job[0]) for one, job in zip(sent, jobs)]

    cut = early * HEAD
    across = range(2, blocks)
    sent, come_early = send_inputs([(k, 0, cut) for k in across], owner)

    cq, sq, ck, sk = tables(tokens_of(held), total)
    own_phase = (held[:, None] * BLOCK + dilation_phase[None, :]).astype(jnp.int32)
    _, _, pick_cos, pick_sin = tables(own_phase, total)
    own_far = pl.pallas_call(
        functools.partial(pick_kernel, heads, blocks),
        in_specs=[smem, anywhere, anywhere, vmem, vmem, anywhere],
        out_specs=anywhere,
        out_shape=jax.ShapeDtypeStruct((devices, 2 * blocks, width), jnp.bfloat16),
        scratch_shapes=[
            pltpu.VMEM((rows, width), jnp.bfloat16),
            pltpu.VMEM((rows, width), jnp.bfloat16),
            pltpu.VMEM((2 * blocks, width), jnp.bfloat16),
            pltpu.SemaphoreType.DMA((2,)),
            pltpu.SemaphoreType.DMA((devices,)),
        ],
        compiler_params=big,
    )(
        dilation_phase,
        keys,
        values,
        pick_cos.reshape(blocks, width),
        pick_sin.reshape(blocks, width),
        sent[0],
    )
    far = lax.all_to_all(
        own_far, ("ctx", "bal"), split_axis=0, concat_axis=0, tiled=True
    ).reshape(devices * 2 * blocks, width)
    _, come_late = send_inputs([(k, cut, edge - cut) for k in across] + [(1, 0, edge)], own_far)
    come_early = [come_late[-1]] + come_early
    come_late = [come_late[-1]] + come_late[:-1]

    side = 2 * count
    wide = jnp.arange(side, dtype=jnp.int32)
    tall = wide[:, None]
    wide = wide[None, :]
    source = tall % count
    pull = (
        wide == source // blocks * (2 * blocks) + tall // count * blocks + source % blocks
    ).astype(jnp.bfloat16)
    lands = owner // blocks * (2 * blocks) + owner % blocks
    push = (jnp.concatenate([lands, lands + blocks])[None, :] == tall).astype(jnp.bfloat16)

    per_step = 2
    columns = per_step * HEAD
    fixed = lambda h, *_: (0, 0)
    square = pl.BlockSpec((side, side), fixed)
    table = pl.BlockSpec((rows, HEAD), fixed)
    part = pl.BlockSpec((4, BLOCK, columns), lambda h, *_: (0, 0, h))
    scratch = [
        pltpu.VMEM((blocks, BLOCK, HEAD), jnp.float32),
        pltpu.VMEM((blocks, BLOCK, HEAD), jnp.float32),
        pltpu.VMEM((side, HEAD), jnp.float32),
    ]
    skip = first // per_step
    tensor = pl.BlockSpec((rows, columns), lambda h, *_: (0, h + skip))
    lane = pl.BlockSpec((side, columns), lambda h, *_: (0, h + skip))
    results = pl.pallas_call(
        functools.partial(attend_kernel, per_step, blocks, count, first, 0),
        grid_spec=pltpu.PrefetchScalarGridSpec(
            num_scalar_prefetch=3,
            grid=(last // per_step,),
            in_specs=[lane, square, square] + [table] * 4 + [tensor] * 4,
            out_specs=[part] * blocks + [lane],
            scratch_shapes=scratch,
        ),
        out_shape=[jax.ShapeDtypeStruct((4, BLOCK, last * HEAD), jnp.bfloat16)] * blocks
        + [jax.ShapeDtypeStruct((side, width), jnp.bfloat16)],
        compiler_params=big,
        cost_estimate=heavy,
    )(info, dilation_phase, segment_device_count, far, pull, push, cq, sq, ck, sk, *originals)
    parts, payload = list(results[:blocks]), results[blocks]
    for k in range(1, blocks):
        parts[k] = swap(parts[k], k)

    ids = (device ^ steps) * blocks
    came = jnp.sum(
        jnp.where(comes_from[None, :] // blocks * blocks == ids[:, None], comes_from[None, :], 0),
        axis=1,
    )
    moved = jnp.concatenate([which, came, partner]).astype(jnp.int32)
    cq, sq, ck, sk = tables(tokens_of(came), total)
    shapes = [jax.ShapeDtypeStruct((blocks, BLOCK, width), jnp.bfloat16)] * 4
    shapes = shapes + [jax.ShapeDtypeStruct((side, width), jnp.bfloat16)]

    def attend_relaid(begin, end, come, carried):
        skip = begin // per_step
        tensor = pl.BlockSpec((BLOCK, columns), lambda h, info, *_: (info[0], h + skip))
        lane = pl.BlockSpec((side, columns), lambda h, *_: (0, h + skip))
        whole = pl.BlockSpec((blocks, BLOCK, columns), lambda h, *_: (0, 0, h + skip))
        operands = 3 + 3 + 4 + 4 + blocks - 1
        return pl.pallas_call(
            functools.partial(attend_kernel, per_step, blocks, count, begin, len(carried)),
            grid_spec=pltpu.PrefetchScalarGridSpec(
                num_scalar_prefetch=3,
                grid=((end - begin) // per_step,),
                in_specs=[lane, square, square]
                + [table] * 4
                + [tensor] * 4
                + [pl.BlockSpec((4, BLOCK, columns), lambda h, *_: (0, 0, h + skip))]
                + [part] * (blocks - 2)
                + [anywhere] * len(carried),
                out_specs=[whole] * 4 + [lane],
                scratch_shapes=scratch,
            ),
            out_shape=shapes,
            input_output_aliases={
                operands + i: 5 - len(carried) + i for i in range(len(carried))
            },
            compiler_params=big,
            cost_estimate=light,
        )(
            moved,
            dilation_phase,
            segment_device_count,
            far,
            pull,
            push,
            cq,
            sq,
            ck,
            sk,
            *originals,
            *come,
            *carried,
        )

    results = attend_relaid(0, early, come_early, [payload])
    results = attend_relaid(early, first, come_late, results)
    finals, payload = [one.reshape(rows, width) for one in results[:4]], results[4]
    payload = pl.pallas_call(
        link_kernel,
        in_specs=[anywhere, anywhere],
        out_specs=anywhere,
        out_shape=jax.ShapeDtypeStruct((side, width), jnp.bfloat16),
        input_output_aliases={0: 0},
        compiler_params=pltpu.CompilerParams(
            vmem_limit_bytes=60 * 1024 * 1024, has_side_effects=True
        ),
    )(payload, parts[2])
    got = lax.all_to_all(
        payload.reshape(devices, 2 * blocks, width),
        ("ctx", "bal"),
        split_axis=0,
        concat_axis=0,
        tiled=True,
    )

    new_phase = (comes_from[:, None] * BLOCK + dilation_phase[None, :]).astype(jnp.int32)
    _, _, new_cos, new_sin = tables(new_phase, total)
    out = jax.ShapeDtypeStruct((rows, width), jnp.bfloat16)
    number = blocks - 1
    slots = partner.astype(jnp.int32)
    finals = pl.pallas_call(
        functools.partial(place_kernel, number, edge),
        in_specs=[smem] + [anywhere] * (number + 4),
        out_specs=[anywhere] * 4,
        out_shape=[out] * 4,
        input_output_aliases={1 + number + t: t for t in range(4)},
        scratch_shapes=[
            pltpu.VMEM((number, 4, BLOCK, last * HEAD), jnp.bfloat16),
            pltpu.SemaphoreType.DMA((number,)),
            pltpu.SemaphoreType.DMA((number, 4)),
        ],
        compiler_params=big,
        cost_estimate=light,
    )(slots, *parts[:number], *finals)
    return tuple(
        pl.pallas_call(
            functools.partial(patch_kernel, heads, blocks, edge),
            in_specs=[smem, smem, anywhere, vmem, vmem] + [anywhere] * 5,
            out_specs=[anywhere] * 4,
            out_shape=[out] * 4,
            input_output_aliases={6 + t: t for t in range(4)},
            scratch_shapes=[
                pltpu.VMEM((devices, 2 * blocks, width), jnp.bfloat16),
                pltpu.VMEM((2, blocks, BLOCK, width), jnp.bfloat16),
                pltpu.VMEM((2, BLOCK, last * HEAD), jnp.bfloat16),
                pltpu.SemaphoreType.DMA(()),
                pltpu.SemaphoreType.DMA((2, blocks)),
                pltpu.SemaphoreType.DMA((2, blocks)),
                pltpu.SemaphoreType.DMA((4,)),
                pltpu.SemaphoreType.DMA((2,)),
            ],
            compiler_params=big,
        )(
            dilation_phase,
            slots,
            got,
            new_cos.reshape(blocks, width),
            new_sin.reshape(blocks, width),
            parts[number],
            *finals,
        )
    )


def solution(mesh):
    token = P(("groups", "ctx", "bal"), "head")
    return jax.shard_map(
        local,
        mesh=mesh,
        in_specs=(token, token, token, token, P("head"), P("head"), P("groups")),
        out_specs=(token, token, token, token),
        check_vma=False,
    )
```

```python
import functools
import math

import jax
import jax.numpy as jnp
from jax import lax
from jax.experimental import pallas as pl
from jax.experimental.pallas import tpu as pltpu
from jax.sharding import PartitionSpec as P

BLOCK = 128
HEAD = 128
LOG2E = 1.4426950408889634
NT = (((1,), (1,)), ((), ()))
TN = (((0,), (0,)), ((), ()))


def tables(positions, total):
    half = HEAD // 2
    pair = jnp.arange(half, dtype=jnp.float32)
    inverse = jnp.exp(pair * (-2.0 * math.log(10000.0) / HEAD))
    where = positions.astype(jnp.float32)[..., None]
    angles = where * inverse
    base = (2.0 * pair / HEAD + 0.4) / 1.4
    growth = jnp.exp((2.0 * where - total) / total * jnp.log(base))
    cosine, sine = jnp.cos(angles), jnp.sin(angles)

    def pack(scale):
        first, second = cosine * scale, sine * scale
        return (
            jnp.concatenate([first, first], axis=-1),
            jnp.concatenate([-second, second], axis=-1),
        )

    return pack(growth) + pack(1.0 / growth)


def flat_tables(positions, total):
    half = HEAD // 2
    lane = jnp.arange(positions.shape[1] * HEAD, dtype=jnp.int32) % HEAD
    pair = (lane % half).astype(jnp.float32)
    inverse = jnp.exp(pair * (-2.0 * math.log(10000.0) / HEAD))
    where = jnp.repeat(positions.astype(jnp.float32), HEAD, axis=1)
    angles = where * inverse[None, :]
    base = (2.0 * pair / HEAD + 0.4) / 1.4
    growth = jnp.exp((2.0 * where - total) / total * jnp.log(base)[None, :])
    sine = jnp.where(lane[None, :] < half, -jnp.sin(angles), jnp.sin(angles))
    return jnp.cos(angles) / growth, sine / growth


def dot(left, right, dims=None):
    if dims is None:
        dims = (((1,), (0,)), ((), ()))
    return lax.dot_general(left, right, dims, preferred_element_type=jnp.float32)


def attend_kernel(
    per_step, blocks, count, first, relaid, info, phase, seg, far_ref, other_ref, pull_ref, push_ref, *rest
):
    cq_ref, sq_ref, ck_ref, sk_ref = rest[:4]
    own = rest[4:8]
    rest = rest[8:]
    if relaid:
        come, rest = rest[: blocks - 1], rest[blocks - 1 + relaid :]
        finals, rest = rest[:4], rest[4:]
    else:
        finals, rest = rest[:blocks], rest[blocks:]
    pay_ref, near_k, near_v, far_sum = rest
    scale = 1.0 / math.sqrt(HEAD)
    key_at = lax.broadcasted_iota(jnp.int32, (BLOCK, BLOCK), 0)
    query_at = lax.broadcasted_iota(jnp.int32, (BLOCK, BLOCK), 1)
    causal = key_at <= query_at
    far_at = lax.broadcasted_iota(jnp.int32, (count, BLOCK), 0)
    half = HEAD // 2
    for sub in range(per_step):
        head = first + pl.program_id(0) * per_step + sub
        lanes = slice(sub * HEAD, (sub + 1) * HEAD)
        held = jnp.concatenate([far_ref[:, lanes], other_ref[:, lanes]], axis=0)
        both = dot(pull_ref[...], held).astype(jnp.bfloat16)
        far_k, far_v = both[:count], both[count:]
        span = seg[head] * blocks
        p_far, d_far, q_all, g_all = [], [], [], []
        for k in range(blocks):
            if relaid:
                rows = slice(k * BLOCK, (k + 1) * BLOCK)
                source = [ref[:, lanes] for ref in own]
                if k:
                    source = [come[k - 1][t, :, lanes] for t in range(4)]
            else:
                rows = pl.ds(pl.multiple_of(info[k] * BLOCK, BLOCK), BLOCK)
                source = [ref[rows, lanes] for ref in own]
            block = info[blocks + k]
            low = block & (-span)
            cq, sq, ck, sk = cq_ref[rows, :], sq_ref[rows, :], ck_ref[rows, :], sk_ref[rows, :]
            raw_q, raw_k, value, grad = source
            raw_q = raw_q.astype(jnp.float32)
            raw_k = raw_k.astype(jnp.float32)
            tq = (raw_q * cq + pltpu.roll(raw_q, half, 1) * sq).astype(jnp.bfloat16)
            tk = (raw_k * ck + pltpu.roll(raw_k, half, 1) * sk).astype(jnp.bfloat16)
            keys = jnp.concatenate([tk, far_k], axis=0)
            vals = jnp.concatenate([value, far_v], axis=0)
            score = dot(keys, tq, NT)
            allowed = (far_at >= low) & (far_at < block)
            score = jnp.concatenate(
                [
                    jnp.where(causal, score[:BLOCK], -jnp.inf),
                    jnp.where(allowed, score[BLOCK:], -jnp.inf),
                ],
                axis=0,
            )
            top = jnp.max(score, axis=0, keepdims=True)
            weight = jnp.exp2((score - top) * (scale * LOG2E))
            prob = weight * (1.0 / jnp.sum(weight, axis=0, keepdims=True))
            p16 = prob.astype(jnp.bfloat16)
            dprob = dot(vals, grad, NT)
            delta = jnp.sum(p16.astype(jnp.float32) * dprob, axis=0, keepdims=True)
            d16 = (prob * (dprob - delta)).astype(jnp.bfloat16)
            out = dot(p16, vals, TN)
            dq = dot(d16, keys, TN) * scale
            dk = dot(d16[:BLOCK], tq) * scale
            dv = dot(p16[:BLOCK], grad)
            near_k[k] = dk
            near_v[k] = dv
            made = (
                out,
                dq * cq - pltpu.roll(dq, half, 1) * sq,
                dk * ck - pltpu.roll(dk, half, 1) * sk,
                dv,
            )
            for t in range(4):
                if relaid:
                    finals[t][info[2 * blocks + k], :, lanes] = made[t].astype(jnp.bfloat16)
                else:
                    finals[k][t, :, lanes] = made[t].astype(jnp.bfloat16)
            p_far.append(p16[BLOCK:])
            d_far.append(d16[BLOCK:])
            q_all.append(tq)
            g_all.append(grad)
        far_sum[:count] = (
            dot(jnp.concatenate(d_far, axis=1), jnp.concatenate(q_all, axis=0)) * scale
        )
        far_sum[count:] = dot(jnp.concatenate(p_far, axis=1), jnp.concatenate(g_all, axis=0))
        at = phase[head]
        for k in range(blocks):
            block = info[blocks + k]
            far_sum[pl.ds(block, 1), :] = far_sum[pl.ds(block, 1), :] + near_k[k, pl.ds(at, 1), :]
            far_sum[pl.ds(count + block, 1), :] = (
                far_sum[pl.ds(count + block, 1), :] + near_v[k, pl.ds(at, 1), :]
            )
        pay_ref[:, lanes] = dot(push_ref[...], far_sum[...].astype(jnp.bfloat16)).astype(
            jnp.bfloat16
        )


def pick_kernel(
    heads, blocks, phase, k_hbm, v_hbm, cos_ref, sin_ref, after, out_ref, k_ref, v_ref, row_ref,
    load, save
):
    moves = [
        pltpu.make_async_copy(k_hbm, k_ref, load.at[0]),
        pltpu.make_async_copy(v_hbm, v_ref, load.at[1]),
    ]
    for move in moves:
        move.start()
    for move in moves:
        move.wait()
    spot = lax.broadcasted_iota(jnp.int32, (16, HEAD), 0)
    for head in range(heads):
        at = phase[head]
        start = pl.multiple_of(at // 16 * 16, 16)
        lanes = slice(head * HEAD, (head + 1) * HEAD)
        both = []
        for ref in (k_ref, v_ref):
            rows = []
            for k in range(blocks):
                tile = ref[pl.ds(pl.multiple_of(k * BLOCK + start, 16), 16), lanes]
                tile = jnp.where(spot == at - start, tile.astype(jnp.float32), 0.0)
                rows.append(jnp.sum(tile, axis=0, keepdims=True))
            both.append(jnp.concatenate(rows, axis=0))
        key, value = both
        key = key * cos_ref[:, lanes] + pltpu.roll(key, HEAD // 2, 1) * sin_ref[:, lanes]
        row_ref[:, lanes] = jnp.concatenate([key, value], axis=0).astype(jnp.bfloat16)
    copies = [
        pltpu.make_async_copy(row_ref, out_ref.at[d], save.at[d]) for d in range(out_ref.shape[0])
    ]
    for copy in copies:
        copy.start()
    for copy in copies:
        copy.wait()


def pack_kernel(jobs, info, after, *rest):
    number = len(jobs)
    inputs, rest = rest[:4], rest[4:]
    outs, rooms, (load, save) = rest[:number], rest[number : 2 * number], rest[2 * number :]
    order = [(job, t) for job in range(number) for t in range(4)]

    def fetch(job, t):
        k, start, width = jobs[job]
        rows = pl.ds(pl.multiple_of(info[k] * BLOCK, BLOCK), BLOCK)
        source = inputs[t].at[rows, pl.ds(start, width)]
        return pltpu.make_async_copy(source, rooms[job].at[t], load.at[job, t])

    def store(job, t):
        return pltpu.make_async_copy(rooms[job].at[t], outs[job].at[t], save.at[job, t])

    for job, t in order:
        fetch(job, t).start()
    for job, t in order:
        fetch(job, t).wait()
        store(job, t).start()
    for job, t in order:
        store(job, t).wait()


def link_kernel(*refs):
    pass


def place_kernel(number, edge, slot, *rest):
    parts = rest[:number]
    finals = rest[number + 4 : number + 8]
    room, load, save = rest[number + 8 :]
    width = room.shape[-1]

    def save_of(k, t):
        start = pl.multiple_of(slot[k] * BLOCK, BLOCK)
        where = finals[t].at[pl.ds(start, BLOCK), pl.ds(edge, width)]
        return pltpu.make_async_copy(room.at[k, t], where, save.at[k, t])

    loads = [pltpu.make_async_copy(parts[k], room.at[k], load.at[k]) for k in range(number)]
    for move in loads:
        move.start()
    for k in range(number):
        loads[k].wait()
        for t in range(4):
            save_of(k, t).start()
    for k in range(number):
        for t in range(4):
            save_of(k, t).wait()


def patch_kernel(
    heads, blocks, edge, phase, slot, got_hbm, cos_ref, sin_ref, part, *rest
):
    outs = rest[4:8]
    got, room, side, get, load, save, side_load, side_save = rest[8:]
    width = room.shape[-1]
    final = blocks - 1

    def rows(k):
        return pl.ds(pl.multiple_of(slot[k] * BLOCK, BLOCK), BLOCK)

    def left(ref, k):
        return ref.at[:, pl.ds(0, edge if k == final else width)]

    def store(t, k):
        return pltpu.make_async_copy(room.at[t, k], outs[2 + t].at[rows(k)], save.at[t, k])

    order = [(k, t) for k in range(blocks) for t in range(2)]
    fetch = pltpu.make_async_copy(got_hbm, got, get)
    loads = [
        pltpu.make_async_copy(
            left(outs[2 + t].at[rows(k)], k), left(room.at[t, k], k), load.at[t, k]
        )
        for k, t in order
    ]
    right = pl.ds(edge, width - edge)
    side_loads = [pltpu.make_async_copy(part.at[t], side.at[t], side_load.at[t]) for t in range(2)]
    side_loads += [
        pltpu.make_async_copy(part.at[2 + t], room.at[t, final].at[:, right], side_load.at[2 + t])
        for t in range(2)
    ]
    side_saves = [
        pltpu.make_async_copy(side.at[t], outs[t].at[rows(final), right], side_save.at[t])
        for t in range(2)
    ]
    fetch.start()
    for move in loads + side_loads:
        move.start()
    fetch.wait()
    total = got[0].astype(jnp.float32)
    for sender in range(1, got.shape[0]):
        total = total + got[sender].astype(jnp.float32)
    got_sum = total
    spot = lax.broadcasted_iota(jnp.int32, (16, HEAD), 0)
    line = lax.broadcasted_iota(jnp.int32, (2 * blocks, HEAD), 0)
    turned = []
    for head in range(heads):
        lanes = slice(head * HEAD, (head + 1) * HEAD)
        far_k = got_sum[:blocks, lanes]
        turned.append(
            far_k * cos_ref[:, lanes] - pltpu.roll(far_k, HEAD // 2, 1) * sin_ref[:, lanes]
        )
    for t in range(2):
        side_loads[t].wait()
        side_saves[t].start()
    for index, (k, t) in enumerate(order):
        loads[index].wait()
        if k == final:
            side_loads[2 + t].wait()
        for head in range(heads):
            at = phase[head]
            start = pl.multiple_of(at // 16 * 16, 16)
            lanes = slice(head * HEAD, (head + 1) * HEAD)
            old = room[t, k, pl.ds(start, 16), lanes].astype(jnp.float32)
            source = turned[head] if t == 0 else got_sum[blocks:, lanes]
            row = jnp.sum(
                jnp.where(line[:blocks] == slot[k], source, 0.0), axis=0, keepdims=True
            )
            room[t, k, pl.ds(start, 16), lanes] = jnp.where(spot == at - start, row, old).astype(
                jnp.bfloat16
            )
        store(t, k).start()
    for k, t in order:
        store(t, k).wait()
    for move in side_saves:
        move.wait()


def local(queries, keys, values, output_gradient, dilation_phase, segment_device_count, owner):
    rows, width = queries.shape
    heads = width // HEAD
    blocks = rows // BLOCK
    bal_size = lax.axis_size("bal")
    devices = lax.axis_size("ctx") * bal_size
    total = rows * devices
    count = owner.shape[0]
    assert blocks == bal_size == 4 and bal_size & (bal_size - 1) == 0
    bal = lax.axis_index("bal")
    device = lax.axis_index("ctx") * bal_size + bal
    big = pltpu.CompilerParams(vmem_limit_bytes=60 * 1024 * 1024)
    smem = pl.BlockSpec(memory_space=pltpu.SMEM)
    vmem = pl.BlockSpec(memory_space=pltpu.VMEM)
    anywhere = pl.BlockSpec(memory_space=pl.ANY)
    light = pl.CostEstimate(flops=2_000_000_000, bytes_accessed=5_000_000, transcendentals=0)
    heavy = pl.CostEstimate(flops=20_000_000_000, bytes_accessed=60_000_000, transcendentals=0)

    def tokens_of(ids):
        return (ids[:, None] * BLOCK + jnp.arange(BLOCK, dtype=jnp.int32)[None, :]).reshape(rows)

    def swap(array, k):
        return lax.ppermute(array, "bal", [(i, i ^ k) for i in range(bal_size)])

    steps = jnp.arange(blocks, dtype=jnp.int32)
    held = device * blocks + steps
    goes_to = lax.dynamic_slice_in_dim(owner, device * blocks, blocks) // blocks % bal_size
    partner = steps ^ bal
    which = jnp.sum(jnp.where(goes_to[None, :] == partner[:, None], steps[None, :], 0), axis=1)
    info = jnp.concatenate([which, device * blocks + which]).astype(jnp.int32)
    comes_from = jnp.sum(
        jnp.where(
            owner[None, :] == held[:, None], jnp.arange(count, dtype=jnp.int32)[None, :], 0
        ),
        axis=1,
    )

    first = heads // 4 * 2
    last = heads - first
    edge = first * HEAD
    originals = (queries, keys, values, output_gradient)

    def send_inputs(jobs, after):
        sizes = [(4, BLOCK, width) for _, _, width in jobs]
        sent = pl.pallas_call(
            functools.partial(pack_kernel, jobs),
            in_specs=[smem] + [anywhere] * 5,
            out_specs=[anywhere] * len(jobs),
            out_shape=[jax.ShapeDtypeStruct(size, jnp.bfloat16) for size in sizes],
            scratch_shapes=[pltpu.VMEM(size, jnp.bfloat16) for size in sizes]
            + [pltpu.SemaphoreType.DMA((len(jobs), 4))] * 2,
            compiler_params=big,
        )(info, after, *originals)
        return sent, [swap(one, job[0]) for one, job in zip(sent, jobs)]

    sent, come_early = send_inputs([(2, 0, edge)], owner)

    cq, sq, ck, sk = tables(tokens_of(held), total)
    own_phase = (held[:, None] * BLOCK + dilation_phase[None, :]).astype(jnp.int32)
    pick_cos, pick_sin = flat_tables(own_phase, total)
    own_far = pl.pallas_call(
        functools.partial(pick_kernel, heads, blocks),
        in_specs=[smem, anywhere, anywhere, vmem, vmem, anywhere],
        out_specs=anywhere,
        out_shape=jax.ShapeDtypeStruct((devices // 2, 2 * blocks, width), jnp.bfloat16),
        scratch_shapes=[
            pltpu.VMEM((rows, width), jnp.bfloat16),
            pltpu.VMEM((rows, width), jnp.bfloat16),
            pltpu.VMEM((2 * blocks, width), jnp.bfloat16),
            pltpu.SemaphoreType.DMA((2,)),
            pltpu.SemaphoreType.DMA((devices // 2,)),
        ],
        compiler_params=big,
    )(
        dilation_phase,
        keys,
        values,
        pick_cos,
        pick_sin,
        sent[0],
    )
    halves = [list(range(0, devices, 2)), list(range(1, devices, 2))]
    near_far = lax.all_to_all(
        own_far,
        ("ctx", "bal"),
        split_axis=0,
        concat_axis=0,
        tiled=True,
        axis_index_groups=halves,
    ).reshape(count, width)
    other_far = swap(near_far, 1)
    later = [3, 1]
    _, come_late = send_inputs([(k, 0, edge) for k in later], own_far)
    come = dict(zip([2] + later, come_early + come_late))
    come = [come[k] for k in range(1, blocks)]

    side = 2 * count
    wide = jnp.arange(side, dtype=jnp.int32)
    tall = wide[:, None]
    wide = wide[None, :]
    source = tall % count
    holder = source // blocks
    held_row = (holder ^ device) % 2 * count + holder // 2 * (2 * blocks)
    pull = (wide == held_row + tall // count * blocks + source % blocks).astype(jnp.bfloat16)
    lands = owner // blocks * (2 * blocks) + owner % blocks
    push = (jnp.concatenate([lands, lands + blocks])[None, :] == tall).astype(jnp.bfloat16)

    per_step = 2
    columns = per_step * HEAD
    fixed = lambda h, *_: (0, 0)
    square = pl.BlockSpec((side, side), fixed)
    table = pl.BlockSpec((rows, HEAD), fixed)
    part = pl.BlockSpec((4, BLOCK, columns), lambda h, *_: (0, 0, h))
    scratch = [
        pltpu.VMEM((blocks, BLOCK, HEAD), jnp.float32),
        pltpu.VMEM((blocks, BLOCK, HEAD), jnp.float32),
        pltpu.VMEM((side, HEAD), jnp.float32),
    ]
    skip = first // per_step
    tensor = pl.BlockSpec((rows, columns), lambda h, *_: (0, h + skip))
    lane = pl.BlockSpec((side, columns), lambda h, *_: (0, h + skip))
    far = pl.BlockSpec((count, columns), lambda h, *_: (0, h + skip))
    results = pl.pallas_call(
        functools.partial(attend_kernel, per_step, blocks, count, first, 0),
        grid_spec=pltpu.PrefetchScalarGridSpec(
            num_scalar_prefetch=3,
            grid=(last // per_step,),
            in_specs=[far, far, square, square] + [table] * 4 + [tensor] * 4,
            out_specs=[part] * blocks + [lane],
            scratch_shapes=scratch,
        ),
        out_shape=[jax.ShapeDtypeStruct((4, BLOCK, last * HEAD), jnp.bfloat16)] * blocks
        + [jax.ShapeDtypeStruct((side, width), jnp.bfloat16)],
        compiler_params=big,
        cost_estimate=heavy,
    )(
        info,
        dilation_phase,
        segment_device_count,
        near_far,
        other_far,
        pull,
        push,
        cq,
        sq,
        ck,
        sk,
        *originals,
    )
    parts, payload = list(results[:blocks]), results[blocks]
    for k in range(1, blocks):
        parts[k] = swap(parts[k], k)

    ids = (device ^ steps) * blocks
    came = jnp.sum(
        jnp.where(comes_from[None, :] // blocks * blocks == ids[:, None], comes_from[None, :], 0),
        axis=1,
    )
    moved = jnp.concatenate([which, came, partner]).astype(jnp.int32)
    cq, sq, ck, sk = tables(tokens_of(came), total)
    shapes = [jax.ShapeDtypeStruct((blocks, BLOCK, width), jnp.bfloat16)] * 4
    shapes = shapes + [jax.ShapeDtypeStruct((side, width), jnp.bfloat16)]

    def attend_relaid(begin, end, come, carried):
        skip = begin // per_step
        tensor = pl.BlockSpec((BLOCK, columns), lambda h, info, *_: (info[0], h + skip))
        lane = pl.BlockSpec((side, columns), lambda h, *_: (0, h + skip))
        far = pl.BlockSpec((count, columns), lambda h, *_: (0, h + skip))
        whole = pl.BlockSpec((blocks, BLOCK, columns), lambda h, *_: (0, 0, h + skip))
        operands = 3 + 4 + 4 + 4 + blocks - 1
        return pl.pallas_call(
            functools.partial(attend_kernel, per_step, blocks, count, begin, len(carried)),
            grid_spec=pltpu.PrefetchScalarGridSpec(
                num_scalar_prefetch=3,
                grid=((end - begin) // per_step,),
                in_specs=[far, far, square, square]
                + [table] * 4
                + [tensor] * 4
                + [part] * (blocks - 1)
                + [anywhere] * len(carried),
                out_specs=[whole] * 4 + [lane],
                scratch_shapes=scratch,
            ),
            out_shape=shapes,
            input_output_aliases={
                operands + i: 5 - len(carried) + i for i in range(len(carried))
            },
            compiler_params=big,
            cost_estimate=light,
        )(
            moved,
            dilation_phase,
            segment_device_count,
            near_far,
            other_far,
            pull,
            push,
            cq,
            sq,
            ck,
            sk,
            *originals,
            *come,
            *carried,
        )

    results = attend_relaid(0, first, come, [payload])
    finals, payload = [one.reshape(rows, width) for one in results[:4]], results[4]
    payload = pl.pallas_call(
        link_kernel,
        in_specs=[anywhere, anywhere],
        out_specs=anywhere,
        out_shape=jax.ShapeDtypeStruct((side, width), jnp.bfloat16),
        input_output_aliases={0: 0},
        compiler_params=pltpu.CompilerParams(
            vmem_limit_bytes=60 * 1024 * 1024, has_side_effects=True
        ),
    )(payload, parts[2])
    got = lax.all_to_all(
        payload.reshape(devices, 2 * blocks, width),
        ("ctx", "bal"),
        split_axis=0,
        concat_axis=0,
        tiled=True,
    )

    new_phase = (comes_from[:, None] * BLOCK + dilation_phase[None, :]).astype(jnp.int32)
    new_cos, new_sin = flat_tables(new_phase, total)
    out = jax.ShapeDtypeStruct((rows, width), jnp.bfloat16)
    number = blocks - 1
    slots = partner.astype(jnp.int32)
    finals = pl.pallas_call(
        functools.partial(place_kernel, number, edge),
        in_specs=[smem] + [anywhere] * (number + 4),
        out_specs=[anywhere] * 4,
        out_shape=[out] * 4,
        input_output_aliases={1 + number + t: t for t in range(4)},
        scratch_shapes=[
            pltpu.VMEM((number, 4, BLOCK, last * HEAD), jnp.bfloat16),
            pltpu.SemaphoreType.DMA((number,)),
            pltpu.SemaphoreType.DMA((number, 4)),
        ],
        compiler_params=big,
        cost_estimate=light,
    )(slots, *parts[:number], *finals)
    return tuple(
        pl.pallas_call(
            functools.partial(patch_kernel, heads, blocks, edge),
            in_specs=[smem, smem, anywhere, vmem, vmem] + [anywhere] * 5,
            out_specs=[anywhere] * 4,
            out_shape=[out] * 4,
            input_output_aliases={6 + t: t for t in range(4)},
            scratch_shapes=[
                pltpu.VMEM((devices, 2 * blocks, width), jnp.bfloat16),
                pltpu.VMEM((2, blocks, BLOCK, width), jnp.bfloat16),
                pltpu.VMEM((2, BLOCK, last * HEAD), jnp.bfloat16),
                pltpu.SemaphoreType.DMA(()),
                pltpu.SemaphoreType.DMA((2, blocks)),
                pltpu.SemaphoreType.DMA((2, blocks)),
                pltpu.SemaphoreType.DMA((4,)),
                pltpu.SemaphoreType.DMA((2,)),
            ],
            compiler_params=big,
        )(
            dilation_phase,
            slots,
            got,
            new_cos,
            new_sin,
            parts[number],
            *finals,
        )
    )


def solution(mesh):
    token = P(("groups", "ctx", "bal"), "head")
    return jax.shard_map(
        local,
        mesh=mesh,
        in_specs=(token, token, token, token, P("head"), P("head"), P("groups")),
        out_specs=(token, token, token, token),
        check_vma=False,
    )
```

```python
import functools
import math

import jax
import jax.numpy as jnp
from jax import lax
from jax.experimental import pallas as pl
from jax.experimental.pallas import tpu as pltpu
from jax.sharding import PartitionSpec as P

BLOCK = 128
HEAD = 128
LOG2E = 1.4426950408889634
NT = (((1,), (1,)), ((), ()))
TN = (((0,), (0,)), ((), ()))


def tables(positions, total):
    half = HEAD // 2
    pair = jnp.arange(half, dtype=jnp.float32)
    inverse = jnp.exp(pair * (-2.0 * math.log(10000.0) / HEAD))
    where = positions.astype(jnp.float32)[..., None]
    angles = where * inverse
    base = (2.0 * pair / HEAD + 0.4) / 1.4
    growth = jnp.exp((2.0 * where - total) / total * jnp.log(base))
    cosine, sine = jnp.cos(angles), jnp.sin(angles)

    def pack(scale):
        first, second = cosine * scale, sine * scale
        return (
            jnp.concatenate([first, first], axis=-1),
            jnp.concatenate([-second, second], axis=-1),
        )

    return pack(growth) + pack(1.0 / growth)


def flat_tables(positions, total):
    half = HEAD // 2
    lane = jnp.arange(positions.shape[1] * HEAD, dtype=jnp.int32) % HEAD
    pair = (lane % half).astype(jnp.float32)
    inverse = jnp.exp(pair * (-2.0 * math.log(10000.0) / HEAD))
    where = jnp.repeat(positions.astype(jnp.float32), HEAD, axis=1)
    angles = where * inverse[None, :]
    base = (2.0 * pair / HEAD + 0.4) / 1.4
    growth = jnp.exp((2.0 * where - total) / total * jnp.log(base)[None, :])
    sine = jnp.where(lane[None, :] < half, -jnp.sin(angles), jnp.sin(angles))
    return jnp.cos(angles) / growth, sine / growth


def dot(left, right, dims=None):
    if dims is None:
        dims = (((1,), (0,)), ((), ()))
    return lax.dot_general(left, right, dims, preferred_element_type=jnp.float32)


def attend_kernel(
    per_step, blocks, count, first, relaid, info, phase, seg, far_ref, other_ref, pull_ref, push_ref, *rest
):
    cq_ref, sq_ref, ck_ref, sk_ref = rest[:4]
    own = rest[4:8]
    rest = rest[8:]
    if relaid:
        come, rest = rest[: blocks - 1], rest[blocks - 1 + relaid :]
        finals, rest = rest[:4], rest[4:]
    else:
        finals, rest = rest[:blocks], rest[blocks:]
    (pay_ref,) = rest
    scale = 1.0 / math.sqrt(HEAD)
    key_at = lax.broadcasted_iota(jnp.int32, (BLOCK, BLOCK), 0)
    query_at = lax.broadcasted_iota(jnp.int32, (BLOCK, BLOCK), 1)
    far_at = lax.broadcasted_iota(jnp.int32, (count, BLOCK), 0)
    far_query = lax.broadcasted_iota(jnp.int32, (count, BLOCK), 1)
    half = HEAD // 2
    for sub in range(per_step):
        head = first + pl.program_id(0) * per_step + sub
        lanes = slice(sub * HEAD, (sub + 1) * HEAD)
        held = jnp.concatenate([far_ref[:, lanes], other_ref[:, lanes]], axis=0)
        both = dot(pull_ref[...], held).astype(jnp.bfloat16)
        far_k, far_v = both[:count], both[count:]
        span = seg[head] * blocks
        at = phase[head]
        causal = (key_at <= query_at) & (key_at != at)
        behind = far_at * BLOCK + at - far_query
        p_far, d_far, q_all, g_all = [], [], [], []
        for k in range(blocks):
            if relaid:
                rows = slice(k * BLOCK, (k + 1) * BLOCK)
                source = [ref[:, lanes] for ref in own]
                if k:
                    source = [come[k - 1][t, :, lanes] for t in range(4)]
            else:
                rows = pl.ds(pl.multiple_of(info[k] * BLOCK, BLOCK), BLOCK)
                source = [ref[rows, lanes] for ref in own]
            block = info[blocks + k]
            low = block & (-span)
            cq, sq, ck, sk = cq_ref[rows, :], sq_ref[rows, :], ck_ref[rows, :], sk_ref[rows, :]
            raw_q, raw_k, value, grad = source
            raw_q = raw_q.astype(jnp.float32)
            raw_k = raw_k.astype(jnp.float32)
            tq = (raw_q * cq + pltpu.roll(raw_q, half, 1) * sq).astype(jnp.bfloat16)
            tk = (raw_k * ck + pltpu.roll(raw_k, half, 1) * sk).astype(jnp.bfloat16)
            keys = jnp.concatenate([tk, far_k], axis=0)
            vals = jnp.concatenate([value, far_v], axis=0)
            score = dot(keys, tq, NT)
            allowed = (far_at >= low) & (behind <= block * BLOCK)
            score = jnp.concatenate(
                [
                    jnp.where(causal, score[:BLOCK], -jnp.inf),
                    jnp.where(allowed, score[BLOCK:], -jnp.inf),
                ],
                axis=0,
            )
            top = jnp.max(score, axis=0, keepdims=True)
            weight = jnp.exp2((score - top) * (scale * LOG2E))
            prob = weight * (1.0 / jnp.sum(weight, axis=0, keepdims=True))
            p16 = prob.astype(jnp.bfloat16)
            dprob = dot(vals, grad, NT)
            delta = jnp.sum(p16.astype(jnp.float32) * dprob, axis=0, keepdims=True)
            d16 = (prob * (dprob - delta)).astype(jnp.bfloat16)
            out = dot(p16, vals, TN)
            dq = dot(d16, keys, TN) * scale
            dk = dot(d16[:BLOCK], tq) * scale
            dv = dot(p16[:BLOCK], grad)
            made = (
                out,
                dq * cq - pltpu.roll(dq, half, 1) * sq,
                dk * ck - pltpu.roll(dk, half, 1) * sk,
                dv,
            )
            for t in range(4):
                if relaid:
                    finals[t][info[2 * blocks + k], :, lanes] = made[t].astype(jnp.bfloat16)
                else:
                    finals[k][t, :, lanes] = made[t].astype(jnp.bfloat16)
            p_far.append(p16[BLOCK:])
            d_far.append(d16[BLOCK:])
            q_all.append(tq)
            g_all.append(grad)
        far_dk = dot(jnp.concatenate(d_far, axis=1), jnp.concatenate(q_all, axis=0)) * scale
        far_dv = dot(jnp.concatenate(p_far, axis=1), jnp.concatenate(g_all, axis=0))
        far_sum = jnp.concatenate([far_dk, far_dv], axis=0).astype(jnp.bfloat16)
        pay_ref[:, lanes] = dot(push_ref[...], far_sum).astype(jnp.bfloat16)


def pick_kernel(
    heads, blocks, phase, k_hbm, v_hbm, cos_ref, sin_ref, after, out_ref, k_ref, v_ref, row_ref,
    load, save
):
    moves = [
        pltpu.make_async_copy(k_hbm, k_ref, load.at[0]),
        pltpu.make_async_copy(v_hbm, v_ref, load.at[1]),
    ]
    for move in moves:
        move.start()
    for move in moves:
        move.wait()
    spot = lax.broadcasted_iota(jnp.int32, (16, HEAD), 0)
    for head in range(heads):
        at = phase[head]
        start = pl.multiple_of(at // 16 * 16, 16)
        lanes = slice(head * HEAD, (head + 1) * HEAD)
        both = []
        for ref in (k_ref, v_ref):
            rows = []
            for k in range(blocks):
                tile = ref[pl.ds(pl.multiple_of(k * BLOCK + start, 16), 16), lanes]
                tile = jnp.where(spot == at - start, tile.astype(jnp.float32), 0.0)
                rows.append(jnp.sum(tile, axis=0, keepdims=True))
            both.append(jnp.concatenate(rows, axis=0))
        key, value = both
        key = key * cos_ref[:, lanes] + pltpu.roll(key, HEAD // 2, 1) * sin_ref[:, lanes]
        row_ref[:, lanes] = jnp.concatenate([key, value], axis=0).astype(jnp.bfloat16)
    copies = [
        pltpu.make_async_copy(row_ref, out_ref.at[d], save.at[d]) for d in range(out_ref.shape[0])
    ]
    for copy in copies:
        copy.start()
    for copy in copies:
        copy.wait()


def pack_kernel(jobs, info, after, *rest):
    number = len(jobs)
    inputs, rest = rest[:4], rest[4:]
    outs, rooms, (load, save) = rest[:number], rest[number : 2 * number], rest[2 * number :]
    order = [(job, t) for job in range(number) for t in range(4)]

    def fetch(job, t):
        k, start, width = jobs[job]
        rows = pl.ds(pl.multiple_of(info[k] * BLOCK, BLOCK), BLOCK)
        source = inputs[t].at[rows, pl.ds(start, width)]
        return pltpu.make_async_copy(source, rooms[job].at[t], load.at[job, t])

    def store(job, t):
        return pltpu.make_async_copy(rooms[job].at[t], outs[job].at[t], save.at[job, t])

    for job, t in order:
        fetch(job, t).start()
    for job, t in order:
        fetch(job, t).wait()
        store(job, t).start()
    for job, t in order:
        store(job, t).wait()


def link_kernel(*refs):
    pass


def place_kernel(number, edge, slot, *rest):
    parts = rest[:number]
    finals = rest[number + 4 : number + 8]
    room, load, save = rest[number + 8 :]
    width = room.shape[-1]

    def save_of(k, t):
        start = pl.multiple_of(slot[k] * BLOCK, BLOCK)
        where = finals[t].at[pl.ds(start, BLOCK), pl.ds(edge, width)]
        return pltpu.make_async_copy(room.at[k, t], where, save.at[k, t])

    loads = [pltpu.make_async_copy(parts[k], room.at[k], load.at[k]) for k in range(number)]
    for move in loads:
        move.start()
    for k in range(number):
        loads[k].wait()
        for t in range(4):
            save_of(k, t).start()
    for k in range(number):
        for t in range(4):
            save_of(k, t).wait()


def patch_kernel(
    heads, blocks, edge, phase, slot, got_hbm, cos_ref, sin_ref, part, *rest
):
    outs = rest[4:8]
    got, room, side, get, load, save, side_load, side_save = rest[8:]
    width = room.shape[-1]
    final = blocks - 1

    def rows(k):
        return pl.ds(pl.multiple_of(slot[k] * BLOCK, BLOCK), BLOCK)

    def left(ref, k):
        return ref.at[:, pl.ds(0, edge if k == final else width)]

    def store(t, k):
        return pltpu.make_async_copy(room.at[t, k], outs[2 + t].at[rows(k)], save.at[t, k])

    order = [(k, t) for k in range(blocks) for t in range(2)]
    fetch = pltpu.make_async_copy(got_hbm, got, get)
    loads = [
        pltpu.make_async_copy(
            left(outs[2 + t].at[rows(k)], k), left(room.at[t, k], k), load.at[t, k]
        )
        for k, t in order
    ]
    right = pl.ds(edge, width - edge)
    side_loads = [pltpu.make_async_copy(part.at[t], side.at[t], side_load.at[t]) for t in range(2)]
    side_loads += [
        pltpu.make_async_copy(part.at[2 + t], room.at[t, final].at[:, right], side_load.at[2 + t])
        for t in range(2)
    ]
    side_saves = [
        pltpu.make_async_copy(side.at[t], outs[t].at[rows(final), right], side_save.at[t])
        for t in range(2)
    ]
    fetch.start()
    for move in loads + side_loads:
        move.start()
    fetch.wait()
    total = got[0].astype(jnp.float32)
    for sender in range(1, got.shape[0]):
        total = total + got[sender].astype(jnp.float32)
    got_sum = total
    spot = lax.broadcasted_iota(jnp.int32, (16, HEAD), 0)
    line = lax.broadcasted_iota(jnp.int32, (2 * blocks, HEAD), 0)
    turned = []
    for head in range(heads):
        lanes = slice(head * HEAD, (head + 1) * HEAD)
        far_k = got_sum[:blocks, lanes]
        turned.append(
            far_k * cos_ref[:, lanes] - pltpu.roll(far_k, HEAD // 2, 1) * sin_ref[:, lanes]
        )
    for t in range(2):
        side_loads[t].wait()
        side_saves[t].start()
    for index, (k, t) in enumerate(order):
        loads[index].wait()
        if k == final:
            side_loads[2 + t].wait()
        for head in range(heads):
            at = phase[head]
            start = pl.multiple_of(at // 16 * 16, 16)
            lanes = slice(head * HEAD, (head + 1) * HEAD)
            old = room[t, k, pl.ds(start, 16), lanes].astype(jnp.float32)
            source = turned[head] if t == 0 else got_sum[blocks:, lanes]
            row = jnp.sum(
                jnp.where(line[:blocks] == slot[k], source, 0.0), axis=0, keepdims=True
            )
            room[t, k, pl.ds(start, 16), lanes] = jnp.where(spot == at - start, row, old).astype(
                jnp.bfloat16
            )
        store(t, k).start()
    for k, t in order:
        store(t, k).wait()
    for move in side_saves:
        move.wait()


def local(queries, keys, values, output_gradient, dilation_phase, segment_device_count, owner):
    rows, width = queries.shape
    heads = width // HEAD
    blocks = rows // BLOCK
    bal_size = lax.axis_size("bal")
    devices = lax.axis_size("ctx") * bal_size
    total = rows * devices
    count = owner.shape[0]
    assert blocks == bal_size == 4 and bal_size & (bal_size - 1) == 0
    bal = lax.axis_index("bal")
    device = lax.axis_index("ctx") * bal_size + bal
    room = 66_000_000
    big = pltpu.CompilerParams(vmem_limit_bytes=room)
    smem = pl.BlockSpec(memory_space=pltpu.SMEM)
    vmem = pl.BlockSpec(memory_space=pltpu.VMEM)
    anywhere = pl.BlockSpec(memory_space=pl.ANY)
    light = pl.CostEstimate(flops=2_000_000_000, bytes_accessed=5_000_000, transcendentals=0)
    heavy = pl.CostEstimate(flops=20_000_000_000, bytes_accessed=60_000_000, transcendentals=0)

    def tokens_of(ids):
        return (ids[:, None] * BLOCK + jnp.arange(BLOCK, dtype=jnp.int32)[None, :]).reshape(rows)

    def swap(array, k):
        return lax.ppermute(array, "bal", [(i, i ^ k) for i in range(bal_size)])

    steps = jnp.arange(blocks, dtype=jnp.int32)
    held = device * blocks + steps
    goes_to = lax.dynamic_slice_in_dim(owner, device * blocks, blocks) // blocks % bal_size
    partner = steps ^ bal
    which = jnp.sum(jnp.where(goes_to[None, :] == partner[:, None], steps[None, :], 0), axis=1)
    info = jnp.concatenate([which, device * blocks + which]).astype(jnp.int32)
    comes_from = jnp.sum(
        jnp.where(
            owner[None, :] == held[:, None], jnp.arange(count, dtype=jnp.int32)[None, :], 0
        ),
        axis=1,
    )

    first = heads * 3 // 10 * 2
    last = heads - first
    edge = first * HEAD
    originals = (queries, keys, values, output_gradient)

    def send_inputs(jobs, after):
        sizes = [(4, BLOCK, width) for _, _, width in jobs]
        sent = pl.pallas_call(
            functools.partial(pack_kernel, jobs),
            in_specs=[smem] + [anywhere] * 5,
            out_specs=[anywhere] * len(jobs),
            out_shape=[jax.ShapeDtypeStruct(size, jnp.bfloat16) for size in sizes],
            scratch_shapes=[pltpu.VMEM(size, jnp.bfloat16) for size in sizes]
            + [pltpu.SemaphoreType.DMA((len(jobs), 4))] * 2,
            compiler_params=big,
        )(info, after, *originals)
        return sent, [swap(one, job[0]) for one, job in zip(sent, jobs)]

    sent, come_early = send_inputs([(2, 0, edge)], owner)

    cq, sq, ck, sk = tables(tokens_of(held), total)
    own_phase = (held[:, None] * BLOCK + dilation_phase[None, :]).astype(jnp.int32)
    pick_cos, pick_sin = flat_tables(own_phase, total)
    own_far = pl.pallas_call(
        functools.partial(pick_kernel, heads, blocks),
        in_specs=[smem, anywhere, anywhere, vmem, vmem, anywhere],
        out_specs=anywhere,
        out_shape=jax.ShapeDtypeStruct((devices // 2, 2 * blocks, width), jnp.bfloat16),
        scratch_shapes=[
            pltpu.VMEM((rows, width), jnp.bfloat16),
            pltpu.VMEM((rows, width), jnp.bfloat16),
            pltpu.VMEM((2 * blocks, width), jnp.bfloat16),
            pltpu.SemaphoreType.DMA((2,)),
            pltpu.SemaphoreType.DMA((devices // 2,)),
        ],
        compiler_params=big,
    )(
        dilation_phase,
        keys,
        values,
        pick_cos,
        pick_sin,
        sent[0],
    )
    halves = [list(range(0, devices, 2)), list(range(1, devices, 2))]
    near_far = lax.all_to_all(
        own_far,
        ("ctx", "bal"),
        split_axis=0,
        concat_axis=0,
        tiled=True,
        axis_index_groups=halves,
    ).reshape(count, width)
    other_far = swap(near_far, 1)
    later = [3, 1]
    _, come_late = send_inputs([(k, 0, edge) for k in later], own_far)
    come = dict(zip([2] + later, come_early + come_late))
    come = [come[k] for k in range(1, blocks)]

    side = 2 * count
    wide = jnp.arange(side, dtype=jnp.int32)
    tall = wide[:, None]
    wide = wide[None, :]
    source = tall % count
    holder = source // blocks
    held_row = (holder ^ device) % 2 * count + holder // 2 * (2 * blocks)
    pull = (wide == held_row + tall // count * blocks + source % blocks).astype(jnp.bfloat16)
    lands = owner // blocks * (2 * blocks) + owner % blocks
    push = (jnp.concatenate([lands, lands + blocks])[None, :] == tall).astype(jnp.bfloat16)

    per_step = 2
    columns = per_step * HEAD
    fixed = lambda h, *_: (0, 0)
    square = pl.BlockSpec((side, side), fixed)
    table = pl.BlockSpec((rows, HEAD), fixed)
    part = pl.BlockSpec((4, BLOCK, columns), lambda h, *_: (0, 0, h))
    skip = first // per_step
    tensor = pl.BlockSpec((rows, columns), lambda h, *_: (0, h + skip))
    lane = pl.BlockSpec((side, columns), lambda h, *_: (0, h + skip))
    far = pl.BlockSpec((count, columns), lambda h, *_: (0, h + skip))
    results = pl.pallas_call(
        functools.partial(attend_kernel, per_step, blocks, count, first, 0),
        grid_spec=pltpu.PrefetchScalarGridSpec(
            num_scalar_prefetch=3,
            grid=(last // per_step,),
            in_specs=[far, far, square, square] + [table] * 4 + [tensor] * 4,
            out_specs=[part] * blocks + [lane],
        ),
        out_shape=[jax.ShapeDtypeStruct((4, BLOCK, last * HEAD), jnp.bfloat16)] * blocks
        + [jax.ShapeDtypeStruct((side, width), jnp.bfloat16)],
        compiler_params=big,
        cost_estimate=heavy,
    )(
        info,
        dilation_phase,
        segment_device_count,
        near_far,
        other_far,
        pull,
        push,
        cq,
        sq,
        ck,
        sk,
        *originals,
    )
    parts, payload = list(results[:blocks]), results[blocks]
    for k in range(1, blocks):
        parts[k] = swap(parts[k], k)

    ids = (device ^ steps) * blocks
    came = jnp.sum(
        jnp.where(comes_from[None, :] // blocks * blocks == ids[:, None], comes_from[None, :], 0),
        axis=1,
    )
    moved = jnp.concatenate([which, came, partner]).astype(jnp.int32)
    cq, sq, ck, sk = tables(tokens_of(came), total)
    shapes = [jax.ShapeDtypeStruct((blocks, BLOCK, width), jnp.bfloat16)] * 4
    shapes = shapes + [jax.ShapeDtypeStruct((side, width), jnp.bfloat16)]

    def attend_relaid(begin, end, come, carried):
        skip = begin // per_step
        tensor = pl.BlockSpec((BLOCK, columns), lambda h, info, *_: (info[0], h + skip))
        lane = pl.BlockSpec((side, columns), lambda h, *_: (0, h + skip))
        far = pl.BlockSpec((count, columns), lambda h, *_: (0, h + skip))
        whole = pl.BlockSpec((blocks, BLOCK, columns), lambda h, *_: (0, 0, h + skip))
        operands = 3 + 4 + 4 + 4 + blocks - 1
        return pl.pallas_call(
            functools.partial(attend_kernel, per_step, blocks, count, begin, len(carried)),
            grid_spec=pltpu.PrefetchScalarGridSpec(
                num_scalar_prefetch=3,
                grid=((end - begin) // per_step,),
                in_specs=[far, far, square, square]
                + [table] * 4
                + [tensor] * 4
                + [part] * (blocks - 1)
                + [anywhere] * len(carried),
                out_specs=[whole] * 4 + [lane],
                ),
            out_shape=shapes,
            input_output_aliases={
                operands + i: 5 - len(carried) + i for i in range(len(carried))
            },
            compiler_params=big,
            cost_estimate=light,
        )(
            moved,
            dilation_phase,
            segment_device_count,
            near_far,
            other_far,
            pull,
            push,
            cq,
            sq,
            ck,
            sk,
            *originals,
            *come,
            *carried,
        )

    results = attend_relaid(0, first, come, [payload])
    finals, payload = [one.reshape(rows, width) for one in results[:4]], results[4]
    payload = pl.pallas_call(
        link_kernel,
        in_specs=[anywhere, anywhere],
        out_specs=anywhere,
        out_shape=jax.ShapeDtypeStruct((side, width), jnp.bfloat16),
        input_output_aliases={0: 0},
        compiler_params=pltpu.CompilerParams(
            vmem_limit_bytes=room, has_side_effects=True
        ),
    )(payload, parts[2])
    got = lax.all_to_all(
        payload.reshape(devices, 2 * blocks, width),
        ("ctx", "bal"),
        split_axis=0,
        concat_axis=0,
        tiled=True,
    )

    new_phase = (comes_from[:, None] * BLOCK + dilation_phase[None, :]).astype(jnp.int32)
    new_cos, new_sin = flat_tables(new_phase, total)
    out = jax.ShapeDtypeStruct((rows, width), jnp.bfloat16)
    number = blocks - 1
    slots = partner.astype(jnp.int32)
    finals = pl.pallas_call(
        functools.partial(place_kernel, number, edge),
        in_specs=[smem] + [anywhere] * (number + 4),
        out_specs=[anywhere] * 4,
        out_shape=[out] * 4,
        input_output_aliases={1 + number + t: t for t in range(4)},
        scratch_shapes=[
            pltpu.VMEM((number, 4, BLOCK, last * HEAD), jnp.bfloat16),
            pltpu.SemaphoreType.DMA((number,)),
            pltpu.SemaphoreType.DMA((number, 4)),
        ],
        compiler_params=big,
        cost_estimate=light,
    )(slots, *parts[:number], *finals)
    return tuple(
        pl.pallas_call(
            functools.partial(patch_kernel, heads, blocks, edge),
            in_specs=[smem, smem, anywhere, vmem, vmem] + [anywhere] * 5,
            out_specs=[anywhere] * 4,
            out_shape=[out] * 4,
            input_output_aliases={6 + t: t for t in range(4)},
            scratch_shapes=[
                pltpu.VMEM((devices, 2 * blocks, width), jnp.bfloat16),
                pltpu.VMEM((2, blocks, BLOCK, width), jnp.bfloat16),
                pltpu.VMEM((2, BLOCK, last * HEAD), jnp.bfloat16),
                pltpu.SemaphoreType.DMA(()),
                pltpu.SemaphoreType.DMA((2, blocks)),
                pltpu.SemaphoreType.DMA((2, blocks)),
                pltpu.SemaphoreType.DMA((4,)),
                pltpu.SemaphoreType.DMA((2,)),
            ],
            compiler_params=big,
        )(
            dilation_phase,
            slots,
            got,
            new_cos,
            new_sin,
            parts[number],
            *finals,
        )
    )


def solution(mesh):
    token = P(("groups", "ctx", "bal"), "head")
    return jax.shard_map(
        local,
        mesh=mesh,
        in_specs=(token, token, token, token, P("head"), P("head"), P("groups")),
        out_specs=(token, token, token, token),
        check_vma=False,
    )
```

```python
import functools
import math

import jax
import jax.numpy as jnp
from jax import lax
from jax.experimental import pallas as pl
from jax.experimental.pallas import tpu as pltpu
from jax.sharding import PartitionSpec as P

BLOCK = 128
HEAD = 128
LOG2E = 1.4426950408889634
NT = (((1,), (1,)), ((), ()))
TN = (((0,), (0,)), ((), ()))


def tables(positions, total):
    half = HEAD // 2
    pair = jnp.arange(half, dtype=jnp.float32)
    inverse = jnp.exp(pair * (-2.0 * math.log(10000.0) / HEAD))
    where = positions.astype(jnp.float32)[..., None]
    angles = where * inverse
    base = (2.0 * pair / HEAD + 0.4) / 1.4
    growth = jnp.exp((2.0 * where - total) / total * jnp.log(base))
    cosine, sine = jnp.cos(angles), jnp.sin(angles)

    def pack(scale):
        first, second = cosine * scale, sine * scale
        return (
            jnp.concatenate([first, first], axis=-1),
            jnp.concatenate([-second, second], axis=-1),
        )

    return pack(growth) + pack(1.0 / growth)


def flat_tables(positions, total):
    half = HEAD // 2
    lane = jnp.arange(positions.shape[1] * HEAD, dtype=jnp.int32) % HEAD
    pair = (lane % half).astype(jnp.float32)
    inverse = jnp.exp(pair * (-2.0 * math.log(10000.0) / HEAD))
    where = jnp.repeat(positions.astype(jnp.float32), HEAD, axis=1)
    angles = where * inverse[None, :]
    base = (2.0 * pair / HEAD + 0.4) / 1.4
    growth = jnp.exp((2.0 * where - total) / total * jnp.log(base)[None, :])
    sine = jnp.where(lane[None, :] < half, -jnp.sin(angles), jnp.sin(angles))
    return jnp.cos(angles) / growth, sine / growth


def dot(left, right, dims=None):
    if dims is None:
        dims = (((1,), (0,)), ((), ()))
    return lax.dot_general(left, right, dims, preferred_element_type=jnp.float32)


def attend_kernel(
    per_step, blocks, count, first, relaid, waits, info, phase, seg, far_ref, other_ref, pull_ref, push_ref, *rest
):
    cq_ref, sq_ref, ck_ref, sk_ref = rest[:4]
    own = rest[4:8]
    rest = rest[8:]
    if relaid:
        come, rest = rest[: blocks - 1], rest[blocks - 1 + relaid :]
        finals, rest = rest[:4], rest[4:]
    else:
        finals, rest = rest[waits : waits + blocks], rest[waits + blocks :]
    (pay_ref,) = rest
    scale = 1.0 / math.sqrt(HEAD)
    key_at = lax.broadcasted_iota(jnp.int32, (BLOCK, BLOCK), 0)
    query_at = lax.broadcasted_iota(jnp.int32, (BLOCK, BLOCK), 1)
    far_at = lax.broadcasted_iota(jnp.int32, (count, BLOCK), 0)
    far_query = lax.broadcasted_iota(jnp.int32, (count, BLOCK), 1)
    half = HEAD // 2
    for sub in range(per_step):
        head = first + pl.program_id(0) * per_step + sub
        lanes = slice(sub * HEAD, (sub + 1) * HEAD)
        held = jnp.concatenate([far_ref[:, lanes], other_ref[:, lanes]], axis=0)
        both = dot(pull_ref[...], held).astype(jnp.bfloat16)
        far_k, far_v = both[:count], both[count:]
        span = seg[head] * blocks
        at = phase[head]
        causal = (key_at <= query_at) & (key_at != at)
        behind = far_at * BLOCK + at - far_query
        p_far, d_far, q_all, g_all = [], [], [], []
        for k in range(blocks):
            if relaid:
                rows = slice(k * BLOCK, (k + 1) * BLOCK)
                source = [ref[:, lanes] for ref in own]
                if k:
                    source = [come[k - 1][t, :, lanes] for t in range(4)]
            else:
                rows = pl.ds(pl.multiple_of(info[k] * BLOCK, BLOCK), BLOCK)
                source = [ref[rows, lanes] for ref in own]
            block = info[blocks + k]
            low = block & (-span)
            cq, sq, ck, sk = cq_ref[rows, :], sq_ref[rows, :], ck_ref[rows, :], sk_ref[rows, :]
            raw_q, raw_k, value, grad = source
            raw_q = raw_q.astype(jnp.float32)
            raw_k = raw_k.astype(jnp.float32)
            tq = (raw_q * cq + pltpu.roll(raw_q, half, 1) * sq).astype(jnp.bfloat16)
            tk = (raw_k * ck + pltpu.roll(raw_k, half, 1) * sk).astype(jnp.bfloat16)
            keys = jnp.concatenate([tk, far_k], axis=0)
            vals = jnp.concatenate([value, far_v], axis=0)
            score = dot(keys, tq, NT)
            allowed = (far_at >= low) & (behind <= block * BLOCK)
            score = jnp.concatenate(
                [
                    jnp.where(causal, score[:BLOCK], -jnp.inf),
                    jnp.where(allowed, score[BLOCK:], -jnp.inf),
                ],
                axis=0,
            )
            top = jnp.max(score, axis=0, keepdims=True)
            weight = jnp.exp2((score - top) * (scale * LOG2E))
            prob = weight * (1.0 / jnp.sum(weight, axis=0, keepdims=True))
            p16 = prob.astype(jnp.bfloat16)
            dprob = dot(vals, grad, NT)
            delta = jnp.sum(p16.astype(jnp.float32) * dprob, axis=0, keepdims=True)
            d16 = (prob * (dprob - delta)).astype(jnp.bfloat16)
            out = dot(p16, vals, TN)
            dq = dot(d16, keys, TN) * scale
            dk = dot(d16[:BLOCK], tq) * scale
            dv = dot(p16[:BLOCK], grad)
            made = (
                out,
                dq * cq - pltpu.roll(dq, half, 1) * sq,
                dk * ck - pltpu.roll(dk, half, 1) * sk,
                dv,
            )
            for t in range(4):
                if relaid:
                    finals[t][info[2 * blocks + k], :, lanes] = made[t].astype(jnp.bfloat16)
                else:
                    finals[k][t, :, lanes] = made[t].astype(jnp.bfloat16)
            p_far.append(p16[BLOCK:])
            d_far.append(d16[BLOCK:])
            q_all.append(tq)
            g_all.append(grad)
        far_dk = dot(jnp.concatenate(d_far, axis=1), jnp.concatenate(q_all, axis=0)) * scale
        far_dv = dot(jnp.concatenate(p_far, axis=1), jnp.concatenate(g_all, axis=0))
        far_sum = jnp.concatenate([far_dk, far_dv], axis=0).astype(jnp.bfloat16)
        pay_ref[:, lanes] = dot(push_ref[...], far_sum).astype(jnp.bfloat16)


def pick_kernel(
    heads, blocks, phase, k_hbm, v_hbm, cos_ref, sin_ref, after, out_ref, k_ref, v_ref, row_ref,
    load, save
):
    moves = [
        pltpu.make_async_copy(k_hbm, k_ref, load.at[0]),
        pltpu.make_async_copy(v_hbm, v_ref, load.at[1]),
    ]
    for move in moves:
        move.start()
    for move in moves:
        move.wait()
    spot = lax.broadcasted_iota(jnp.int32, (16, HEAD), 0)
    for head in range(heads):
        at = phase[head]
        start = pl.multiple_of(at // 16 * 16, 16)
        lanes = slice(head * HEAD, (head + 1) * HEAD)
        both = []
        for ref in (k_ref, v_ref):
            rows = []
            for k in range(blocks):
                tile = ref[pl.ds(pl.multiple_of(k * BLOCK + start, 16), 16), lanes]
                tile = jnp.where(spot == at - start, tile.astype(jnp.float32), 0.0)
                rows.append(jnp.sum(tile, axis=0, keepdims=True))
            both.append(jnp.concatenate(rows, axis=0))
        key, value = both
        key = key * cos_ref[:, lanes] + pltpu.roll(key, HEAD // 2, 1) * sin_ref[:, lanes]
        row_ref[:, lanes] = jnp.concatenate([key, value], axis=0).astype(jnp.bfloat16)
    copies = [
        pltpu.make_async_copy(row_ref, out_ref.at[d], save.at[d]) for d in range(out_ref.shape[0])
    ]
    for copy in copies:
        copy.start()
    for copy in copies:
        copy.wait()


def pack_kernel(jobs, info, after, *rest):
    number = len(jobs)
    inputs, rest = rest[:4], rest[4:]
    outs, rooms, (load, save) = rest[:number], rest[number : 2 * number], rest[2 * number :]
    order = [(job, t) for job in range(number) for t in range(4)]

    def fetch(job, t):
        k, start, width = jobs[job]
        rows = pl.ds(pl.multiple_of(info[k] * BLOCK, BLOCK), BLOCK)
        source = inputs[t].at[rows, pl.ds(start, width)]
        return pltpu.make_async_copy(source, rooms[job].at[t], load.at[job, t])

    def store(job, t):
        return pltpu.make_async_copy(rooms[job].at[t], outs[job].at[t], save.at[job, t])

    for job, t in order:
        fetch(job, t).start()
    for job, t in order:
        fetch(job, t).wait()
        store(job, t).start()
    for job, t in order:
        store(job, t).wait()


def link_kernel(*refs):
    pass


def place_kernel(items, slot, *rest):
    number = len(items)
    parts = rest[:number]
    finals = rest[number + 4 : number + 8]
    rooms, (load, save) = rest[number + 8 : 2 * number + 8], rest[2 * number + 8 :]

    def save_of(i, t):
        k, start, width = items[i]
        top = pl.multiple_of(slot[k] * BLOCK, BLOCK)
        where = finals[t].at[pl.ds(top, BLOCK), pl.ds(start, width)]
        return pltpu.make_async_copy(rooms[i].at[t], where, save.at[i, t])

    loads = [pltpu.make_async_copy(parts[i], rooms[i], load.at[i]) for i in range(number)]
    for move in loads:
        move.start()
    for i in range(number):
        loads[i].wait()
        for t in range(4):
            save_of(i, t).start()
    for i in range(number):
        for t in range(4):
            save_of(i, t).wait()


def far_rows(got, cos_ref, sin_ref, blocks):
    total = got[0].astype(jnp.float32)
    for sender in range(1, got.shape[0]):
        total = total + got[sender].astype(jnp.float32)
    far_k, far_v = total[:blocks], total[blocks:]
    heads = far_k.shape[1] // HEAD
    turned = []
    for head in range(heads):
        lanes = slice(head * HEAD, (head + 1) * HEAD)
        one = far_k[:, lanes]
        turned.append(
            one * cos_ref[:, lanes] - pltpu.roll(one, HEAD // 2, 1) * sin_ref[:, lanes]
        )
    values = [far_v[:, head * HEAD : (head + 1) * HEAD] for head in range(heads)]
    return turned, values


def overwrite(ref, lanes, at, source, pick):
    spot = lax.broadcasted_iota(jnp.int32, (16, HEAD), 0)
    line = lax.broadcasted_iota(jnp.int32, source.shape, 0)
    start = pl.multiple_of(at // 16 * 16, 16)
    row = jnp.sum(jnp.where(line == pick, source, 0.0), axis=0, keepdims=True)
    old = ref[pl.ds(start, 16), lanes].astype(jnp.float32)
    ref[pl.ds(start, 16), lanes] = jnp.where(spot == at - start, row, old).astype(jnp.bfloat16)


def patch_kernel(
    heads, blocks, late, edge, phase, slot, got_hbm, cos_ref, sin_ref, dk_in, dv_in, dk, dv, got,
    room, get, load, save
):
    outs = (dk, dv)
    width = room.shape[-1]
    order = [(k, t) for k in range(blocks) for t in range(2)]

    def span(k):
        return pl.ds(0, edge if k in late else width)

    def here(t, k):
        rows = pl.ds(pl.multiple_of(slot[k] * BLOCK, BLOCK), BLOCK)
        return outs[t].at[rows, span(k)]

    def fetch(t, k):
        return pltpu.make_async_copy(here(t, k), room.at[t, k, :, span(k)], load.at[t, k])

    def store(t, k):
        return pltpu.make_async_copy(room.at[t, k, :, span(k)], here(t, k), save.at[t, k])

    first = pltpu.make_async_copy(got_hbm, got, get)
    first.start()
    for k, t in order:
        fetch(t, k).start()
    first.wait()
    fresh = far_rows(got, cos_ref, sin_ref, blocks)
    for k, t in order:
        fetch(t, k).wait()
        for head in range(edge // HEAD if k in late else heads):
            lanes = slice(head * HEAD, (head + 1) * HEAD)
            overwrite(room.at[t, k], lanes, phase[head], fresh[t][head], slot[k])
        store(t, k).start()
    for k, t in order:
        store(t, k).wait()


def last_kernel(heads, blocks, late, edge, phase, slot, got_hbm, cos_ref, sin_ref, *rest):
    number = len(late)
    parts = rest[:number]
    outs = rest[number + 4 : number + 8]
    got, room, get, load, save = rest[number + 8 :]
    right = pl.ds(edge, room.shape[-1])

    def store(i, t):
        rows = pl.ds(pl.multiple_of(slot[late[i]] * BLOCK, BLOCK), BLOCK)
        return pltpu.make_async_copy(room.at[i, t], outs[t].at[rows, right], save.at[i, t])

    first = pltpu.make_async_copy(got_hbm.at[:, :, right], got, get)
    loads = [pltpu.make_async_copy(parts[i], room.at[i], load.at[i]) for i in range(number)]
    for move in loads + [first]:
        move.start()
    for i in range(number):
        loads[i].wait()
        for t in range(2):
            store(i, t).start()
    first.wait()
    fresh = far_rows(got, cos_ref, sin_ref, blocks)
    for i in range(number):
        for t in range(2):
            for head in range(edge // HEAD, heads):
                local_head = head - edge // HEAD
                lanes = slice(local_head * HEAD, (local_head + 1) * HEAD)
                source = fresh[t][local_head]
                overwrite(room.at[i, 2 + t], lanes, phase[head], source, slot[late[i]])
            store(i, 2 + t).start()
    for i in range(number):
        for t in range(4):
            store(i, t).wait()


def local(queries, keys, values, output_gradient, dilation_phase, segment_device_count, owner):
    rows, width = queries.shape
    heads = width // HEAD
    blocks = rows // BLOCK
    bal_size = lax.axis_size("bal")
    devices = lax.axis_size("ctx") * bal_size
    total = rows * devices
    count = owner.shape[0]
    assert blocks == bal_size == 4 and bal_size & (bal_size - 1) == 0
    bal = lax.axis_index("bal")
    device = lax.axis_index("ctx") * bal_size + bal
    room = 66_000_000
    big = pltpu.CompilerParams(vmem_limit_bytes=room)
    smem = pl.BlockSpec(memory_space=pltpu.SMEM)
    vmem = pl.BlockSpec(memory_space=pltpu.VMEM)
    anywhere = pl.BlockSpec(memory_space=pl.ANY)
    light = pl.CostEstimate(flops=2_000_000_000, bytes_accessed=5_000_000, transcendentals=0)
    heavy = pl.CostEstimate(flops=20_000_000_000, bytes_accessed=60_000_000, transcendentals=0)

    def tokens_of(ids):
        return (ids[:, None] * BLOCK + jnp.arange(BLOCK, dtype=jnp.int32)[None, :]).reshape(rows)

    def swap(array, k):
        return lax.ppermute(array, "bal", [(i, i ^ k) for i in range(bal_size)])

    steps = jnp.arange(blocks, dtype=jnp.int32)
    held = device * blocks + steps
    goes_to = lax.dynamic_slice_in_dim(owner, device * blocks, blocks) // blocks % bal_size
    partner = steps ^ bal
    which = jnp.sum(jnp.where(goes_to[None, :] == partner[:, None], steps[None, :], 0), axis=1)
    info = jnp.concatenate([which, device * blocks + which]).astype(jnp.int32)
    comes_from = jnp.sum(
        jnp.where(
            owner[None, :] == held[:, None], jnp.arange(count, dtype=jnp.int32)[None, :], 0
        ),
        axis=1,
    )

    first = heads * 3 // 10 * 2
    early = first // 4 * 2
    middle = heads - 2
    cut, edge, brim = early * HEAD, first * HEAD, middle * HEAD
    originals = (queries, keys, values, output_gradient)

    def send_inputs(jobs, after):
        sizes = [(4, BLOCK, width) for _, _, width in jobs]
        sent = pl.pallas_call(
            functools.partial(pack_kernel, jobs),
            in_specs=[smem] + [anywhere] * 5,
            out_specs=[anywhere] * len(jobs),
            out_shape=[jax.ShapeDtypeStruct(size, jnp.bfloat16) for size in sizes],
            scratch_shapes=[pltpu.VMEM(size, jnp.bfloat16) for size in sizes]
            + [pltpu.SemaphoreType.DMA((len(jobs), 4))] * 2,
            compiler_params=big,
        )(info, after, *originals)
        return sent, [swap(one, job[0]) for one, job in zip(sent, jobs)]

    sent, come_early = send_inputs([(2, 0, cut)], owner)

    cq, sq, ck, sk = tables(tokens_of(held), total)
    own_phase = (held[:, None] * BLOCK + dilation_phase[None, :]).astype(jnp.int32)
    pick_cos, pick_sin = flat_tables(own_phase, total)
    own_far = pl.pallas_call(
        functools.partial(pick_kernel, heads, blocks),
        in_specs=[smem, anywhere, anywhere, vmem, vmem, anywhere],
        out_specs=anywhere,
        out_shape=jax.ShapeDtypeStruct((devices // 2, 2 * blocks, width), jnp.bfloat16),
        scratch_shapes=[
            pltpu.VMEM((rows, width), jnp.bfloat16),
            pltpu.VMEM((rows, width), jnp.bfloat16),
            pltpu.VMEM((2 * blocks, width), jnp.bfloat16),
            pltpu.SemaphoreType.DMA((2,)),
            pltpu.SemaphoreType.DMA((devices // 2,)),
        ],
        compiler_params=big,
    )(
        dilation_phase,
        keys,
        values,
        pick_cos,
        pick_sin,
        sent[0],
    )
    halves = [list(range(0, devices, 2)), list(range(1, devices, 2))]
    near_far = lax.all_to_all(
        own_far,
        ("ctx", "bal"),
        split_axis=0,
        concat_axis=0,
        tiled=True,
        axis_index_groups=halves,
    ).reshape(count, width)
    other_far = swap(near_far, 1)
    jobs = [(2, cut, edge - cut), (3, 0, edge), (1, 0, edge)]
    _, (come_rest, come_3, come_1) = send_inputs(jobs, own_far)
    come_2 = come_early[0]

    ids = (device ^ steps) * blocks
    came = jnp.sum(
        jnp.where(comes_from[None, :] // blocks * blocks == ids[:, None], comes_from[None, :], 0),
        axis=1,
    )
    moved = jnp.concatenate([which, came, partner]).astype(jnp.int32)
    moved_tables = tables(tokens_of(came), total)

    side = 2 * count
    wide = jnp.arange(side, dtype=jnp.int32)
    tall = wide[:, None]
    wide = wide[None, :]
    source = tall % count
    holder = source // blocks
    held_row = (holder ^ device) % 2 * count + holder // 2 * (2 * blocks)
    pull = (wide == held_row + tall // count * blocks + source % blocks).astype(jnp.bfloat16)
    lands = owner // blocks * (2 * blocks) + owner % blocks
    push = (jnp.concatenate([lands, lands + blocks])[None, :] == tall).astype(jnp.bfloat16)

    per_step = 2
    columns = per_step * HEAD
    fixed = lambda h, *_: (0, 0)
    square = pl.BlockSpec((side, side), fixed)
    table = pl.BlockSpec((rows, HEAD), fixed)
    part = pl.BlockSpec((4, BLOCK, columns), lambda h, *_: (0, 0, h))
    def attend_held(begin, end, waits, carried):
        skip = begin // per_step
        tensor = pl.BlockSpec((rows, columns), lambda h, *_: (0, h + skip))
        lane = pl.BlockSpec((side, columns), lambda h, *_: (0, h + skip))
        far = pl.BlockSpec((count, columns), lambda h, *_: (0, h + skip))
        extra = carried + waits
        results = pl.pallas_call(
            functools.partial(attend_kernel, per_step, blocks, count, begin, 0, len(extra)),
            grid_spec=pltpu.PrefetchScalarGridSpec(
                num_scalar_prefetch=3,
                grid=((end - begin) // per_step,),
                in_specs=[far, far, square, square]
                + [table] * 4
                + [tensor] * 4
                + [anywhere] * len(extra),
                out_specs=[part] * blocks + [lane],
            ),
            out_shape=[jax.ShapeDtypeStruct((4, BLOCK, (end - begin) * HEAD), jnp.bfloat16)]
            * blocks
            + [jax.ShapeDtypeStruct((side, width), jnp.bfloat16)],
            input_output_aliases={15 + i: blocks for i in range(len(carried))},
            compiler_params=big,
            cost_estimate=heavy,
        )(
            info,
            dilation_phase,
            segment_device_count,
            near_far,
            other_far,
            pull,
            push,
            cq,
            sq,
            ck,
            sk,
            *originals,
            *extra,
        )
        return list(results[:blocks]), results[blocks]

    waits = list(moved_tables) + [come_1, come_2]
    parts, payload = attend_held(first, middle, waits, [])
    parts_last, payload = attend_held(middle, heads, [], [payload])
    for k in range(1, blocks):
        parts[k] = swap(parts[k], k)
        parts_last[k] = swap(parts_last[k], k)

    shapes = [jax.ShapeDtypeStruct((blocks, BLOCK, width), jnp.bfloat16)] * 4
    shapes = shapes + [jax.ShapeDtypeStruct((side, width), jnp.bfloat16)]

    def attend_relaid(begin, end, come, carried):
        skip = begin // per_step
        tensor = pl.BlockSpec((BLOCK, columns), lambda h, info, *_: (info[0], h + skip))
        lane = pl.BlockSpec((side, columns), lambda h, *_: (0, h + skip))
        far = pl.BlockSpec((count, columns), lambda h, *_: (0, h + skip))
        whole = pl.BlockSpec((blocks, BLOCK, columns), lambda h, *_: (0, 0, h + skip))
        shifted = pl.BlockSpec((4, BLOCK, columns), lambda h, *_: (0, 0, h + skip))
        operands = 3 + 4 + 4 + 4 + blocks - 1
        return pl.pallas_call(
            functools.partial(attend_kernel, per_step, blocks, count, begin, len(carried), 0),
            grid_spec=pltpu.PrefetchScalarGridSpec(
                num_scalar_prefetch=3,
                grid=((end - begin) // per_step,),
                in_specs=[far, far, square, square]
                + [table] * 4
                + [tensor] * 4
                + [shifted, part, shifted]
                + [anywhere] * len(carried),
                out_specs=[whole] * 4 + [lane],
                ),
            out_shape=shapes,
            input_output_aliases={
                operands + i: 5 - len(carried) + i for i in range(len(carried))
            },
            compiler_params=big,
            cost_estimate=light,
        )(
            moved,
            dilation_phase,
            segment_device_count,
            near_far,
            other_far,
            pull,
            push,
            *moved_tables,
            *originals,
            *come,
            *carried,
        )

    results = attend_relaid(0, early, [come_1, come_2, come_3], [payload])
    results = attend_relaid(early, first, [come_1, come_rest, come_3], results)
    finals, payload = [one.reshape(rows, width) for one in results[:4]], results[4]
    payload = pl.pallas_call(
        link_kernel,
        in_specs=[anywhere] * 3,
        out_specs=anywhere,
        out_shape=jax.ShapeDtypeStruct((side, width), jnp.bfloat16),
        input_output_aliases={0: 0},
        compiler_params=pltpu.CompilerParams(
            vmem_limit_bytes=room, has_side_effects=True
        ),
    )(payload, parts[2], parts[3])
    got = lax.all_to_all(
        payload.reshape(devices, 2 * blocks, width),
        ("ctx", "bal"),
        split_axis=0,
        concat_axis=0,
        tiled=True,
    )

    new_phase = (comes_from[:, None] * BLOCK + dilation_phase[None, :]).astype(jnp.int32)
    new_cos, new_sin = flat_tables(new_phase, total)
    out = jax.ShapeDtypeStruct((rows, width), jnp.bfloat16)
    slots = partner.astype(jnp.int32)
    items = [(k, edge, brim - edge) for k in range(blocks)]
    items += [(k, brim, width - brim) for k in range(2)]
    number = len(items)
    finals = pl.pallas_call(
        functools.partial(place_kernel, items),
        in_specs=[smem] + [anywhere] * (number + 4),
        out_specs=[anywhere] * 4,
        out_shape=[out] * 4,
        input_output_aliases={1 + number + t: t for t in range(4)},
        scratch_shapes=[pltpu.VMEM((4, BLOCK, item[2]), jnp.bfloat16) for item in items]
        + [pltpu.SemaphoreType.DMA((number,)), pltpu.SemaphoreType.DMA((number, 4))],
        compiler_params=big,
        cost_estimate=light,
    )(slots, *parts, *parts_last[:2], *finals)
    late = (2, 3)
    patched = pl.pallas_call(
        functools.partial(patch_kernel, heads, blocks, late, brim),
        in_specs=[smem, smem, anywhere, vmem, vmem, anywhere, anywhere],
        out_specs=[anywhere] * 2,
        out_shape=[out] * 2,
        input_output_aliases={5: 0, 6: 1},
        scratch_shapes=[
            pltpu.VMEM((devices, 2 * blocks, width), jnp.bfloat16),
            pltpu.VMEM((2, blocks, BLOCK, width), jnp.bfloat16),
            pltpu.SemaphoreType.DMA(()),
            pltpu.SemaphoreType.DMA((2, blocks)),
            pltpu.SemaphoreType.DMA((2, blocks)),
        ],
        compiler_params=big,
        cost_estimate=light,
    )(dilation_phase, slots, got, new_cos, new_sin, finals[2], finals[3])
    return tuple(
        pl.pallas_call(
            functools.partial(last_kernel, heads, blocks, late, brim),
            in_specs=[smem, smem, anywhere, vmem, vmem] + [anywhere] * 6,
            out_specs=[anywhere] * 4,
            out_shape=[out] * 4,
            input_output_aliases={7 + t: t for t in range(4)},
            scratch_shapes=[
                pltpu.VMEM((devices, 2 * blocks, width - brim), jnp.bfloat16),
                pltpu.VMEM((2, 4, BLOCK, width - brim), jnp.bfloat16),
                pltpu.SemaphoreType.DMA(()),
                pltpu.SemaphoreType.DMA((2,)),
                pltpu.SemaphoreType.DMA((2, 4)),
            ],
            compiler_params=big,
        )(
            dilation_phase,
            slots,
            got,
            new_cos[:, brim:],
            new_sin[:, brim:],
            *parts_last[2:],
            finals[0],
            finals[1],
            *patched,
        )
    )


def solution(mesh):
    token = P(("groups", "ctx", "bal"), "head")
    return jax.shard_map(
        local,
        mesh=mesh,
        in_specs=(token, token, token, token, P("head"), P("head"), P("groups")),
        out_specs=(token, token, token, token),
        check_vma=False,
    )
```

```python
import functools
import math

import jax
import jax.numpy as jnp
from jax import lax
from jax.experimental import pallas as pl
from jax.experimental.pallas import tpu as pltpu
from jax.sharding import PartitionSpec as P

BLOCK = 128
HEAD = 128
LOG2E = 1.4426950408889634
NT = (((1,), (1,)), ((), ()))
TN = (((0,), (0,)), ((), ()))


def tables(positions, total):
    half = HEAD // 2
    pair = jnp.arange(half, dtype=jnp.float32)
    inverse = jnp.exp(pair * (-2.0 * math.log(10000.0) / HEAD))
    where = positions.astype(jnp.float32)[..., None]
    angles = where * inverse
    base = (2.0 * pair / HEAD + 0.4) / 1.4
    growth = jnp.exp((2.0 * where - total) / total * jnp.log(base))
    cosine, sine = jnp.cos(angles), jnp.sin(angles)

    def pack(scale):
        first, second = cosine * scale, sine * scale
        return (
            jnp.concatenate([first, first], axis=-1),
            jnp.concatenate([-second, second], axis=-1),
        )

    return pack(growth) + pack(1.0 / growth)


def flat_tables(positions, total):
    half = HEAD // 2
    lane = jnp.arange(positions.shape[1] * HEAD, dtype=jnp.int32) % HEAD
    pair = (lane % half).astype(jnp.float32)
    inverse = jnp.exp(pair * (-2.0 * math.log(10000.0) / HEAD))
    where = jnp.repeat(positions.astype(jnp.float32), HEAD, axis=1)
    angles = where * inverse[None, :]
    base = (2.0 * pair / HEAD + 0.4) / 1.4
    growth = jnp.exp((2.0 * where - total) / total * jnp.log(base)[None, :])
    sine = jnp.where(lane[None, :] < half, -jnp.sin(angles), jnp.sin(angles))
    return jnp.cos(angles) / growth, sine / growth


def dot(left, right, dims=None):
    if dims is None:
        dims = (((1,), (0,)), ((), ()))
    return lax.dot_general(left, right, dims, preferred_element_type=jnp.float32)


def attend_kernel(
    per_step, blocks, count, first, relaid, waits, info, phase, seg, far_ref, other_ref, pull_ref, push_ref, *rest
):
    cq_ref, sq_ref, ck_ref, sk_ref = rest[:4]
    own = rest[4:8]
    rest = rest[8:]
    if relaid:
        come, rest = rest[: blocks - 1], rest[blocks - 1 + relaid :]
        finals, rest = rest[:4], rest[4:]
    else:
        finals, rest = rest[waits : waits + blocks], rest[waits + blocks :]
    own_pay, other_pay = rest
    scale = 1.0 / math.sqrt(HEAD)
    key_at = lax.broadcasted_iota(jnp.int32, (BLOCK, BLOCK), 0)
    query_at = lax.broadcasted_iota(jnp.int32, (BLOCK, BLOCK), 1)
    far_at = lax.broadcasted_iota(jnp.int32, (count, BLOCK), 0)
    far_query = lax.broadcasted_iota(jnp.int32, (count, BLOCK), 1)
    half = HEAD // 2
    for sub in range(per_step):
        head = first + pl.program_id(0) * per_step + sub
        lanes = slice(sub * HEAD, (sub + 1) * HEAD)
        held = jnp.concatenate([far_ref[:, lanes], other_ref[:, lanes]], axis=0)
        both = dot(pull_ref[...], held).astype(jnp.bfloat16)
        far_k, far_v = both[:count], both[count:]
        span = seg[head] * blocks
        at = phase[head]
        causal = (key_at <= query_at) & (key_at != at)
        behind = far_at * BLOCK + at - far_query
        p_far, d_far, q_all, g_all = [], [], [], []
        for k in range(blocks):
            if relaid:
                rows = slice(k * BLOCK, (k + 1) * BLOCK)
                source = [ref[:, lanes] for ref in own]
                if k:
                    source = [come[k - 1][t, :, lanes] for t in range(4)]
            else:
                rows = pl.ds(pl.multiple_of(info[k] * BLOCK, BLOCK), BLOCK)
                source = [ref[rows, lanes] for ref in own]
            block = info[blocks + k]
            low = block & (-span)
            cq, sq, ck, sk = cq_ref[rows, :], sq_ref[rows, :], ck_ref[rows, :], sk_ref[rows, :]
            raw_q, raw_k, value, grad = source
            raw_q = raw_q.astype(jnp.float32)
            raw_k = raw_k.astype(jnp.float32)
            tq = (raw_q * cq + pltpu.roll(raw_q, half, 1) * sq).astype(jnp.bfloat16)
            tk = (raw_k * ck + pltpu.roll(raw_k, half, 1) * sk).astype(jnp.bfloat16)
            keys = jnp.concatenate([tk, far_k], axis=0)
            vals = jnp.concatenate([value, far_v], axis=0)
            score = dot(keys, tq, NT)
            allowed = (far_at >= low) & (behind <= block * BLOCK)
            score = jnp.concatenate(
                [
                    jnp.where(causal, score[:BLOCK], -jnp.inf),
                    jnp.where(allowed, score[BLOCK:], -jnp.inf),
                ],
                axis=0,
            )
            top = jnp.max(score, axis=0, keepdims=True)
            weight = jnp.exp2((score - top) * (scale * LOG2E))
            prob = weight * (1.0 / jnp.sum(weight, axis=0, keepdims=True))
            p16 = prob.astype(jnp.bfloat16)
            dprob = dot(vals, grad, NT)
            delta = jnp.sum(p16.astype(jnp.float32) * dprob, axis=0, keepdims=True)
            d16 = (prob * (dprob - delta)).astype(jnp.bfloat16)
            out = dot(p16, vals, TN)
            dq = dot(d16, keys, TN) * scale
            dk = dot(d16[:BLOCK], tq) * scale
            dv = dot(p16[:BLOCK], grad)
            made = (
                out,
                dq * cq - pltpu.roll(dq, half, 1) * sq,
                dk * ck - pltpu.roll(dk, half, 1) * sk,
                dv,
            )
            for t in range(4):
                if relaid:
                    finals[t][info[2 * blocks + k], :, lanes] = made[t].astype(jnp.bfloat16)
                else:
                    finals[k][t, :, lanes] = made[t].astype(jnp.bfloat16)
            p_far.append(p16[BLOCK:])
            d_far.append(d16[BLOCK:])
            q_all.append(tq)
            g_all.append(grad)
        far_dk = dot(jnp.concatenate(d_far, axis=1), jnp.concatenate(q_all, axis=0)) * scale
        far_dv = dot(jnp.concatenate(p_far, axis=1), jnp.concatenate(g_all, axis=0))
        far_sum = jnp.concatenate([far_dk, far_dv], axis=0).astype(jnp.bfloat16)
        pay = dot(push_ref[...], far_sum).astype(jnp.bfloat16)
        own_pay[:, lanes] = pay[:count]
        other_pay[:, lanes] = pay[count:]


def pick_kernel(
    heads, blocks, phase, k_hbm, v_hbm, cos_ref, sin_ref, after, out_ref, k_ref, v_ref, row_ref,
    load, save
):
    moves = [
        pltpu.make_async_copy(k_hbm, k_ref, load.at[0]),
        pltpu.make_async_copy(v_hbm, v_ref, load.at[1]),
    ]
    for move in moves:
        move.start()
    for move in moves:
        move.wait()
    spot = lax.broadcasted_iota(jnp.int32, (16, HEAD), 0)
    for head in range(heads):
        at = phase[head]
        start = pl.multiple_of(at // 16 * 16, 16)
        lanes = slice(head * HEAD, (head + 1) * HEAD)
        both = []
        for ref in (k_ref, v_ref):
            rows = []
            for k in range(blocks):
                tile = ref[pl.ds(pl.multiple_of(k * BLOCK + start, 16), 16), lanes]
                tile = jnp.where(spot == at - start, tile.astype(jnp.float32), 0.0)
                rows.append(jnp.sum(tile, axis=0, keepdims=True))
            both.append(jnp.concatenate(rows, axis=0))
        key, value = both
        key = key * cos_ref[:, lanes] + pltpu.roll(key, HEAD // 2, 1) * sin_ref[:, lanes]
        row_ref[:, lanes] = jnp.concatenate([key, value], axis=0).astype(jnp.bfloat16)
    copies = [
        pltpu.make_async_copy(row_ref, out_ref.at[d], save.at[d]) for d in range(out_ref.shape[0])
    ]
    for copy in copies:
        copy.start()
    for copy in copies:
        copy.wait()


def pack_kernel(jobs, info, after, *rest):
    number = len(jobs)
    inputs, rest = rest[:4], rest[4:]
    outs, rooms, (load, save) = rest[:number], rest[number : 2 * number], rest[2 * number :]
    order = [(job, t) for job in range(number) for t in range(4)]

    def fetch(job, t):
        k, start, width = jobs[job]
        rows = pl.ds(pl.multiple_of(info[k] * BLOCK, BLOCK), BLOCK)
        source = inputs[t].at[rows, pl.ds(start, width)]
        return pltpu.make_async_copy(source, rooms[job].at[t], load.at[job, t])

    def store(job, t):
        return pltpu.make_async_copy(rooms[job].at[t], outs[job].at[t], save.at[job, t])

    for job, t in order:
        fetch(job, t).start()
    for job, t in order:
        fetch(job, t).wait()
        store(job, t).start()
    for job, t in order:
        store(job, t).wait()


def link_kernel(*refs):
    pass


def place_kernel(items, slot, *rest):
    number = len(items)
    parts = rest[:number]
    finals = rest[number + 4 : number + 8]
    rooms, (load, save) = rest[number + 8 : 2 * number + 8], rest[2 * number + 8 :]

    def save_of(i, t):
        k, start, width = items[i]
        top = pl.multiple_of(slot[k] * BLOCK, BLOCK)
        where = finals[t].at[pl.ds(top, BLOCK), pl.ds(start, width)]
        return pltpu.make_async_copy(rooms[i].at[t], where, save.at[i, t])

    loads = [pltpu.make_async_copy(parts[i], rooms[i], load.at[i]) for i in range(number)]
    for move in loads:
        move.start()
    for i in range(number):
        loads[i].wait()
        for t in range(4):
            save_of(i, t).start()
    for i in range(number):
        for t in range(4):
            save_of(i, t).wait()


def far_rows(got, cos_ref, sin_ref, blocks):
    total = got[0].astype(jnp.float32)
    for sender in range(1, got.shape[0]):
        total = total + got[sender].astype(jnp.float32)
    far_k, far_v = total[:blocks], total[blocks:]
    heads = far_k.shape[1] // HEAD
    turned = []
    for head in range(heads):
        lanes = slice(head * HEAD, (head + 1) * HEAD)
        one = far_k[:, lanes]
        turned.append(
            one * cos_ref[:, lanes] - pltpu.roll(one, HEAD // 2, 1) * sin_ref[:, lanes]
        )
    values = [far_v[:, head * HEAD : (head + 1) * HEAD] for head in range(heads)]
    return turned, values


def overwrite(ref, lanes, at, source, pick):
    spot = lax.broadcasted_iota(jnp.int32, (16, HEAD), 0)
    line = lax.broadcasted_iota(jnp.int32, source.shape, 0)
    start = pl.multiple_of(at // 16 * 16, 16)
    row = jnp.sum(jnp.where(line == pick, source, 0.0), axis=0, keepdims=True)
    old = ref[pl.ds(start, 16), lanes].astype(jnp.float32)
    ref[pl.ds(start, 16), lanes] = jnp.where(spot == at - start, row, old).astype(jnp.bfloat16)


def patch_kernel(
    heads, blocks, late, edge, phase, slot, got_hbm, cos_ref, sin_ref, dk_in, dv_in, dk, dv, got,
    room, get, load, save
):
    outs = (dk, dv)
    width = room.shape[-1]
    order = [(k, t) for k in range(blocks) for t in range(2)]

    def span(k):
        return pl.ds(0, edge if k in late else width)

    def here(t, k):
        rows = pl.ds(pl.multiple_of(slot[k] * BLOCK, BLOCK), BLOCK)
        return outs[t].at[rows, span(k)]

    def fetch(t, k):
        return pltpu.make_async_copy(here(t, k), room.at[t, k, :, span(k)], load.at[t, k])

    def store(t, k):
        return pltpu.make_async_copy(room.at[t, k, :, span(k)], here(t, k), save.at[t, k])

    first = pltpu.make_async_copy(got_hbm, got, get)
    first.start()
    for k, t in order:
        fetch(t, k).start()
    first.wait()
    fresh = far_rows(got, cos_ref, sin_ref, blocks)
    for k, t in order:
        fetch(t, k).wait()
        for head in range(edge // HEAD if k in late else heads):
            lanes = slice(head * HEAD, (head + 1) * HEAD)
            overwrite(room.at[t, k], lanes, phase[head], fresh[t][head], slot[k])
        store(t, k).start()
    for k, t in order:
        store(t, k).wait()


def last_kernel(heads, blocks, late, edge, phase, slot, got_hbm, cos_ref, sin_ref, *rest):
    number = len(late)
    parts = rest[:number]
    outs = rest[number + 4 : number + 8]
    got, room, get, load, save = rest[number + 8 :]
    right = pl.ds(edge, room.shape[-1])

    def store(i, t):
        rows = pl.ds(pl.multiple_of(slot[late[i]] * BLOCK, BLOCK), BLOCK)
        return pltpu.make_async_copy(room.at[i, t], outs[t].at[rows, right], save.at[i, t])

    first = pltpu.make_async_copy(got_hbm.at[:, :, right], got, get)
    loads = [pltpu.make_async_copy(parts[i], room.at[i], load.at[i]) for i in range(number)]
    for move in loads + [first]:
        move.start()
    for i in range(number):
        loads[i].wait()
        for t in range(2):
            store(i, t).start()
    first.wait()
    fresh = far_rows(got, cos_ref, sin_ref, blocks)
    for i in range(number):
        for t in range(2):
            for head in range(edge // HEAD, heads):
                local_head = head - edge // HEAD
                lanes = slice(local_head * HEAD, (local_head + 1) * HEAD)
                source = fresh[t][local_head]
                overwrite(room.at[i, 2 + t], lanes, phase[head], source, slot[late[i]])
            store(i, 2 + t).start()
    for i in range(number):
        for t in range(4):
            store(i, t).wait()


def local(queries, keys, values, output_gradient, dilation_phase, segment_device_count, owner):
    rows, width = queries.shape
    heads = width // HEAD
    blocks = rows // BLOCK
    bal_size = lax.axis_size("bal")
    devices = lax.axis_size("ctx") * bal_size
    total = rows * devices
    count = owner.shape[0]
    assert blocks == bal_size == 4 and bal_size & (bal_size - 1) == 0
    bal = lax.axis_index("bal")
    device = lax.axis_index("ctx") * bal_size + bal
    room = 66_000_000
    big = pltpu.CompilerParams(vmem_limit_bytes=room)
    smem = pl.BlockSpec(memory_space=pltpu.SMEM)
    vmem = pl.BlockSpec(memory_space=pltpu.VMEM)
    anywhere = pl.BlockSpec(memory_space=pl.ANY)
    light = pl.CostEstimate(flops=2_000_000_000, bytes_accessed=5_000_000, transcendentals=0)
    heavy = pl.CostEstimate(flops=20_000_000_000, bytes_accessed=60_000_000, transcendentals=0)

    def tokens_of(ids):
        return (ids[:, None] * BLOCK + jnp.arange(BLOCK, dtype=jnp.int32)[None, :]).reshape(rows)

    def swap(array, k):
        return lax.ppermute(array, "bal", [(i, i ^ k) for i in range(bal_size)])

    steps = jnp.arange(blocks, dtype=jnp.int32)
    held = device * blocks + steps
    goes_to = lax.dynamic_slice_in_dim(owner, device * blocks, blocks) // blocks % bal_size
    partner = steps ^ bal
    which = jnp.sum(jnp.where(goes_to[None, :] == partner[:, None], steps[None, :], 0), axis=1)
    info = jnp.concatenate([which, device * blocks + which]).astype(jnp.int32)
    comes_from = jnp.sum(
        jnp.where(
            owner[None, :] == held[:, None], jnp.arange(count, dtype=jnp.int32)[None, :], 0
        ),
        axis=1,
    )

    first = heads * 3 // 10 * 2
    early = first // 4 * 2
    middle = first + (heads - first) // 4 * 2
    cut, edge, brim = early * HEAD, first * HEAD, middle * HEAD
    originals = (queries, keys, values, output_gradient)

    def send_inputs(jobs, after):
        sizes = [(4, BLOCK, width) for _, _, width in jobs]
        sent = pl.pallas_call(
            functools.partial(pack_kernel, jobs),
            in_specs=[smem] + [anywhere] * 5,
            out_specs=[anywhere] * len(jobs),
            out_shape=[jax.ShapeDtypeStruct(size, jnp.bfloat16) for size in sizes],
            scratch_shapes=[pltpu.VMEM(size, jnp.bfloat16) for size in sizes]
            + [pltpu.SemaphoreType.DMA((len(jobs), 4))] * 2,
            compiler_params=big,
        )(info, after, *originals)
        return sent, [swap(one, job[0]) for one, job in zip(sent, jobs)]

    sent, come_early = send_inputs([(2, 0, cut)], owner)

    cq, sq, ck, sk = tables(tokens_of(held), total)
    own_phase = (held[:, None] * BLOCK + dilation_phase[None, :]).astype(jnp.int32)
    pick_cos, pick_sin = flat_tables(own_phase, total)
    own_far = pl.pallas_call(
        functools.partial(pick_kernel, heads, blocks),
        in_specs=[smem, anywhere, anywhere, vmem, vmem, anywhere],
        out_specs=anywhere,
        out_shape=jax.ShapeDtypeStruct((devices // 2, 2 * blocks, width), jnp.bfloat16),
        scratch_shapes=[
            pltpu.VMEM((rows, width), jnp.bfloat16),
            pltpu.VMEM((rows, width), jnp.bfloat16),
            pltpu.VMEM((2 * blocks, width), jnp.bfloat16),
            pltpu.SemaphoreType.DMA((2,)),
            pltpu.SemaphoreType.DMA((devices // 2,)),
        ],
        compiler_params=big,
    )(
        dilation_phase,
        keys,
        values,
        pick_cos,
        pick_sin,
        sent[0],
    )
    halves = [list(range(0, devices, 2)), list(range(1, devices, 2))]
    near_far = lax.all_to_all(
        own_far,
        ("ctx", "bal"),
        split_axis=0,
        concat_axis=0,
        tiled=True,
        axis_index_groups=halves,
    ).reshape(count, width)
    other_far = swap(near_far, 1)
    jobs = [(2, cut, edge - cut), (3, 0, edge), (1, 0, edge)]
    _, (come_rest, come_3, come_1) = send_inputs(jobs, own_far)
    come_2 = come_early[0]

    ids = (device ^ steps) * blocks
    came = jnp.sum(
        jnp.where(comes_from[None, :] // blocks * blocks == ids[:, None], comes_from[None, :], 0),
        axis=1,
    )
    moved = jnp.concatenate([which, came, partner]).astype(jnp.int32)
    moved_tables = tables(tokens_of(came), total)

    side = 2 * count
    wide = jnp.arange(side, dtype=jnp.int32)
    tall = wide[:, None]
    wide = wide[None, :]
    source = tall % count
    holder = source // blocks
    held_row = (holder ^ device) % 2 * count + holder // 2 * (2 * blocks)
    pull = (wide == held_row + tall // count * blocks + source % blocks).astype(jnp.bfloat16)
    lands = owner // blocks
    lands = (lands ^ device) % 2 * count + lands // 2 * (2 * blocks) + owner % blocks
    push = (jnp.concatenate([lands, lands + blocks])[None, :] == tall).astype(jnp.bfloat16)

    per_step = 2
    columns = per_step * HEAD
    fixed = lambda h, *_: (0, 0)
    square = pl.BlockSpec((side, side), fixed)
    table = pl.BlockSpec((rows, HEAD), fixed)
    part = pl.BlockSpec((4, BLOCK, columns), lambda h, *_: (0, 0, h))
    def attend_held(begin, end, waits, carried):
        skip = begin // per_step
        tensor = pl.BlockSpec((rows, columns), lambda h, *_: (0, h + skip))
        far = pl.BlockSpec((count, columns), lambda h, *_: (0, h + skip))
        extra = carried + waits
        results = pl.pallas_call(
            functools.partial(attend_kernel, per_step, blocks, count, begin, 0, len(extra)),
            grid_spec=pltpu.PrefetchScalarGridSpec(
                num_scalar_prefetch=3,
                grid=((end - begin) // per_step,),
                in_specs=[far, far, square, square]
                + [table] * 4
                + [tensor] * 4
                + [anywhere] * len(extra),
                out_specs=[part] * blocks + [far] * 2,
            ),
            out_shape=[jax.ShapeDtypeStruct((4, BLOCK, (end - begin) * HEAD), jnp.bfloat16)]
            * blocks
            + [jax.ShapeDtypeStruct((count, width), jnp.bfloat16)] * 2,
            input_output_aliases={15 + i: blocks + i for i in range(len(carried))},
            compiler_params=big,
            cost_estimate=heavy,
        )(
            info,
            dilation_phase,
            segment_device_count,
            near_far,
            other_far,
            pull,
            push,
            cq,
            sq,
            ck,
            sk,
            *originals,
            *extra,
        )
        return list(results[:blocks]), list(results[blocks:])

    waits = list(moved_tables) + [come_1, come_2]
    parts, payload = attend_held(first, middle, waits, [])
    parts_last, payload = attend_held(middle, heads, [], payload)
    for k in range(1, blocks):
        parts[k] = swap(parts[k], k)
        parts_last[k] = swap(parts_last[k], k)

    shapes = [jax.ShapeDtypeStruct((blocks, BLOCK, width), jnp.bfloat16)] * 4
    shapes = shapes + [jax.ShapeDtypeStruct((count, width), jnp.bfloat16)] * 2

    def attend_relaid(begin, end, come, carried):
        skip = begin // per_step
        tensor = pl.BlockSpec((BLOCK, columns), lambda h, info, *_: (info[0], h + skip))
        far = pl.BlockSpec((count, columns), lambda h, *_: (0, h + skip))
        whole = pl.BlockSpec((blocks, BLOCK, columns), lambda h, *_: (0, 0, h + skip))
        shifted = pl.BlockSpec((4, BLOCK, columns), lambda h, *_: (0, 0, h + skip))
        operands = 3 + 4 + 4 + 4 + blocks - 1
        return pl.pallas_call(
            functools.partial(attend_kernel, per_step, blocks, count, begin, len(carried), 0),
            grid_spec=pltpu.PrefetchScalarGridSpec(
                num_scalar_prefetch=3,
                grid=((end - begin) // per_step,),
                in_specs=[far, far, square, square]
                + [table] * 4
                + [tensor] * 4
                + [shifted, part, shifted]
                + [anywhere] * len(carried),
                out_specs=[whole] * 4 + [far] * 2,
                ),
            out_shape=shapes,
            input_output_aliases={
                operands + i: 6 - len(carried) + i for i in range(len(carried))
            },
            compiler_params=big,
            cost_estimate=light,
        )(
            moved,
            dilation_phase,
            segment_device_count,
            near_far,
            other_far,
            pull,
            push,
            *moved_tables,
            *originals,
            *come,
            *carried,
        )

    results = attend_relaid(0, early, [come_1, come_2, come_3], payload)
    results = attend_relaid(early, first, [come_1, come_rest, come_3], results)
    finals = [one.reshape(rows, width) for one in results[:4]]
    payload = results[4].astype(jnp.float32) + swap(results[5], 1).astype(jnp.float32)
    payload = payload.astype(jnp.bfloat16)
    payload = pl.pallas_call(
        link_kernel,
        in_specs=[anywhere] * 3,
        out_specs=anywhere,
        out_shape=jax.ShapeDtypeStruct((count, width), jnp.bfloat16),
        input_output_aliases={0: 0},
        compiler_params=pltpu.CompilerParams(
            vmem_limit_bytes=room, has_side_effects=True
        ),
    )(payload, parts[2], parts[3])
    got = lax.all_to_all(
        payload.reshape(devices // 2, 2 * blocks, width),
        ("ctx", "bal"),
        split_axis=0,
        concat_axis=0,
        tiled=True,
        axis_index_groups=halves,
    )

    new_phase = (comes_from[:, None] * BLOCK + dilation_phase[None, :]).astype(jnp.int32)
    new_cos, new_sin = flat_tables(new_phase, total)
    out = jax.ShapeDtypeStruct((rows, width), jnp.bfloat16)
    slots = partner.astype(jnp.int32)
    items = [(k, edge, brim - edge) for k in range(blocks)]
    items += [(k, brim, width - brim) for k in range(2)]
    number = len(items)
    finals = pl.pallas_call(
        functools.partial(place_kernel, items),
        in_specs=[smem] + [anywhere] * (number + 4),
        out_specs=[anywhere] * 4,
        out_shape=[out] * 4,
        input_output_aliases={1 + number + t: t for t in range(4)},
        scratch_shapes=[pltpu.VMEM((4, BLOCK, item[2]), jnp.bfloat16) for item in items]
        + [pltpu.SemaphoreType.DMA((number,)), pltpu.SemaphoreType.DMA((number, 4))],
        compiler_params=big,
        cost_estimate=light,
    )(slots, *parts, *parts_last[:2], *finals)
    late = (2, 3)
    patched = pl.pallas_call(
        functools.partial(patch_kernel, heads, blocks, late, brim),
        in_specs=[smem, smem, anywhere, vmem, vmem, anywhere, anywhere],
        out_specs=[anywhere] * 2,
        out_shape=[out] * 2,
        input_output_aliases={5: 0, 6: 1},
        scratch_shapes=[
            pltpu.VMEM((devices // 2, 2 * blocks, width), jnp.bfloat16),
            pltpu.VMEM((2, blocks, BLOCK, width), jnp.bfloat16),
            pltpu.SemaphoreType.DMA(()),
            pltpu.SemaphoreType.DMA((2, blocks)),
            pltpu.SemaphoreType.DMA((2, blocks)),
        ],
        compiler_params=big,
        cost_estimate=light,
    )(dilation_phase, slots, got, new_cos, new_sin, finals[2], finals[3])
    return tuple(
        pl.pallas_call(
            functools.partial(last_kernel, heads, blocks, late, brim),
            in_specs=[smem, smem, anywhere, vmem, vmem] + [anywhere] * 6,
            out_specs=[anywhere] * 4,
            out_shape=[out] * 4,
            input_output_aliases={7 + t: t for t in range(4)},
            scratch_shapes=[
                pltpu.VMEM((devices // 2, 2 * blocks, width - brim), jnp.bfloat16),
                pltpu.VMEM((2, 4, BLOCK, width - brim), jnp.bfloat16),
                pltpu.SemaphoreType.DMA(()),
                pltpu.SemaphoreType.DMA((2,)),
                pltpu.SemaphoreType.DMA((2, 4)),
            ],
            compiler_params=big,
        )(
            dilation_phase,
            slots,
            got,
            new_cos[:, brim:],
            new_sin[:, brim:],
            *parts_last[2:],
            finals[0],
            finals[1],
            *patched,
        )
    )


def solution(mesh):
    token = P(("groups", "ctx", "bal"), "head")
    return jax.shard_map(
        local,
        mesh=mesh,
        in_specs=(token, token, token, token, P("head"), P("head"), P("groups")),
        out_specs=(token, token, token, token),
        check_vma=False,
    )
```

```python
import functools
import math

import jax
import jax.numpy as jnp
from jax import lax
from jax.experimental import pallas as pl
from jax.experimental.pallas import tpu as pltpu
from jax.sharding import PartitionSpec as P

BLOCK = 128
HEAD = 128
LOG2E = 1.4426950408889634
NT = (((1,), (1,)), ((), ()))
TN = (((0,), (0,)), ((), ()))


def tables(positions, total):
    half = HEAD // 2
    pair = jnp.arange(half, dtype=jnp.float32)
    inverse = jnp.exp(pair * (-2.0 * math.log(10000.0) / HEAD))
    where = positions.astype(jnp.float32)[..., None]
    angles = where * inverse
    base = (2.0 * pair / HEAD + 0.4) / 1.4
    growth = jnp.exp((2.0 * where - total) / total * jnp.log(base))
    cosine, sine = jnp.cos(angles), jnp.sin(angles)

    def pack(scale):
        first, second = cosine * scale, sine * scale
        return (
            jnp.concatenate([first, first], axis=-1),
            jnp.concatenate([-second, second], axis=-1),
        )

    return pack(growth) + pack(1.0 / growth)


def flat_tables(positions, total):
    half = HEAD // 2
    lane = jnp.arange(positions.shape[1] * HEAD, dtype=jnp.int32) % HEAD
    pair = (lane % half).astype(jnp.float32)
    inverse = jnp.exp(pair * (-2.0 * math.log(10000.0) / HEAD))
    where = jnp.repeat(positions.astype(jnp.float32), HEAD, axis=1)
    angles = where * inverse[None, :]
    base = (2.0 * pair / HEAD + 0.4) / 1.4
    growth = jnp.exp((2.0 * where - total) / total * jnp.log(base)[None, :])
    sine = jnp.where(lane[None, :] < half, -jnp.sin(angles), jnp.sin(angles))
    return jnp.cos(angles) / growth, sine / growth


def dot(left, right, dims=None):
    if dims is None:
        dims = (((1,), (0,)), ((), ()))
    return lax.dot_general(left, right, dims, preferred_element_type=jnp.float32)


def attend_kernel(
    per_step, blocks, count, first, relaid, waits, info, phase, seg, far_ref, other_ref, pull_ref, push_ref, *rest
):
    cq_ref, sq_ref, ck_ref, sk_ref = rest[:4]
    own = rest[4:8]
    rest = rest[8:]
    if relaid:
        come, rest = rest[: blocks - 1], rest[blocks - 1 + relaid :]
        finals, rest = rest[:4], rest[4:]
    else:
        finals, rest = rest[waits : waits + blocks], rest[waits + blocks :]
    own_pay, other_pay = rest
    scale = 1.0 / math.sqrt(HEAD)
    key_at = lax.broadcasted_iota(jnp.int32, (BLOCK, BLOCK), 0)
    query_at = lax.broadcasted_iota(jnp.int32, (BLOCK, BLOCK), 1)
    far_at = lax.broadcasted_iota(jnp.int32, (count, BLOCK), 0)
    far_query = lax.broadcasted_iota(jnp.int32, (count, BLOCK), 1)
    half = HEAD // 2
    for sub in range(per_step):
        head = first + pl.program_id(0) * per_step + sub
        lanes = slice(sub * HEAD, (sub + 1) * HEAD)
        held = jnp.concatenate([far_ref[:, lanes], other_ref[:, lanes]], axis=0)
        both = dot(pull_ref[...], held).astype(jnp.bfloat16)
        far_k, far_v = both[:count], both[count:]
        span = seg[head] * blocks
        at = phase[head]
        causal = (key_at <= query_at) & (key_at != at)
        behind = far_at * BLOCK + at - far_query
        p_far, d_far, q_all, g_all = [], [], [], []
        for k in range(blocks):
            if relaid:
                rows = slice(k * BLOCK, (k + 1) * BLOCK)
                source = [ref[:, lanes] for ref in own]
                if k:
                    source = [come[k - 1][t, :, lanes] for t in range(4)]
            else:
                rows = pl.ds(pl.multiple_of(info[k] * BLOCK, BLOCK), BLOCK)
                source = [ref[rows, lanes] for ref in own]
            block = info[blocks + k]
            low = block & (-span)
            cq, sq, ck, sk = cq_ref[rows, :], sq_ref[rows, :], ck_ref[rows, :], sk_ref[rows, :]
            raw_q, raw_k, value, grad = source
            raw_q = raw_q.astype(jnp.float32)
            raw_k = raw_k.astype(jnp.float32)
            tq = (raw_q * cq + pltpu.roll(raw_q, half, 1) * sq).astype(jnp.bfloat16)
            tk = (raw_k * ck + pltpu.roll(raw_k, half, 1) * sk).astype(jnp.bfloat16)
            keys = jnp.concatenate([tk, far_k], axis=0)
            vals = jnp.concatenate([value, far_v], axis=0)
            score = dot(keys, tq, NT)
            allowed = (far_at >= low) & (behind <= block * BLOCK)
            score = jnp.concatenate(
                [
                    jnp.where(causal, score[:BLOCK], -jnp.inf),
                    jnp.where(allowed, score[BLOCK:], -jnp.inf),
                ],
                axis=0,
            )
            top = jnp.max(score, axis=0, keepdims=True)
            weight = jnp.exp2((score - top) * (scale * LOG2E))
            prob = weight * (1.0 / jnp.sum(weight, axis=0, keepdims=True))
            p16 = prob.astype(jnp.bfloat16)
            dprob = dot(vals, grad, NT)
            delta = jnp.sum(p16.astype(jnp.float32) * dprob, axis=0, keepdims=True)
            d16 = (prob * (dprob - delta)).astype(jnp.bfloat16)
            out = dot(p16, vals, TN)
            dq = dot(d16, keys, TN) * scale
            dk = dot(d16[:BLOCK], tq) * scale
            dv = dot(p16[:BLOCK], grad)
            made = (
                out,
                dq * cq - pltpu.roll(dq, half, 1) * sq,
                dk * ck - pltpu.roll(dk, half, 1) * sk,
                dv,
            )
            for t in range(4):
                if relaid:
                    finals[t][info[2 * blocks + k], :, lanes] = made[t].astype(jnp.bfloat16)
                else:
                    finals[k][t, :, lanes] = made[t].astype(jnp.bfloat16)
            p_far.append(p16[BLOCK:])
            d_far.append(d16[BLOCK:])
            q_all.append(tq)
            g_all.append(grad)
        far_dk = dot(jnp.concatenate(d_far, axis=1), jnp.concatenate(q_all, axis=0)) * scale
        far_dv = dot(jnp.concatenate(p_far, axis=1), jnp.concatenate(g_all, axis=0))
        far_sum = jnp.concatenate([far_dk, far_dv], axis=0).astype(jnp.bfloat16)
        pay = dot(push_ref[...], far_sum).astype(jnp.bfloat16)
        own_pay[:, lanes] = pay[:count]
        other_pay[:, lanes] = pay[count:]


def pick_kernel(
    heads, blocks, phase, k_hbm, v_hbm, cos_ref, sin_ref, after, out_ref, k_ref, v_ref, row_ref,
    load, save
):
    moves = [
        pltpu.make_async_copy(k_hbm, k_ref, load.at[0]),
        pltpu.make_async_copy(v_hbm, v_ref, load.at[1]),
    ]
    for move in moves:
        move.start()
    for move in moves:
        move.wait()
    spot = lax.broadcasted_iota(jnp.int32, (16, HEAD), 0)
    for head in range(heads):
        at = phase[head]
        start = pl.multiple_of(at // 16 * 16, 16)
        lanes = slice(head * HEAD, (head + 1) * HEAD)
        both = []
        for ref in (k_ref, v_ref):
            rows = []
            for k in range(blocks):
                tile = ref[pl.ds(pl.multiple_of(k * BLOCK + start, 16), 16), lanes]
                tile = jnp.where(spot == at - start, tile.astype(jnp.float32), 0.0)
                rows.append(jnp.sum(tile, axis=0, keepdims=True))
            both.append(jnp.concatenate(rows, axis=0))
        key, value = both
        key = key * cos_ref[:, lanes] + pltpu.roll(key, HEAD // 2, 1) * sin_ref[:, lanes]
        row_ref[:, lanes] = jnp.concatenate([key, value], axis=0).astype(jnp.bfloat16)
    copies = [
        pltpu.make_async_copy(row_ref, out_ref.at[d], save.at[d]) for d in range(out_ref.shape[0])
    ]
    for copy in copies:
        copy.start()
    for copy in copies:
        copy.wait()


def pack_kernel(jobs, info, after, *rest):
    number = len(jobs)
    inputs, rest = rest[:4], rest[4:]
    outs, rooms, (load, save) = rest[:number], rest[number : 2 * number], rest[2 * number :]
    order = [(job, t) for job in range(number) for t in range(4)]

    def fetch(job, t):
        k, start, width = jobs[job]
        rows = pl.ds(pl.multiple_of(info[k] * BLOCK, BLOCK), BLOCK)
        source = inputs[t].at[rows, pl.ds(start, width)]
        return pltpu.make_async_copy(source, rooms[job].at[t], load.at[job, t])

    def store(job, t):
        return pltpu.make_async_copy(rooms[job].at[t], outs[job].at[t], save.at[job, t])

    for job, t in order:
        fetch(job, t).start()
    for job, t in order:
        fetch(job, t).wait()
        store(job, t).start()
    for job, t in order:
        store(job, t).wait()


def link_kernel(*refs):
    pass


def place_kernel(items, slot, *rest):
    number = len(items)
    parts = rest[:number]
    finals = rest[number + 4 : number + 8]
    rooms, (load, save) = rest[number + 8 : 2 * number + 8], rest[2 * number + 8 :]

    def save_of(i, t):
        k, start, width = items[i]
        top = pl.multiple_of(slot[k] * BLOCK, BLOCK)
        where = finals[t].at[pl.ds(top, BLOCK), pl.ds(start, width)]
        return pltpu.make_async_copy(rooms[i].at[t], where, save.at[i, t])

    loads = [pltpu.make_async_copy(parts[i], rooms[i], load.at[i]) for i in range(number)]
    for move in loads:
        move.start()
    for i in range(number):
        loads[i].wait()
        for t in range(4):
            save_of(i, t).start()
    for i in range(number):
        for t in range(4):
            save_of(i, t).wait()


def far_rows(got, cos_ref, sin_ref, blocks):
    total = got[0].astype(jnp.float32)
    for sender in range(1, got.shape[0]):
        total = total + got[sender].astype(jnp.float32)
    far_k, far_v = total[:blocks], total[blocks:]
    heads = far_k.shape[1] // HEAD
    turned = []
    for head in range(heads):
        lanes = slice(head * HEAD, (head + 1) * HEAD)
        one = far_k[:, lanes]
        turned.append(
            one * cos_ref[:, lanes] - pltpu.roll(one, HEAD // 2, 1) * sin_ref[:, lanes]
        )
    values = [far_v[:, head * HEAD : (head + 1) * HEAD] for head in range(heads)]
    return turned, values


def overwrite(ref, lanes, at, source, pick):
    spot = lax.broadcasted_iota(jnp.int32, (16, HEAD), 0)
    line = lax.broadcasted_iota(jnp.int32, source.shape, 0)
    start = pl.multiple_of(at // 16 * 16, 16)
    row = jnp.sum(jnp.where(line == pick, source, 0.0), axis=0, keepdims=True)
    old = ref[pl.ds(start, 16), lanes].astype(jnp.float32)
    ref[pl.ds(start, 16), lanes] = jnp.where(spot == at - start, row, old).astype(jnp.bfloat16)


def patch_kernel(
    heads, blocks, late, edge, phase, slot, got_hbm, cos_ref, sin_ref, dk_in, dv_in, dk, dv, got,
    room, get, load, save
):
    outs = (dk, dv)
    width = room.shape[-1]
    order = [(k, t) for k in range(blocks) for t in range(2)]

    def span(k):
        return pl.ds(0, edge if k in late else width)

    def here(t, k):
        rows = pl.ds(pl.multiple_of(slot[k] * BLOCK, BLOCK), BLOCK)
        return outs[t].at[rows, span(k)]

    def fetch(t, k):
        return pltpu.make_async_copy(here(t, k), room.at[t, k, :, span(k)], load.at[t, k])

    def store(t, k):
        return pltpu.make_async_copy(room.at[t, k, :, span(k)], here(t, k), save.at[t, k])

    first = pltpu.make_async_copy(got_hbm, got, get)
    first.start()
    for k, t in order:
        fetch(t, k).start()
    first.wait()
    fresh = far_rows(got, cos_ref, sin_ref, blocks)
    for k, t in order:
        fetch(t, k).wait()
        for head in range(edge // HEAD if k in late else heads):
            lanes = slice(head * HEAD, (head + 1) * HEAD)
            overwrite(room.at[t, k], lanes, phase[head], fresh[t][head], slot[k])
        store(t, k).start()
    for k, t in order:
        store(t, k).wait()


def last_kernel(heads, blocks, late, edge, phase, slot, got_hbm, cos_ref, sin_ref, *rest):
    number = len(late)
    parts = rest[:number]
    outs = rest[number + 4 : number + 8]
    got, room, get, load, save = rest[number + 8 :]
    right = pl.ds(edge, room.shape[-1])

    def store(i, t):
        rows = pl.ds(pl.multiple_of(slot[late[i]] * BLOCK, BLOCK), BLOCK)
        return pltpu.make_async_copy(room.at[i, t], outs[t].at[rows, right], save.at[i, t])

    first = pltpu.make_async_copy(got_hbm.at[:, :, right], got, get)
    loads = [pltpu.make_async_copy(parts[i], room.at[i], load.at[i]) for i in range(number)]
    for move in loads + [first]:
        move.start()
    for i in range(number):
        loads[i].wait()
        for t in range(2):
            store(i, t).start()
    first.wait()
    fresh = far_rows(got, cos_ref, sin_ref, blocks)
    for i in range(number):
        for t in range(2):
            for head in range(edge // HEAD, heads):
                local_head = head - edge // HEAD
                lanes = slice(local_head * HEAD, (local_head + 1) * HEAD)
                source = fresh[t][local_head]
                overwrite(room.at[i, 2 + t], lanes, phase[head], source, slot[late[i]])
            store(i, 2 + t).start()
    for i in range(number):
        for t in range(4):
            store(i, t).wait()


def local(queries, keys, values, output_gradient, dilation_phase, segment_device_count, owner):
    rows, width = queries.shape
    heads = width // HEAD
    blocks = rows // BLOCK
    bal_size = lax.axis_size("bal")
    devices = lax.axis_size("ctx") * bal_size
    total = rows * devices
    count = owner.shape[0]
    assert blocks == bal_size == 4 and bal_size & (bal_size - 1) == 0
    bal = lax.axis_index("bal")
    device = lax.axis_index("ctx") * bal_size + bal
    room = 66_000_000
    big = pltpu.CompilerParams(vmem_limit_bytes=room)
    smem = pl.BlockSpec(memory_space=pltpu.SMEM)
    vmem = pl.BlockSpec(memory_space=pltpu.VMEM)
    anywhere = pl.BlockSpec(memory_space=pl.ANY)
    light = pl.CostEstimate(flops=2_000_000_000, bytes_accessed=5_000_000, transcendentals=0)
    heavy = pl.CostEstimate(flops=20_000_000_000, bytes_accessed=60_000_000, transcendentals=0)

    def tokens_of(ids):
        return (ids[:, None] * BLOCK + jnp.arange(BLOCK, dtype=jnp.int32)[None, :]).reshape(rows)

    def swap(array, k):
        return lax.ppermute(array, "bal", [(i, i ^ k) for i in range(bal_size)])

    steps = jnp.arange(blocks, dtype=jnp.int32)
    held = device * blocks + steps
    goes_to = lax.dynamic_slice_in_dim(owner, device * blocks, blocks) // blocks % bal_size
    partner = steps ^ bal
    which = jnp.sum(jnp.where(goes_to[None, :] == partner[:, None], steps[None, :], 0), axis=1)
    info = jnp.concatenate([which, device * blocks + which]).astype(jnp.int32)
    comes_from = jnp.sum(
        jnp.where(
            owner[None, :] == held[:, None], jnp.arange(count, dtype=jnp.int32)[None, :], 0
        ),
        axis=1,
    )

    first = heads * 3 // 10 * 2
    early = first // 4 * 2
    middle = heads - 2
    cut, edge, brim = early * HEAD, first * HEAD, middle * HEAD
    originals = (queries, keys, values, output_gradient)

    def send_inputs(jobs, after):
        sizes = [(4, BLOCK, width) for _, _, width in jobs]
        sent = pl.pallas_call(
            functools.partial(pack_kernel, jobs),
            in_specs=[smem] + [anywhere] * 5,
            out_specs=[anywhere] * len(jobs),
            out_shape=[jax.ShapeDtypeStruct(size, jnp.bfloat16) for size in sizes],
            scratch_shapes=[pltpu.VMEM(size, jnp.bfloat16) for size in sizes]
            + [pltpu.SemaphoreType.DMA((len(jobs), 4))] * 2,
            compiler_params=big,
        )(info, after, *originals)
        return sent, [swap(one, job[0]) for one, job in zip(sent, jobs)]

    sent, come_early = send_inputs([(2, 0, cut)], owner)

    cq, sq, ck, sk = tables(tokens_of(held), total)
    own_phase = (held[:, None] * BLOCK + dilation_phase[None, :]).astype(jnp.int32)
    pick_cos, pick_sin = flat_tables(own_phase, total)
    own_far = pl.pallas_call(
        functools.partial(pick_kernel, heads, blocks),
        in_specs=[smem, anywhere, anywhere, vmem, vmem, anywhere],
        out_specs=anywhere,
        out_shape=jax.ShapeDtypeStruct((devices // 2, 2 * blocks, width), jnp.bfloat16),
        scratch_shapes=[
            pltpu.VMEM((rows, width), jnp.bfloat16),
            pltpu.VMEM((rows, width), jnp.bfloat16),
            pltpu.VMEM((2 * blocks, width), jnp.bfloat16),
            pltpu.SemaphoreType.DMA((2,)),
            pltpu.SemaphoreType.DMA((devices // 2,)),
        ],
        compiler_params=big,
    )(
        dilation_phase,
        keys,
        values,
        pick_cos,
        pick_sin,
        sent[0],
    )
    halves = [list(range(0, devices, 2)), list(range(1, devices, 2))]
    near_far = lax.all_to_all(
        own_far,
        ("ctx", "bal"),
        split_axis=0,
        concat_axis=0,
        tiled=True,
        axis_index_groups=halves,
    ).reshape(count, width)
    other_far = swap(near_far, 1)
    jobs = [(2, cut, edge - cut), (3, 0, edge), (1, 0, edge)]
    _, (come_rest, come_3, come_1) = send_inputs(jobs, own_far)
    come_2 = come_early[0]

    ids = (device ^ steps) * blocks
    came = jnp.sum(
        jnp.where(comes_from[None, :] // blocks * blocks == ids[:, None], comes_from[None, :], 0),
        axis=1,
    )
    moved = jnp.concatenate([which, came, partner]).astype(jnp.int32)
    moved_tables = tables(tokens_of(came), total)

    side = 2 * count
    wide = jnp.arange(side, dtype=jnp.int32)
    tall = wide[:, None]
    wide = wide[None, :]
    source = tall % count
    holder = source // blocks
    held_row = (holder ^ device) % 2 * count + holder // 2 * (2 * blocks)
    pull = (wide == held_row + tall // count * blocks + source % blocks).astype(jnp.bfloat16)
    lands = owner // blocks
    lands = (lands ^ device) % 2 * count + lands // 2 * (2 * blocks) + owner % blocks
    push = (jnp.concatenate([lands, lands + blocks])[None, :] == tall).astype(jnp.bfloat16)

    per_step = 2
    columns = per_step * HEAD
    fixed = lambda h, *_: (0, 0)
    square = pl.BlockSpec((side, side), fixed)
    table = pl.BlockSpec((rows, HEAD), fixed)
    part = pl.BlockSpec((4, BLOCK, columns), lambda h, *_: (0, 0, h))
    def attend_held(begin, end, waits, carried):
        skip = begin // per_step
        tensor = pl.BlockSpec((rows, columns), lambda h, *_: (0, h + skip))
        far = pl.BlockSpec((count, columns), lambda h, *_: (0, h + skip))
        extra = carried + waits
        results = pl.pallas_call(
            functools.partial(attend_kernel, per_step, blocks, count, begin, 0, len(extra)),
            grid_spec=pltpu.PrefetchScalarGridSpec(
                num_scalar_prefetch=3,
                grid=((end - begin) // per_step,),
                in_specs=[far, far, square, square]
                + [table] * 4
                + [tensor] * 4
                + [anywhere] * len(extra),
                out_specs=[part] * blocks + [far] * 2,
            ),
            out_shape=[jax.ShapeDtypeStruct((4, BLOCK, (end - begin) * HEAD), jnp.bfloat16)]
            * blocks
            + [jax.ShapeDtypeStruct((count, width), jnp.bfloat16)] * 2,
            input_output_aliases={15 + i: blocks + i for i in range(len(carried))},
            compiler_params=big,
            cost_estimate=heavy,
        )(
            info,
            dilation_phase,
            segment_device_count,
            near_far,
            other_far,
            pull,
            push,
            cq,
            sq,
            ck,
            sk,
            *originals,
            *extra,
        )
        return list(results[:blocks]), list(results[blocks:])

    waits = list(moved_tables) + [come_1, come_2]
    parts, payload = attend_held(first, middle, waits, [])
    parts_last, payload = attend_held(middle, heads, [], payload)
    for k in range(1, blocks):
        parts[k] = swap(parts[k], k)
        parts_last[k] = swap(parts_last[k], k)

    shapes = [jax.ShapeDtypeStruct((blocks, BLOCK, width), jnp.bfloat16)] * 4
    shapes = shapes + [jax.ShapeDtypeStruct((count, width), jnp.bfloat16)] * 2

    def attend_relaid(begin, end, come, carried):
        skip = begin // per_step
        tensor = pl.BlockSpec((BLOCK, columns), lambda h, info, *_: (info[0], h + skip))
        far = pl.BlockSpec((count, columns), lambda h, *_: (0, h + skip))
        whole = pl.BlockSpec((blocks, BLOCK, columns), lambda h, *_: (0, 0, h + skip))
        shifted = pl.BlockSpec((4, BLOCK, columns), lambda h, *_: (0, 0, h + skip))
        operands = 3 + 4 + 4 + 4 + blocks - 1
        return pl.pallas_call(
            functools.partial(attend_kernel, per_step, blocks, count, begin, len(carried), 0),
            grid_spec=pltpu.PrefetchScalarGridSpec(
                num_scalar_prefetch=3,
                grid=((end - begin) // per_step,),
                in_specs=[far, far, square, square]
                + [table] * 4
                + [tensor] * 4
                + [shifted, part, shifted]
                + [anywhere] * len(carried),
                out_specs=[whole] * 4 + [far] * 2,
                ),
            out_shape=shapes,
            input_output_aliases={
                operands + i: 6 - len(carried) + i for i in range(len(carried))
            },
            compiler_params=big,
            cost_estimate=light,
        )(
            moved,
            dilation_phase,
            segment_device_count,
            near_far,
            other_far,
            pull,
            push,
            *moved_tables,
            *originals,
            *come,
            *carried,
        )

    results = attend_relaid(0, early, [come_1, come_2, come_3], payload)
    results = attend_relaid(early, first, [come_1, come_rest, come_3], results)
    finals = [one.reshape(rows, width) for one in results[:4]]

    def after(array, wait):
        return pl.pallas_call(
            link_kernel,
            in_specs=[anywhere] * 2,
            out_specs=anywhere,
            out_shape=jax.ShapeDtypeStruct(array.shape, array.dtype),
            input_output_aliases={0: 0},
            compiler_params=pltpu.CompilerParams(vmem_limit_bytes=room, has_side_effects=True),
        )(array, wait)

    crossing = swap(after(results[5], parts[2]), 1)
    payload = results[4].astype(jnp.float32) + crossing.astype(jnp.float32)
    payload = after(payload.astype(jnp.bfloat16), parts[3])
    got = lax.all_to_all(
        payload.reshape(devices // 2, 2 * blocks, width),
        ("ctx", "bal"),
        split_axis=0,
        concat_axis=0,
        tiled=True,
        axis_index_groups=halves,
    )

    new_phase = (comes_from[:, None] * BLOCK + dilation_phase[None, :]).astype(jnp.int32)
    new_cos, new_sin = flat_tables(new_phase, total)
    out = jax.ShapeDtypeStruct((rows, width), jnp.bfloat16)
    slots = partner.astype(jnp.int32)
    items = [(k, edge, brim - edge) for k in range(blocks)]
    items += [(k, brim, width - brim) for k in range(2)]
    number = len(items)
    finals = pl.pallas_call(
        functools.partial(place_kernel, items),
        in_specs=[smem] + [anywhere] * (number + 4),
        out_specs=[anywhere] * 4,
        out_shape=[out] * 4,
        input_output_aliases={1 + number + t: t for t in range(4)},
        scratch_shapes=[pltpu.VMEM((4, BLOCK, item[2]), jnp.bfloat16) for item in items]
        + [pltpu.SemaphoreType.DMA((number,)), pltpu.SemaphoreType.DMA((number, 4))],
        compiler_params=big,
        cost_estimate=light,
    )(slots, *parts, *parts_last[:2], *finals)
    late = (2, 3)
    patched = pl.pallas_call(
        functools.partial(patch_kernel, heads, blocks, late, brim),
        in_specs=[smem, smem, anywhere, vmem, vmem, anywhere, anywhere],
        out_specs=[anywhere] * 2,
        out_shape=[out] * 2,
        input_output_aliases={5: 0, 6: 1},
        scratch_shapes=[
            pltpu.VMEM((devices // 2, 2 * blocks, width), jnp.bfloat16),
            pltpu.VMEM((2, blocks, BLOCK, width), jnp.bfloat16),
            pltpu.SemaphoreType.DMA(()),
            pltpu.SemaphoreType.DMA((2, blocks)),
            pltpu.SemaphoreType.DMA((2, blocks)),
        ],
        compiler_params=big,
        cost_estimate=light,
    )(dilation_phase, slots, got, new_cos, new_sin, finals[2], finals[3])
    return tuple(
        pl.pallas_call(
            functools.partial(last_kernel, heads, blocks, late, brim),
            in_specs=[smem, smem, anywhere, vmem, vmem] + [anywhere] * 6,
            out_specs=[anywhere] * 4,
            out_shape=[out] * 4,
            input_output_aliases={7 + t: t for t in range(4)},
            scratch_shapes=[
                pltpu.VMEM((devices // 2, 2 * blocks, width - brim), jnp.bfloat16),
                pltpu.VMEM((2, 4, BLOCK, width - brim), jnp.bfloat16),
                pltpu.SemaphoreType.DMA(()),
                pltpu.SemaphoreType.DMA((2,)),
                pltpu.SemaphoreType.DMA((2, 4)),
            ],
            compiler_params=big,
        )(
            dilation_phase,
            slots,
            got,
            new_cos[:, brim:],
            new_sin[:, brim:],
            *parts_last[2:],
            finals[0],
            finals[1],
            *patched,
        )
    )


def solution(mesh):
    token = P(("groups", "ctx", "bal"), "head")
    return jax.shard_map(
        local,
        mesh=mesh,
        in_specs=(token, token, token, token, P("head"), P("head"), P("groups")),
        out_specs=(token, token, token, token),
        check_vma=False,
    )
```

```python
import functools
import math

import jax
import jax.numpy as jnp
from jax import lax
from jax.experimental import pallas as pl
from jax.experimental.pallas import tpu as pltpu
from jax.sharding import PartitionSpec as P

BLOCK = 128
HEAD = 128
LOG2E = 1.4426950408889634
NT = (((1,), (1,)), ((), ()))
TN = (((0,), (0,)), ((), ()))


def tables(positions, total):
    half = HEAD // 2
    pair = jnp.arange(half, dtype=jnp.float32)
    inverse = jnp.exp(pair * (-2.0 * math.log(10000.0) / HEAD))
    where = positions.astype(jnp.float32)[..., None]
    angles = where * inverse
    base = (2.0 * pair / HEAD + 0.4) / 1.4
    growth = jnp.exp((2.0 * where - total) / total * jnp.log(base))
    cosine, sine = jnp.cos(angles), jnp.sin(angles)

    def pack(scale):
        first, second = cosine * scale, sine * scale
        return (
            jnp.concatenate([first, first], axis=-1),
            jnp.concatenate([-second, second], axis=-1),
        )

    return pack(growth) + pack(1.0 / growth)


def flat_tables(positions, total):
    half = HEAD // 2
    lane = jnp.arange(positions.shape[1] * HEAD, dtype=jnp.int32) % HEAD
    pair = (lane % half).astype(jnp.float32)
    inverse = jnp.exp(pair * (-2.0 * math.log(10000.0) / HEAD))
    where = jnp.repeat(positions.astype(jnp.float32), HEAD, axis=1)
    angles = where * inverse[None, :]
    base = (2.0 * pair / HEAD + 0.4) / 1.4
    growth = jnp.exp((2.0 * where - total) / total * jnp.log(base)[None, :])
    sine = jnp.where(lane[None, :] < half, -jnp.sin(angles), jnp.sin(angles))
    return jnp.cos(angles) / growth, sine / growth


def dot(left, right, dims=None):
    if dims is None:
        dims = (((1,), (0,)), ((), ()))
    return lax.dot_general(left, right, dims, preferred_element_type=jnp.float32)


def attend_kernel(
    per_step, blocks, count, first, relaid, waits, info, phase, seg, far_ref, other_ref, pull_ref, push_ref, *rest
):
    cq_ref, sq_ref, ck_ref, sk_ref = rest[:4]
    own = rest[4:8]
    rest = rest[8:]
    if relaid:
        come, rest = rest[: blocks - 1], rest[blocks - 1 + relaid :]
        finals, rest = rest[:4], rest[4:]
    else:
        finals, rest = rest[waits : waits + blocks], rest[waits + blocks :]
    own_pay, other_pay = rest
    scale = 1.0 / math.sqrt(HEAD)
    key_at = lax.broadcasted_iota(jnp.int32, (BLOCK, BLOCK), 0)
    query_at = lax.broadcasted_iota(jnp.int32, (BLOCK, BLOCK), 1)
    far_at = lax.broadcasted_iota(jnp.int32, (count, BLOCK), 0)
    far_query = lax.broadcasted_iota(jnp.int32, (count, BLOCK), 1)
    half = HEAD // 2
    for sub in range(per_step):
        head = first + pl.program_id(0) * per_step + sub
        lanes = slice(sub * HEAD, (sub + 1) * HEAD)
        held = jnp.concatenate([far_ref[:, lanes], other_ref[:, lanes]], axis=0)
        both = dot(pull_ref[...], held).astype(jnp.bfloat16)
        far_k, far_v = both[:count], both[count:]
        span = seg[head] * blocks
        at = phase[head]
        causal = (key_at <= query_at) & (key_at != at)
        behind = far_at * BLOCK + at - far_query
        p_far, d_far, q_all, g_all = [], [], [], []
        for k in range(blocks):
            if relaid:
                rows = slice(k * BLOCK, (k + 1) * BLOCK)
                source = [ref[:, lanes] for ref in own]
                if k:
                    source = [come[k - 1][t, :, lanes] for t in range(4)]
            else:
                rows = pl.ds(pl.multiple_of(info[k] * BLOCK, BLOCK), BLOCK)
                source = [ref[rows, lanes] for ref in own]
            block = info[blocks + k]
            low = block & (-span)
            cq, sq, ck, sk = cq_ref[rows, :], sq_ref[rows, :], ck_ref[rows, :], sk_ref[rows, :]
            raw_q, raw_k, value, grad = source
            raw_q = raw_q.astype(jnp.float32)
            raw_k = raw_k.astype(jnp.float32)
            tq = (raw_q * cq + pltpu.roll(raw_q, half, 1) * sq).astype(jnp.bfloat16)
            tk = (raw_k * ck + pltpu.roll(raw_k, half, 1) * sk).astype(jnp.bfloat16)
            keys = jnp.concatenate([tk, far_k], axis=0)
            vals = jnp.concatenate([value, far_v], axis=0)
            score = dot(keys, tq, NT)
            allowed = (far_at >= low) & (behind <= block * BLOCK)
            score = jnp.concatenate(
                [
                    jnp.where(causal, score[:BLOCK], -jnp.inf),
                    jnp.where(allowed, score[BLOCK:], -jnp.inf),
                ],
                axis=0,
            )
            top = jnp.max(score, axis=0, keepdims=True)
            weight = jnp.exp2((score - top) * (scale * LOG2E))
            prob = weight * (1.0 / jnp.sum(weight, axis=0, keepdims=True))
            p16 = prob.astype(jnp.bfloat16)
            dprob = dot(vals, grad, NT)
            delta = jnp.sum(p16.astype(jnp.float32) * dprob, axis=0, keepdims=True)
            d16 = (prob * (dprob - delta)).astype(jnp.bfloat16)
            out = dot(p16, vals, TN)
            dq = dot(d16, keys, TN) * scale
            dk = dot(d16[:BLOCK], tq) * scale
            dv = dot(p16[:BLOCK], grad)
            made = (
                out,
                dq * cq - pltpu.roll(dq, half, 1) * sq,
                dk * ck - pltpu.roll(dk, half, 1) * sk,
                dv,
            )
            for t in range(4):
                if relaid:
                    finals[t][info[2 * blocks + k], :, lanes] = made[t].astype(jnp.bfloat16)
                else:
                    finals[k][t, :, lanes] = made[t].astype(jnp.bfloat16)
            p_far.append(p16[BLOCK:])
            d_far.append(d16[BLOCK:])
            q_all.append(tq)
            g_all.append(grad)
        far_dk = dot(jnp.concatenate(d_far, axis=1), jnp.concatenate(q_all, axis=0)) * scale
        far_dv = dot(jnp.concatenate(p_far, axis=1), jnp.concatenate(g_all, axis=0))
        far_sum = jnp.concatenate([far_dk, far_dv], axis=0).astype(jnp.bfloat16)
        pay = dot(push_ref[...], far_sum).astype(jnp.bfloat16)
        own_pay[:, lanes] = pay[:count]
        other_pay[:, lanes] = pay[count:]


def pick_kernel(
    heads, blocks, phase, k_hbm, v_hbm, cos_ref, sin_ref, after, out_ref, k_ref, v_ref, row_ref,
    load, save
):
    moves = [
        pltpu.make_async_copy(k_hbm, k_ref, load.at[0]),
        pltpu.make_async_copy(v_hbm, v_ref, load.at[1]),
    ]
    for move in moves:
        move.start()
    for move in moves:
        move.wait()
    spot = lax.broadcasted_iota(jnp.int32, (16, HEAD), 0)
    for head in range(heads):
        at = phase[head]
        start = pl.multiple_of(at // 16 * 16, 16)
        lanes = slice(head * HEAD, (head + 1) * HEAD)
        both = []
        for ref in (k_ref, v_ref):
            rows = []
            for k in range(blocks):
                tile = ref[pl.ds(pl.multiple_of(k * BLOCK + start, 16), 16), lanes]
                tile = jnp.where(spot == at - start, tile.astype(jnp.float32), 0.0)
                rows.append(jnp.sum(tile, axis=0, keepdims=True))
            both.append(jnp.concatenate(rows, axis=0))
        key, value = both
        key = key * cos_ref[:, lanes] + pltpu.roll(key, HEAD // 2, 1) * sin_ref[:, lanes]
        row_ref[:, lanes] = jnp.concatenate([key, value], axis=0).astype(jnp.bfloat16)
    copies = [
        pltpu.make_async_copy(row_ref, out_ref.at[d], save.at[d]) for d in range(out_ref.shape[0])
    ]
    for copy in copies:
        copy.start()
    for copy in copies:
        copy.wait()


def pack_kernel(jobs, info, after, *rest):
    number = len(jobs)
    inputs, rest = rest[:4], rest[4:]
    outs, rooms, (load, save) = rest[:number], rest[number : 2 * number], rest[2 * number :]
    order = [(job, t) for job in range(number) for t in range(4)]

    def fetch(job, t):
        k, start, width = jobs[job]
        rows = pl.ds(pl.multiple_of(info[k] * BLOCK, BLOCK), BLOCK)
        source = inputs[t].at[rows, pl.ds(start, width)]
        return pltpu.make_async_copy(source, rooms[job].at[t], load.at[job, t])

    def store(job, t):
        return pltpu.make_async_copy(rooms[job].at[t], outs[job].at[t], save.at[job, t])

    for job, t in order:
        fetch(job, t).start()
    for job, t in order:
        fetch(job, t).wait()
        store(job, t).start()
    for job, t in order:
        store(job, t).wait()


def link_kernel(*refs):
    pass


def place_kernel(items, slot, *rest):
    number = len(items)
    parts = rest[:number]
    finals = rest[number + 4 : number + 8]
    rooms, (load, save) = rest[number + 8 : 2 * number + 8], rest[2 * number + 8 :]

    def save_of(i, t):
        k, start, width = items[i]
        top = pl.multiple_of(slot[k] * BLOCK, BLOCK)
        where = finals[t].at[pl.ds(top, BLOCK), pl.ds(start, width)]
        return pltpu.make_async_copy(rooms[i].at[t], where, save.at[i, t])

    loads = [pltpu.make_async_copy(parts[i], rooms[i], load.at[i]) for i in range(number)]
    for move in loads:
        move.start()
    for i in range(number):
        loads[i].wait()
        for t in range(4):
            save_of(i, t).start()
    for i in range(number):
        for t in range(4):
            save_of(i, t).wait()


def far_rows(got, cos_ref, sin_ref, blocks):
    total = got[0].astype(jnp.float32)
    for sender in range(1, got.shape[0]):
        total = total + got[sender].astype(jnp.float32)
    far_k, far_v = total[:blocks], total[blocks:]
    heads = far_k.shape[1] // HEAD
    turned = []
    for head in range(heads):
        lanes = slice(head * HEAD, (head + 1) * HEAD)
        one = far_k[:, lanes]
        turned.append(
            one * cos_ref[:, lanes] - pltpu.roll(one, HEAD // 2, 1) * sin_ref[:, lanes]
        )
    values = [far_v[:, head * HEAD : (head + 1) * HEAD] for head in range(heads)]
    return turned, values


def overwrite(ref, lanes, at, source, pick):
    spot = lax.broadcasted_iota(jnp.int32, (16, HEAD), 0)
    line = lax.broadcasted_iota(jnp.int32, source.shape, 0)
    start = pl.multiple_of(at // 16 * 16, 16)
    row = jnp.sum(jnp.where(line == pick, source, 0.0), axis=0, keepdims=True)
    old = ref[pl.ds(start, 16), lanes].astype(jnp.float32)
    ref[pl.ds(start, 16), lanes] = jnp.where(spot == at - start, row, old).astype(jnp.bfloat16)


def patch_kernel(
    heads, blocks, late, edge, phase, slot, got_hbm, cos_ref, sin_ref, dk_in, dv_in, dk, dv, got,
    room, get, load, save
):
    outs = (dk, dv)
    width = room.shape[-1]
    order = [(k, t) for k in range(blocks) for t in range(2)]

    def span(k):
        return pl.ds(0, edge if k in late else width)

    def here(t, k):
        rows = pl.ds(pl.multiple_of(slot[k] * BLOCK, BLOCK), BLOCK)
        return outs[t].at[rows, span(k)]

    def fetch(t, k):
        return pltpu.make_async_copy(here(t, k), room.at[t, k, :, span(k)], load.at[t, k])

    def store(t, k):
        return pltpu.make_async_copy(room.at[t, k, :, span(k)], here(t, k), save.at[t, k])

    first = pltpu.make_async_copy(got_hbm, got, get)
    first.start()
    for k, t in order:
        fetch(t, k).start()
    first.wait()
    fresh = far_rows(got, cos_ref, sin_ref, blocks)
    for k, t in order:
        fetch(t, k).wait()
        for head in range(edge // HEAD if k in late else heads):
            lanes = slice(head * HEAD, (head + 1) * HEAD)
            overwrite(room.at[t, k], lanes, phase[head], fresh[t][head], slot[k])
        store(t, k).start()
    for k, t in order:
        store(t, k).wait()


def last_kernel(heads, late, edge, phase, slot, got_hbm, cos_ref, sin_ref, *rest):
    pieces = rest[:2]
    outs = rest[6:10]
    got, room, get, load, save = rest[10:]
    blocks = got.shape[1] // 2
    right = pl.ds(edge, room.shape[-1])
    rows = pl.ds(pl.multiple_of(slot[late] * BLOCK, BLOCK), BLOCK)
    first = pltpu.make_async_copy(got_hbm.at[:, :, right], got, get)
    loads, start = [], 0
    for i, piece in enumerate(pieces):
        part = pl.ds(start, piece.shape[-1])
        loads.append(pltpu.make_async_copy(piece, room.at[:, :, part], load.at[i]))
        start += piece.shape[-1]
    stores = [
        pltpu.make_async_copy(room.at[t], outs[t].at[rows, right], save.at[t]) for t in range(4)
    ]
    for move in loads + [first]:
        move.start()
    for move in loads:
        move.wait()
    for t in range(2):
        stores[t].start()
    first.wait()
    fresh = far_rows(got, cos_ref, sin_ref, blocks)
    for t in range(2):
        for head in range(edge // HEAD, heads):
            local_head = head - edge // HEAD
            lanes = slice(local_head * HEAD, (local_head + 1) * HEAD)
            overwrite(room.at[2 + t], lanes, phase[head], fresh[t][local_head], slot[late])
        stores[2 + t].start()
    for store in stores:
        store.wait()


def local(queries, keys, values, output_gradient, dilation_phase, segment_device_count, owner):
    rows, width = queries.shape
    heads = width // HEAD
    blocks = rows // BLOCK
    bal_size = lax.axis_size("bal")
    devices = lax.axis_size("ctx") * bal_size
    total = rows * devices
    count = owner.shape[0]
    assert blocks == bal_size == 4 and bal_size & (bal_size - 1) == 0
    bal = lax.axis_index("bal")
    device = lax.axis_index("ctx") * bal_size + bal
    room = 66_900_000
    big = pltpu.CompilerParams(vmem_limit_bytes=room)
    smem = pl.BlockSpec(memory_space=pltpu.SMEM)
    vmem = pl.BlockSpec(memory_space=pltpu.VMEM)
    anywhere = pl.BlockSpec(memory_space=pl.ANY)
    light = pl.CostEstimate(flops=2_000_000_000, bytes_accessed=5_000_000, transcendentals=0)
    heavy = pl.CostEstimate(flops=20_000_000_000, bytes_accessed=60_000_000, transcendentals=0)

    def tokens_of(ids):
        return (ids[:, None] * BLOCK + jnp.arange(BLOCK, dtype=jnp.int32)[None, :]).reshape(rows)

    def swap(array, k):
        return lax.ppermute(array, "bal", [(i, i ^ k) for i in range(bal_size)])

    steps = jnp.arange(blocks, dtype=jnp.int32)
    held = device * blocks + steps
    goes_to = lax.dynamic_slice_in_dim(owner, device * blocks, blocks) // blocks % bal_size
    partner = steps ^ bal
    which = jnp.sum(jnp.where(goes_to[None, :] == partner[:, None], steps[None, :], 0), axis=1)
    info = jnp.concatenate([which, device * blocks + which]).astype(jnp.int32)
    comes_from = jnp.sum(
        jnp.where(
            owner[None, :] == held[:, None], jnp.arange(count, dtype=jnp.int32)[None, :], 0
        ),
        axis=1,
    )

    first = heads * 3 // 10 * 2
    early = first // 3 * 2
    middle = first + (heads - first) // 4 * 2
    cut, edge, brim = early * HEAD, first * HEAD, middle * HEAD
    originals = (queries, keys, values, output_gradient)

    def send_inputs(jobs, after):
        sizes = [(4, BLOCK, width) for _, _, width in jobs]
        sent = pl.pallas_call(
            functools.partial(pack_kernel, jobs),
            in_specs=[smem] + [anywhere] * 5,
            out_specs=[anywhere] * len(jobs),
            out_shape=[jax.ShapeDtypeStruct(size, jnp.bfloat16) for size in sizes],
            scratch_shapes=[pltpu.VMEM(size, jnp.bfloat16) for size in sizes]
            + [pltpu.SemaphoreType.DMA((len(jobs), 4))] * 2,
            compiler_params=big,
        )(info, after, *originals)
        return sent, [swap(one, job[0]) for one, job in zip(sent, jobs)]

    sent, come_early = send_inputs([(2, 0, cut)], owner)

    cq, sq, ck, sk = tables(tokens_of(held), total)
    own_phase = (held[:, None] * BLOCK + dilation_phase[None, :]).astype(jnp.int32)
    pick_cos, pick_sin = flat_tables(own_phase, total)
    own_far = pl.pallas_call(
        functools.partial(pick_kernel, heads, blocks),
        in_specs=[smem, anywhere, anywhere, vmem, vmem, anywhere],
        out_specs=anywhere,
        out_shape=jax.ShapeDtypeStruct((devices // 2, 2 * blocks, width), jnp.bfloat16),
        scratch_shapes=[
            pltpu.VMEM((rows, width), jnp.bfloat16),
            pltpu.VMEM((rows, width), jnp.bfloat16),
            pltpu.VMEM((2 * blocks, width), jnp.bfloat16),
            pltpu.SemaphoreType.DMA((2,)),
            pltpu.SemaphoreType.DMA((devices // 2,)),
        ],
        compiler_params=big,
    )(
        dilation_phase,
        keys,
        values,
        pick_cos,
        pick_sin,
        sent[0],
    )
    halves = [list(range(0, devices, 2)), list(range(1, devices, 2))]
    near_far = lax.all_to_all(
        own_far,
        ("ctx", "bal"),
        split_axis=0,
        concat_axis=0,
        tiled=True,
        axis_index_groups=halves,
    ).reshape(count, width)
    other_far = swap(near_far, 1)
    jobs = [(2, cut, edge - cut), (3, 0, edge), (1, 0, edge)]
    _, (come_rest, come_3, come_1) = send_inputs(jobs, own_far)
    come_2 = come_early[0]

    ids = (device ^ steps) * blocks
    came = jnp.sum(
        jnp.where(comes_from[None, :] // blocks * blocks == ids[:, None], comes_from[None, :], 0),
        axis=1,
    )
    moved = jnp.concatenate([which, came, partner]).astype(jnp.int32)
    moved_tables = tables(tokens_of(came), total)

    side = 2 * count
    wide = jnp.arange(side, dtype=jnp.int32)
    tall = wide[:, None]
    wide = wide[None, :]
    source = tall % count
    holder = source // blocks
    held_row = (holder ^ device) % 2 * count + holder // 2 * (2 * blocks)
    pull = (wide == held_row + tall // count * blocks + source % blocks).astype(jnp.bfloat16)
    lands = owner // blocks
    lands = (lands ^ device) % 2 * count + lands // 2 * (2 * blocks) + owner % blocks
    push = (jnp.concatenate([lands, lands + blocks])[None, :] == tall).astype(jnp.bfloat16)

    per_step = 2
    columns = per_step * HEAD
    fixed = lambda h, *_: (0, 0)
    square = pl.BlockSpec((side, side), fixed)
    table = pl.BlockSpec((rows, HEAD), fixed)
    part = pl.BlockSpec((4, BLOCK, columns), lambda h, *_: (0, 0, h))
    def attend_held(begin, end, waits, carried):
        skip = begin // per_step
        tensor = pl.BlockSpec((rows, columns), lambda h, *_: (0, h + skip))
        far = pl.BlockSpec((count, columns), lambda h, *_: (0, h + skip))
        extra = carried + waits
        results = pl.pallas_call(
            functools.partial(attend_kernel, per_step, blocks, count, begin, 0, len(extra)),
            grid_spec=pltpu.PrefetchScalarGridSpec(
                num_scalar_prefetch=3,
                grid=((end - begin) // per_step,),
                in_specs=[far, far, square, square]
                + [table] * 4
                + [tensor] * 4
                + [anywhere] * len(extra),
                out_specs=[part] * blocks + [far] * 2,
            ),
            out_shape=[jax.ShapeDtypeStruct((4, BLOCK, (end - begin) * HEAD), jnp.bfloat16)]
            * blocks
            + [jax.ShapeDtypeStruct((count, width), jnp.bfloat16)] * 2,
            input_output_aliases={15 + i: blocks + i for i in range(len(carried))},
            compiler_params=big,
            cost_estimate=heavy,
        )(
            info,
            dilation_phase,
            segment_device_count,
            near_far,
            other_far,
            pull,
            push,
            cq,
            sq,
            ck,
            sk,
            *originals,
            *extra,
        )
        return list(results[:blocks]), list(results[blocks:])

    waits = list(moved_tables) + [come_1, come_2]
    parts, payload = attend_held(first, middle, waits, [])
    parts_last, payload = attend_held(middle, heads, [], payload)
    for k in range(1, blocks):
        parts[k] = swap(parts[k], k)
        parts_last[k] = swap(parts_last[k], k)

    shapes = [jax.ShapeDtypeStruct((blocks, BLOCK, width), jnp.bfloat16)] * 4
    shapes = shapes + [jax.ShapeDtypeStruct((count, width), jnp.bfloat16)] * 2

    def attend_relaid(begin, end, come, carried):
        skip = begin // per_step
        tensor = pl.BlockSpec((BLOCK, columns), lambda h, info, *_: (info[0], h + skip))
        far = pl.BlockSpec((count, columns), lambda h, *_: (0, h + skip))
        whole = pl.BlockSpec((blocks, BLOCK, columns), lambda h, *_: (0, 0, h + skip))
        shifted = pl.BlockSpec((4, BLOCK, columns), lambda h, *_: (0, 0, h + skip))
        operands = 3 + 4 + 4 + 4 + blocks - 1
        return pl.pallas_call(
            functools.partial(attend_kernel, per_step, blocks, count, begin, len(carried), 0),
            grid_spec=pltpu.PrefetchScalarGridSpec(
                num_scalar_prefetch=3,
                grid=((end - begin) // per_step,),
                in_specs=[far, far, square, square]
                + [table] * 4
                + [tensor] * 4
                + [shifted, part, shifted]
                + [anywhere] * len(carried),
                out_specs=[whole] * 4 + [far] * 2,
                ),
            out_shape=shapes,
            input_output_aliases={
                operands + i: 6 - len(carried) + i for i in range(len(carried))
            },
            compiler_params=big,
            cost_estimate=light,
        )(
            moved,
            dilation_phase,
            segment_device_count,
            near_far,
            other_far,
            pull,
            push,
            *moved_tables,
            *originals,
            *come,
            *carried,
        )

    results = attend_relaid(0, early, [come_1, come_2, come_3], payload)
    results = attend_relaid(early, first, [come_1, come_rest, come_3], results)
    finals = [one.reshape(rows, width) for one in results[:4]]

    def after(array, wait):
        return pl.pallas_call(
            link_kernel,
            in_specs=[anywhere] * 2,
            out_specs=anywhere,
            out_shape=jax.ShapeDtypeStruct(array.shape, array.dtype),
            input_output_aliases={0: 0},
            compiler_params=pltpu.CompilerParams(vmem_limit_bytes=room, has_side_effects=True),
        )(array, wait)

    crossing = swap(after(results[5], parts[2]), 1)
    payload = results[4].astype(jnp.float32) + crossing.astype(jnp.float32)
    payload = after(payload.astype(jnp.bfloat16), parts_last[2])
    got = lax.all_to_all(
        payload.reshape(devices // 2, 2 * blocks, width),
        ("ctx", "bal"),
        split_axis=0,
        concat_axis=0,
        tiled=True,
        axis_index_groups=halves,
    )

    new_phase = (comes_from[:, None] * BLOCK + dilation_phase[None, :]).astype(jnp.int32)
    new_cos, new_sin = flat_tables(new_phase, total)
    out = jax.ShapeDtypeStruct((rows, width), jnp.bfloat16)
    slots = partner.astype(jnp.int32)
    items = [(k, edge, brim - edge) for k in range(3)]
    items += [(k, brim, width - brim) for k in range(3)]
    number = len(items)
    finals = pl.pallas_call(
        functools.partial(place_kernel, items),
        in_specs=[smem] + [anywhere] * (number + 4),
        out_specs=[anywhere] * 4,
        out_shape=[out] * 4,
        input_output_aliases={1 + number + t: t for t in range(4)},
        scratch_shapes=[pltpu.VMEM((4, BLOCK, item[2]), jnp.bfloat16) for item in items]
        + [pltpu.SemaphoreType.DMA((number,)), pltpu.SemaphoreType.DMA((number, 4))],
        compiler_params=big,
        cost_estimate=light,
    )(slots, *parts[:3], *parts_last[:3], *finals)
    late = 3
    patched = pl.pallas_call(
        functools.partial(patch_kernel, heads, blocks, (late,), edge),
        in_specs=[smem, smem, anywhere, vmem, vmem, anywhere, anywhere],
        out_specs=[anywhere] * 2,
        out_shape=[out] * 2,
        input_output_aliases={5: 0, 6: 1},
        scratch_shapes=[
            pltpu.VMEM((devices // 2, 2 * blocks, width), jnp.bfloat16),
            pltpu.VMEM((2, blocks, BLOCK, width), jnp.bfloat16),
            pltpu.SemaphoreType.DMA(()),
            pltpu.SemaphoreType.DMA((2, blocks)),
            pltpu.SemaphoreType.DMA((2, blocks)),
        ],
        compiler_params=big,
        cost_estimate=light,
    )(dilation_phase, slots, got, new_cos, new_sin, finals[2], finals[3])
    return tuple(
        pl.pallas_call(
            functools.partial(last_kernel, heads, late, edge),
            in_specs=[smem, smem, anywhere, vmem, vmem] + [anywhere] * 6,
            out_specs=[anywhere] * 4,
            out_shape=[out] * 4,
            input_output_aliases={7 + t: t for t in range(4)},
            scratch_shapes=[
                pltpu.VMEM((devices // 2, 2 * blocks, width - edge), jnp.bfloat16),
                pltpu.VMEM((4, BLOCK, width - edge), jnp.bfloat16),
                pltpu.SemaphoreType.DMA(()),
                pltpu.SemaphoreType.DMA((2,)),
                pltpu.SemaphoreType.DMA((4,)),
            ],
            compiler_params=big,
        )(
            dilation_phase,
            slots,
            got,
            new_cos[:, edge:],
            new_sin[:, edge:],
            parts[late],
            parts_last[late],
            finals[0],
            finals[1],
            *patched,
        )
    )


def solution(mesh):
    token = P(("groups", "ctx", "bal"), "head")
    return jax.shard_map(
        local,
        mesh=mesh,
        in_specs=(token, token, token, token, P("head"), P("head"), P("groups")),
        out_specs=(token, token, token, token),
        check_vma=False,
    )
```

```python
import functools
import math

import jax
import jax.numpy as jnp
from jax import lax
from jax.experimental import pallas as pl
from jax.experimental.pallas import tpu as pltpu
from jax.sharding import PartitionSpec as P

BLOCK = 128
HEAD = 128
LOG2E = 1.4426950408889634
NT = (((1,), (1,)), ((), ()))
TN = (((0,), (0,)), ((), ()))


def tables(positions, total):
    half = HEAD // 2
    pair = jnp.arange(half, dtype=jnp.float32)
    inverse = jnp.exp(pair * (-2.0 * math.log(10000.0) / HEAD))
    where = positions.astype(jnp.float32)[..., None]
    angles = where * inverse
    base = (2.0 * pair / HEAD + 0.4) / 1.4
    growth = jnp.exp((2.0 * where - total) / total * jnp.log(base))
    cosine, sine = jnp.cos(angles), jnp.sin(angles)

    def pack(scale):
        first, second = cosine * scale, sine * scale
        return (
            jnp.concatenate([first, first], axis=-1),
            jnp.concatenate([-second, second], axis=-1),
        )

    return pack(growth) + pack(1.0 / growth)


def flat_tables(positions, total):
    half = HEAD // 2
    lane = jnp.arange(positions.shape[1] * HEAD, dtype=jnp.int32) % HEAD
    pair = (lane % half).astype(jnp.float32)
    inverse = jnp.exp(pair * (-2.0 * math.log(10000.0) / HEAD))
    where = jnp.repeat(positions.astype(jnp.float32), HEAD, axis=1)
    angles = where * inverse[None, :]
    base = (2.0 * pair / HEAD + 0.4) / 1.4
    growth = jnp.exp((2.0 * where - total) / total * jnp.log(base)[None, :])
    sine = jnp.where(lane[None, :] < half, -jnp.sin(angles), jnp.sin(angles))
    return jnp.cos(angles) / growth, sine / growth


def dot(left, right, dims=None):
    if dims is None:
        dims = (((1,), (0,)), ((), ()))
    return lax.dot_general(left, right, dims, preferred_element_type=jnp.float32)


def attend_kernel(
    per_step, blocks, count, first, relaid, waits, info, phase, seg, far_ref, other_ref, pull_ref, push_ref, *rest
):
    cq_ref, sq_ref, ck_ref, sk_ref = rest[:4]
    own = rest[4:8]
    rest = rest[8:]
    if relaid:
        come, rest = rest[: blocks - 1], rest[blocks - 1 + relaid :]
        finals, rest = rest[:4], rest[4:]
    else:
        finals, rest = rest[waits : waits + blocks], rest[waits + blocks :]
    own_pay, other_pay = rest
    scale = 1.0 / math.sqrt(HEAD)
    key_at = lax.broadcasted_iota(jnp.int32, (BLOCK, BLOCK), 0)
    query_at = lax.broadcasted_iota(jnp.int32, (BLOCK, BLOCK), 1)
    far_at = lax.broadcasted_iota(jnp.int32, (count, BLOCK), 0)
    far_query = lax.broadcasted_iota(jnp.int32, (count, BLOCK), 1)
    half = HEAD // 2
    for sub in range(per_step):
        head = first + pl.program_id(0) * per_step + sub
        lanes = slice(sub * HEAD, (sub + 1) * HEAD)
        held = jnp.concatenate([far_ref[:, lanes], other_ref[:, lanes]], axis=0)
        both = dot(pull_ref[...], held).astype(jnp.bfloat16)
        far_k, far_v = both[:count], both[count:]
        span = seg[head] * blocks
        at = phase[head]
        causal = (key_at <= query_at) & (key_at != at)
        behind = far_at * BLOCK + at - far_query
        p_far, d_far, q_all, g_all = [], [], [], []
        for k in range(blocks):
            if relaid:
                rows = slice(k * BLOCK, (k + 1) * BLOCK)
                source = [ref[:, lanes] for ref in own]
                if k:
                    source = [come[k - 1][t, :, lanes] for t in range(4)]
            else:
                rows = pl.ds(pl.multiple_of(info[k] * BLOCK, BLOCK), BLOCK)
                source = [ref[rows, lanes] for ref in own]
            block = info[blocks + k]
            low = block & (-span)
            cq, sq, ck, sk = cq_ref[rows, :], sq_ref[rows, :], ck_ref[rows, :], sk_ref[rows, :]
            raw_q, raw_k, value, grad = source
            raw_q = raw_q.astype(jnp.float32)
            raw_k = raw_k.astype(jnp.float32)
            tq = (raw_q * cq + pltpu.roll(raw_q, half, 1) * sq).astype(jnp.bfloat16)
            tk = (raw_k * ck + pltpu.roll(raw_k, half, 1) * sk).astype(jnp.bfloat16)
            keys = jnp.concatenate([tk, far_k], axis=0)
            vals = jnp.concatenate([value, far_v], axis=0)
            score = dot(keys, tq, NT)
            allowed = (far_at >= low) & (behind <= block * BLOCK)
            score = jnp.concatenate(
                [
                    jnp.where(causal, score[:BLOCK], -jnp.inf),
                    jnp.where(allowed, score[BLOCK:], -jnp.inf),
                ],
                axis=0,
            )
            top = jnp.max(score, axis=0, keepdims=True)
            weight = jnp.exp2((score - top) * (scale * LOG2E))
            prob = weight * (1.0 / jnp.sum(weight, axis=0, keepdims=True))
            p16 = prob.astype(jnp.bfloat16)
            dprob = dot(vals, grad, NT)
            delta = jnp.sum(p16.astype(jnp.float32) * dprob, axis=0, keepdims=True)
            d16 = (prob * (dprob - delta)).astype(jnp.bfloat16)
            out = dot(p16, vals, TN)
            dq = dot(d16, keys, TN) * scale
            dk = dot(d16[:BLOCK], tq) * scale
            dv = dot(p16[:BLOCK], grad)
            made = (
                out,
                dq * cq - pltpu.roll(dq, half, 1) * sq,
                dk * ck - pltpu.roll(dk, half, 1) * sk,
                dv,
            )
            for t in range(4):
                if relaid:
                    finals[t][info[2 * blocks + k], :, lanes] = made[t].astype(jnp.bfloat16)
                else:
                    finals[k][t, :, lanes] = made[t].astype(jnp.bfloat16)
            p_far.append(p16[BLOCK:])
            d_far.append(d16[BLOCK:])
            q_all.append(tq)
            g_all.append(grad)
        far_dk = dot(jnp.concatenate(d_far, axis=1), jnp.concatenate(q_all, axis=0)) * scale
        far_dv = dot(jnp.concatenate(p_far, axis=1), jnp.concatenate(g_all, axis=0))
        far_sum = jnp.concatenate([far_dk, far_dv], axis=0).astype(jnp.bfloat16)
        pay = dot(push_ref[...], far_sum).astype(jnp.bfloat16)
        own_pay[:, lanes] = pay[:count]
        other_pay[:, lanes] = pay[count:]


def pick_kernel(
    heads, blocks, phase, k_hbm, v_hbm, cos_ref, sin_ref, after, out_ref, k_ref, v_ref, row_ref,
    load, save
):
    moves = [
        pltpu.make_async_copy(k_hbm, k_ref, load.at[0]),
        pltpu.make_async_copy(v_hbm, v_ref, load.at[1]),
    ]
    for move in moves:
        move.start()
    for move in moves:
        move.wait()
    spot = lax.broadcasted_iota(jnp.int32, (16, HEAD), 0)
    for head in range(heads):
        at = phase[head]
        start = pl.multiple_of(at // 16 * 16, 16)
        lanes = slice(head * HEAD, (head + 1) * HEAD)
        both = []
        for ref in (k_ref, v_ref):
            rows = []
            for k in range(blocks):
                tile = ref[pl.ds(pl.multiple_of(k * BLOCK + start, 16), 16), lanes]
                tile = jnp.where(spot == at - start, tile.astype(jnp.float32), 0.0)
                rows.append(jnp.sum(tile, axis=0, keepdims=True))
            both.append(jnp.concatenate(rows, axis=0))
        key, value = both
        key = key * cos_ref[:, lanes] + pltpu.roll(key, HEAD // 2, 1) * sin_ref[:, lanes]
        row_ref[:, lanes] = jnp.concatenate([key, value], axis=0).astype(jnp.bfloat16)
    copies = [
        pltpu.make_async_copy(row_ref, out_ref.at[d], save.at[d]) for d in range(out_ref.shape[0])
    ]
    for copy in copies:
        copy.start()
    for copy in copies:
        copy.wait()


def pack_kernel(jobs, info, after, *rest):
    number = len(jobs)
    inputs, rest = rest[:4], rest[4:]
    outs, rooms, (load, save) = rest[:number], rest[number : 2 * number], rest[2 * number :]
    order = [(job, t) for job in range(number) for t in range(4)]

    def fetch(job, t):
        k, start, width = jobs[job]
        rows = pl.ds(pl.multiple_of(info[k] * BLOCK, BLOCK), BLOCK)
        source = inputs[t].at[rows, pl.ds(start, width)]
        return pltpu.make_async_copy(source, rooms[job].at[t], load.at[job, t])

    def store(job, t):
        return pltpu.make_async_copy(rooms[job].at[t], outs[job].at[t], save.at[job, t])

    for job, t in order:
        fetch(job, t).start()
    for job, t in order:
        fetch(job, t).wait()
        store(job, t).start()
    for job, t in order:
        store(job, t).wait()


def link_kernel(*refs):
    pass


def place_kernel(items, slot, *rest):
    number = len(items)
    parts = rest[:number]
    finals = rest[number + 4 : number + 8]
    rooms, (load, save) = rest[number + 8 : 2 * number + 8], rest[2 * number + 8 :]

    def save_of(i, t):
        k, start, width = items[i]
        top = pl.multiple_of(slot[k] * BLOCK, BLOCK)
        where = finals[t].at[pl.ds(top, BLOCK), pl.ds(start, width)]
        return pltpu.make_async_copy(rooms[i].at[t], where, save.at[i, t])

    loads = [pltpu.make_async_copy(parts[i], rooms[i], load.at[i]) for i in range(number)]
    for move in loads:
        move.start()
    for i in range(number):
        loads[i].wait()
        for t in range(4):
            save_of(i, t).start()
    for i in range(number):
        for t in range(4):
            save_of(i, t).wait()


def far_rows(got, cos_ref, sin_ref, blocks):
    total = got[0].astype(jnp.float32)
    for sender in range(1, got.shape[0]):
        total = total + got[sender].astype(jnp.float32)
    far_k, far_v = total[:blocks], total[blocks:]
    heads = far_k.shape[1] // HEAD
    turned = []
    for head in range(heads):
        lanes = slice(head * HEAD, (head + 1) * HEAD)
        one = far_k[:, lanes]
        turned.append(
            one * cos_ref[:, lanes] - pltpu.roll(one, HEAD // 2, 1) * sin_ref[:, lanes]
        )
    values = [far_v[:, head * HEAD : (head + 1) * HEAD] for head in range(heads)]
    return turned, values


def overwrite(ref, lanes, at, source, pick):
    spot = lax.broadcasted_iota(jnp.int32, (16, HEAD), 0)
    line = lax.broadcasted_iota(jnp.int32, source.shape, 0)
    start = pl.multiple_of(at // 16 * 16, 16)
    row = jnp.sum(jnp.where(line == pick, source, 0.0), axis=0, keepdims=True)
    old = ref[pl.ds(start, 16), lanes].astype(jnp.float32)
    ref[pl.ds(start, 16), lanes] = jnp.where(spot == at - start, row, old).astype(jnp.bfloat16)


def patch_kernel(
    heads, blocks, late, edge, phase, slot, got_hbm, cos_ref, sin_ref, dk_in, dv_in, dk, dv, got,
    room, get, load, save
):
    outs = (dk, dv)
    width = room.shape[-1]
    order = [(k, t) for k in range(blocks) for t in range(2)]

    def span(k):
        return pl.ds(0, edge if k in late else width)

    def here(t, k):
        rows = pl.ds(pl.multiple_of(slot[k] * BLOCK, BLOCK), BLOCK)
        return outs[t].at[rows, span(k)]

    def fetch(t, k):
        return pltpu.make_async_copy(here(t, k), room.at[t, k, :, span(k)], load.at[t, k])

    def store(t, k):
        return pltpu.make_async_copy(room.at[t, k, :, span(k)], here(t, k), save.at[t, k])

    first = pltpu.make_async_copy(got_hbm, got, get)
    first.start()
    for k, t in order:
        fetch(t, k).start()
    first.wait()
    fresh = far_rows(got, cos_ref, sin_ref, blocks)
    for k, t in order:
        fetch(t, k).wait()
        for head in range(edge // HEAD if k in late else heads):
            lanes = slice(head * HEAD, (head + 1) * HEAD)
            overwrite(room.at[t, k], lanes, phase[head], fresh[t][head], slot[k])
        store(t, k).start()
    for k, t in order:
        store(t, k).wait()


def last_kernel(heads, late, edge, phase, slot, got_hbm, cos_ref, sin_ref, *rest):
    pieces = rest[:2]
    outs = rest[6:10]
    got, room, get, load, save = rest[10:]
    blocks = got.shape[1] // 2
    right = pl.ds(edge, room.shape[-1])
    rows = pl.ds(pl.multiple_of(slot[late] * BLOCK, BLOCK), BLOCK)
    first = pltpu.make_async_copy(got_hbm.at[:, :, right], got, get)
    loads, start = [], 0
    for i, piece in enumerate(pieces):
        part = pl.ds(start, piece.shape[-1])
        loads.append(pltpu.make_async_copy(piece, room.at[:, :, part], load.at[i]))
        start += piece.shape[-1]
    stores = [
        pltpu.make_async_copy(room.at[t], outs[t].at[rows, right], save.at[t]) for t in range(4)
    ]
    for move in loads + [first]:
        move.start()
    for move in loads:
        move.wait()
    for t in range(2):
        stores[t].start()
    first.wait()
    fresh = far_rows(got, cos_ref, sin_ref, blocks)
    for t in range(2):
        for head in range(edge // HEAD, heads):
            local_head = head - edge // HEAD
            lanes = slice(local_head * HEAD, (local_head + 1) * HEAD)
            overwrite(room.at[2 + t], lanes, phase[head], fresh[t][local_head], slot[late])
        stores[2 + t].start()
    for store in stores:
        store.wait()


def local(queries, keys, values, output_gradient, dilation_phase, segment_device_count, owner):
    rows, width = queries.shape
    heads = width // HEAD
    blocks = rows // BLOCK
    bal_size = lax.axis_size("bal")
    devices = lax.axis_size("ctx") * bal_size
    total = rows * devices
    count = owner.shape[0]
    assert blocks == bal_size == 4 and bal_size & (bal_size - 1) == 0
    bal = lax.axis_index("bal")
    device = lax.axis_index("ctx") * bal_size + bal
    room = 66_900_000
    big = pltpu.CompilerParams(vmem_limit_bytes=room)
    smem = pl.BlockSpec(memory_space=pltpu.SMEM)
    vmem = pl.BlockSpec(memory_space=pltpu.VMEM)
    anywhere = pl.BlockSpec(memory_space=pl.ANY)
    light = pl.CostEstimate(flops=2_000_000_000, bytes_accessed=5_000_000, transcendentals=0)
    heavy = pl.CostEstimate(flops=20_000_000_000, bytes_accessed=60_000_000, transcendentals=0)

    def tokens_of(ids):
        return (ids[:, None] * BLOCK + jnp.arange(BLOCK, dtype=jnp.int32)[None, :]).reshape(rows)

    def swap(array, k):
        return lax.ppermute(array, "bal", [(i, i ^ k) for i in range(bal_size)])

    steps = jnp.arange(blocks, dtype=jnp.int32)
    held = device * blocks + steps
    goes_to = lax.dynamic_slice_in_dim(owner, device * blocks, blocks) // blocks % bal_size
    partner = steps ^ bal
    which = jnp.sum(jnp.where(goes_to[None, :] == partner[:, None], steps[None, :], 0), axis=1)
    info = jnp.concatenate([which, device * blocks + which]).astype(jnp.int32)
    comes_from = jnp.sum(
        jnp.where(
            owner[None, :] == held[:, None], jnp.arange(count, dtype=jnp.int32)[None, :], 0
        ),
        axis=1,
    )

    first = heads * 3 // 10 * 2
    early = first // 4 * 2
    middle = heads - 2
    cut, edge, brim = early * HEAD, first * HEAD, middle * HEAD
    originals = (queries, keys, values, output_gradient)

    def send_inputs(jobs, after):
        sizes = [(4, BLOCK, width) for _, _, width in jobs]
        sent = pl.pallas_call(
            functools.partial(pack_kernel, jobs),
            in_specs=[smem] + [anywhere] * 5,
            out_specs=[anywhere] * len(jobs),
            out_shape=[jax.ShapeDtypeStruct(size, jnp.bfloat16) for size in sizes],
            scratch_shapes=[pltpu.VMEM(size, jnp.bfloat16) for size in sizes]
            + [pltpu.SemaphoreType.DMA((len(jobs), 4))] * 2,
            compiler_params=big,
        )(info, after, *originals)
        return sent, [swap(one, job[0]) for one, job in zip(sent, jobs)]

    sent, come_early = send_inputs([(2, 0, cut)], owner)

    cq, sq, ck, sk = tables(tokens_of(held), total)
    own_phase = (held[:, None] * BLOCK + dilation_phase[None, :]).astype(jnp.int32)
    pick_cos, pick_sin = flat_tables(own_phase, total)
    own_far = pl.pallas_call(
        functools.partial(pick_kernel, heads, blocks),
        in_specs=[smem, anywhere, anywhere, vmem, vmem, anywhere],
        out_specs=anywhere,
        out_shape=jax.ShapeDtypeStruct((devices // 2, 2 * blocks, width), jnp.bfloat16),
        scratch_shapes=[
            pltpu.VMEM((rows, width), jnp.bfloat16),
            pltpu.VMEM((rows, width), jnp.bfloat16),
            pltpu.VMEM((2 * blocks, width), jnp.bfloat16),
            pltpu.SemaphoreType.DMA((2,)),
            pltpu.SemaphoreType.DMA((devices // 2,)),
        ],
        compiler_params=big,
    )(
        dilation_phase,
        keys,
        values,
        pick_cos,
        pick_sin,
        sent[0],
    )
    halves = [list(range(0, devices, 2)), list(range(1, devices, 2))]
    near_far = lax.all_to_all(
        own_far,
        ("ctx", "bal"),
        split_axis=0,
        concat_axis=0,
        tiled=True,
        axis_index_groups=halves,
    ).reshape(count, width)
    other_far = swap(near_far, 1)
    jobs = [(2, cut, edge - cut), (3, 0, edge), (1, 0, edge)]
    _, (come_rest, come_3, come_1) = send_inputs(jobs, own_far)
    come_2 = come_early[0]

    ids = (device ^ steps) * blocks
    came = jnp.sum(
        jnp.where(comes_from[None, :] // blocks * blocks == ids[:, None], comes_from[None, :], 0),
        axis=1,
    )
    moved = jnp.concatenate([which, came, partner]).astype(jnp.int32)
    moved_tables = tables(tokens_of(came), total)

    side = 2 * count
    wide = jnp.arange(side, dtype=jnp.int32)
    tall = wide[:, None]
    wide = wide[None, :]
    source = tall % count
    holder = source // blocks
    held_row = (holder ^ device) % 2 * count + holder // 2 * (2 * blocks)
    pull = (wide == held_row + tall // count * blocks + source % blocks).astype(jnp.bfloat16)
    lands = owner // blocks
    lands = (lands ^ device) % 2 * count + lands // 2 * (2 * blocks) + owner % blocks
    push = (jnp.concatenate([lands, lands + blocks])[None, :] == tall).astype(jnp.bfloat16)

    per_step = 2
    columns = per_step * HEAD
    fixed = lambda h, *_: (0, 0)
    square = pl.BlockSpec((side, side), fixed)
    table = pl.BlockSpec((rows, HEAD), fixed)
    part = pl.BlockSpec((4, BLOCK, columns), lambda h, *_: (0, 0, h))
    def attend_held(begin, end, waits, carried):
        skip = begin // per_step
        tensor = pl.BlockSpec((rows, columns), lambda h, *_: (0, h + skip))
        far = pl.BlockSpec((count, columns), lambda h, *_: (0, h + skip))
        extra = carried + waits
        results = pl.pallas_call(
            functools.partial(attend_kernel, per_step, blocks, count, begin, 0, len(extra)),
            grid_spec=pltpu.PrefetchScalarGridSpec(
                num_scalar_prefetch=3,
                grid=((end - begin) // per_step,),
                in_specs=[far, far, square, square]
                + [table] * 4
                + [tensor] * 4
                + [anywhere] * len(extra),
                out_specs=[part] * blocks + [far] * 2,
            ),
            out_shape=[jax.ShapeDtypeStruct((4, BLOCK, (end - begin) * HEAD), jnp.bfloat16)]
            * blocks
            + [jax.ShapeDtypeStruct((count, width), jnp.bfloat16)] * 2,
            input_output_aliases={15 + i: blocks + i for i in range(len(carried))},
            compiler_params=big,
            cost_estimate=heavy,
        )(
            info,
            dilation_phase,
            segment_device_count,
            near_far,
            other_far,
            pull,
            push,
            cq,
            sq,
            ck,
            sk,
            *originals,
            *extra,
        )
        return list(results[:blocks]), list(results[blocks:])

    waits = list(moved_tables) + [come_1, come_2]
    parts, payload = attend_held(first, middle, waits, [])
    parts_last, payload = attend_held(middle, heads, [], payload)
    for k in range(1, blocks):
        parts[k] = swap(parts[k], k)
        parts_last[k] = swap(parts_last[k], k)

    shapes = [jax.ShapeDtypeStruct((blocks, BLOCK, width), jnp.bfloat16)] * 4
    shapes = shapes + [jax.ShapeDtypeStruct((count, width), jnp.bfloat16)] * 2

    def attend_relaid(begin, end, come, carried):
        skip = begin // per_step
        tensor = pl.BlockSpec((BLOCK, columns), lambda h, info, *_: (info[0], h + skip))
        far = pl.BlockSpec((count, columns), lambda h, *_: (0, h + skip))
        whole = pl.BlockSpec((blocks, BLOCK, columns), lambda h, *_: (0, 0, h + skip))
        shifted = pl.BlockSpec((4, BLOCK, columns), lambda h, *_: (0, 0, h + skip))
        operands = 3 + 4 + 4 + 4 + blocks - 1
        return pl.pallas_call(
            functools.partial(attend_kernel, per_step, blocks, count, begin, len(carried), 0),
            grid_spec=pltpu.PrefetchScalarGridSpec(
                num_scalar_prefetch=3,
                grid=((end - begin) // per_step,),
                in_specs=[far, far, square, square]
                + [table] * 4
                + [tensor] * 4
                + [shifted, part, shifted]
                + [anywhere] * len(carried),
                out_specs=[whole] * 4 + [far] * 2,
                ),
            out_shape=shapes,
            input_output_aliases={
                operands + i: 6 - len(carried) + i for i in range(len(carried))
            },
            compiler_params=big,
            cost_estimate=light,
        )(
            moved,
            dilation_phase,
            segment_device_count,
            near_far,
            other_far,
            pull,
            push,
            *moved_tables,
            *originals,
            *come,
            *carried,
        )

    results = attend_relaid(0, early, [come_1, come_2, come_3], payload)
    results = attend_relaid(early, first, [come_1, come_rest, come_3], results)
    finals = [one.reshape(rows, width) for one in results[:4]]

    def after(array, wait):
        return pl.pallas_call(
            link_kernel,
            in_specs=[anywhere] * 2,
            out_specs=anywhere,
            out_shape=jax.ShapeDtypeStruct(array.shape, array.dtype),
            input_output_aliases={0: 0},
            compiler_params=pltpu.CompilerParams(vmem_limit_bytes=room, has_side_effects=True),
        )(array, wait)

    crossing = swap(after(results[5], parts[2]), 1)
    payload = results[4].astype(jnp.float32) + crossing.astype(jnp.float32)
    payload = after(payload.astype(jnp.bfloat16), parts_last[2])
    got = lax.all_to_all(
        payload.reshape(devices // 2, 2 * blocks, width),
        ("ctx", "bal"),
        split_axis=0,
        concat_axis=0,
        tiled=True,
        axis_index_groups=halves,
    )

    new_phase = (comes_from[:, None] * BLOCK + dilation_phase[None, :]).astype(jnp.int32)
    new_cos, new_sin = flat_tables(new_phase, total)
    out = jax.ShapeDtypeStruct((rows, width), jnp.bfloat16)
    slots = partner.astype(jnp.int32)
    items = [(k, edge, brim - edge) for k in range(3)]
    items += [(k, brim, width - brim) for k in range(3)]
    number = len(items)
    finals = pl.pallas_call(
        functools.partial(place_kernel, items),
        in_specs=[smem] + [anywhere] * (number + 4),
        out_specs=[anywhere] * 4,
        out_shape=[out] * 4,
        input_output_aliases={1 + number + t: t for t in range(4)},
        scratch_shapes=[pltpu.VMEM((4, BLOCK, item[2]), jnp.bfloat16) for item in items]
        + [pltpu.SemaphoreType.DMA((number,)), pltpu.SemaphoreType.DMA((number, 4))],
        compiler_params=big,
        cost_estimate=light,
    )(slots, *parts[:3], *parts_last[:3], *finals)
    late = 3
    patched = pl.pallas_call(
        functools.partial(patch_kernel, heads, blocks, (late,), edge),
        in_specs=[smem, smem, anywhere, vmem, vmem, anywhere, anywhere],
        out_specs=[anywhere] * 2,
        out_shape=[out] * 2,
        input_output_aliases={5: 0, 6: 1},
        scratch_shapes=[
            pltpu.VMEM((devices // 2, 2 * blocks, width), jnp.bfloat16),
            pltpu.VMEM((2, blocks, BLOCK, width), jnp.bfloat16),
            pltpu.SemaphoreType.DMA(()),
            pltpu.SemaphoreType.DMA((2, blocks)),
            pltpu.SemaphoreType.DMA((2, blocks)),
        ],
        compiler_params=big,
        cost_estimate=light,
    )(dilation_phase, slots, got, new_cos, new_sin, finals[2], finals[3])
    return tuple(
        pl.pallas_call(
            functools.partial(last_kernel, heads, late, edge),
            in_specs=[smem, smem, anywhere, vmem, vmem] + [anywhere] * 6,
            out_specs=[anywhere] * 4,
            out_shape=[out] * 4,
            input_output_aliases={7 + t: t for t in range(4)},
            scratch_shapes=[
                pltpu.VMEM((devices // 2, 2 * blocks, width - edge), jnp.bfloat16),
                pltpu.VMEM((4, BLOCK, width - edge), jnp.bfloat16),
                pltpu.SemaphoreType.DMA(()),
                pltpu.SemaphoreType.DMA((2,)),
                pltpu.SemaphoreType.DMA((4,)),
            ],
            compiler_params=big,
        )(
            dilation_phase,
            slots,
            got,
            new_cos[:, edge:],
            new_sin[:, edge:],
            parts[late],
            parts_last[late],
            finals[0],
            finals[1],
            *patched,
        )
    )


def solution(mesh):
    token = P(("groups", "ctx", "bal"), "head")
    return jax.shard_map(
        local,
        mesh=mesh,
        in_specs=(token, token, token, token, P("head"), P("head"), P("groups")),
        out_specs=(token, token, token, token),
        check_vma=False,
    )
```

```python
import functools
import math

import jax
import jax.numpy as jnp
from jax import lax
from jax.experimental import pallas as pl
from jax.experimental.pallas import tpu as pltpu
from jax.sharding import PartitionSpec as P

BLOCK = 128
HEAD = 128
LOG2E = 1.4426950408889634
NT = (((1,), (1,)), ((), ()))
TN = (((0,), (0,)), ((), ()))


def tables(positions, total):
    half = HEAD // 2
    pair = jnp.arange(half, dtype=jnp.float32)
    inverse = jnp.exp(pair * (-2.0 * math.log(10000.0) / HEAD))
    where = positions.astype(jnp.float32)[..., None]
    angles = where * inverse
    base = (2.0 * pair / HEAD + 0.4) / 1.4
    growth = jnp.exp((2.0 * where - total) / total * jnp.log(base))
    cosine, sine = jnp.cos(angles), jnp.sin(angles)

    def pack(scale):
        first, second = cosine * scale, sine * scale
        return (
            jnp.concatenate([first, first], axis=-1),
            jnp.concatenate([-second, second], axis=-1),
        )

    return pack(growth) + pack(1.0 / growth)


def flat_tables(positions, total):
    half = HEAD // 2
    lane = jnp.arange(positions.shape[1] * HEAD, dtype=jnp.int32) % HEAD
    pair = (lane % half).astype(jnp.float32)
    inverse = jnp.exp(pair * (-2.0 * math.log(10000.0) / HEAD))
    where = jnp.repeat(positions.astype(jnp.float32), HEAD, axis=1)
    angles = where * inverse[None, :]
    base = (2.0 * pair / HEAD + 0.4) / 1.4
    growth = jnp.exp((2.0 * where - total) / total * jnp.log(base)[None, :])
    sine = jnp.where(lane[None, :] < half, -jnp.sin(angles), jnp.sin(angles))
    return jnp.cos(angles) / growth, sine / growth


def dot(left, right, dims=None):
    if dims is None:
        dims = (((1,), (0,)), ((), ()))
    return lax.dot_general(left, right, dims, preferred_element_type=jnp.float32)


def attend_kernel(
    per_step, blocks, count, first, relaid, waits, info, phase, seg, far_ref, other_ref, pull_ref, push_ref, *rest
):
    cq_ref, sq_ref, ck_ref, sk_ref = rest[:4]
    own = rest[4:8]
    rest = rest[8:]
    if relaid:
        come, rest = rest[: blocks - 1], rest[blocks - 1 + relaid :]
        finals, rest = rest[:4], rest[4:]
    else:
        finals, rest = rest[waits : waits + blocks], rest[waits + blocks :]
    own_pay, other_pay = rest
    scale = 1.0 / math.sqrt(HEAD)
    key_at = lax.broadcasted_iota(jnp.int32, (BLOCK, BLOCK), 0)
    query_at = lax.broadcasted_iota(jnp.int32, (BLOCK, BLOCK), 1)
    far_at = lax.broadcasted_iota(jnp.int32, (count, BLOCK), 0)
    far_query = lax.broadcasted_iota(jnp.int32, (count, BLOCK), 1)
    half = HEAD // 2
    for sub in range(per_step):
        head = first + pl.program_id(0) * per_step + sub
        lanes = slice(sub * HEAD, (sub + 1) * HEAD)
        held = jnp.concatenate([far_ref[:, lanes], other_ref[:, lanes]], axis=0)
        both = dot(pull_ref[...], held).astype(jnp.bfloat16)
        far_k, far_v = both[:count], both[count:]
        span = seg[head] * blocks
        at = phase[head]
        causal = (key_at <= query_at) & (key_at != at)
        behind = far_at * BLOCK + at - far_query
        p_far, d_far, q_all, g_all = [], [], [], []
        for k in range(blocks):
            if relaid:
                rows = slice(k * BLOCK, (k + 1) * BLOCK)
                source = [ref[:, lanes] for ref in own]
                if k:
                    source = [come[k - 1][t, :, lanes] for t in range(4)]
            else:
                rows = pl.ds(pl.multiple_of(info[k] * BLOCK, BLOCK), BLOCK)
                source = [ref[rows, lanes] for ref in own]
            block = info[blocks + k]
            low = block & (-span)
            cq, sq, ck, sk = cq_ref[rows, :], sq_ref[rows, :], ck_ref[rows, :], sk_ref[rows, :]
            raw_q, raw_k, value, grad = source
            raw_q = raw_q.astype(jnp.float32)
            raw_k = raw_k.astype(jnp.float32)
            tq = (raw_q * cq + pltpu.roll(raw_q, half, 1) * sq).astype(jnp.bfloat16)
            tk = (raw_k * ck + pltpu.roll(raw_k, half, 1) * sk).astype(jnp.bfloat16)
            keys = jnp.concatenate([tk, far_k], axis=0)
            vals = jnp.concatenate([value, far_v], axis=0)
            score = dot(keys, tq, NT)
            allowed = (far_at >= low) & (behind <= block * BLOCK)
            score = jnp.concatenate(
                [
                    jnp.where(causal, score[:BLOCK], -jnp.inf),
                    jnp.where(allowed, score[BLOCK:], -jnp.inf),
                ],
                axis=0,
            )
            top = jnp.max(score, axis=0, keepdims=True)
            weight = jnp.exp2((score - top) * (scale * LOG2E))
            prob = weight * (1.0 / jnp.sum(weight, axis=0, keepdims=True))
            p16 = prob.astype(jnp.bfloat16)
            dprob = dot(vals, grad, NT)
            delta = jnp.sum(p16.astype(jnp.float32) * dprob, axis=0, keepdims=True)
            d16 = (prob * (dprob - delta)).astype(jnp.bfloat16)
            out = dot(p16, vals, TN)
            dq = dot(d16, keys, TN) * scale
            dk = dot(d16[:BLOCK], tq) * scale
            dv = dot(p16[:BLOCK], grad)
            made = (
                out,
                dq * cq - pltpu.roll(dq, half, 1) * sq,
                dk * ck - pltpu.roll(dk, half, 1) * sk,
                dv,
            )
            for t in range(4):
                if relaid:
                    finals[t][info[2 * blocks + k], :, lanes] = made[t].astype(jnp.bfloat16)
                else:
                    finals[k][t, :, lanes] = made[t].astype(jnp.bfloat16)
            p_far.append(p16[BLOCK:])
            d_far.append(d16[BLOCK:])
            q_all.append(tq)
            g_all.append(grad)
        far_dk = dot(jnp.concatenate(d_far, axis=1), jnp.concatenate(q_all, axis=0)) * scale
        far_dv = dot(jnp.concatenate(p_far, axis=1), jnp.concatenate(g_all, axis=0))
        far_sum = jnp.concatenate([far_dk, far_dv], axis=0).astype(jnp.bfloat16)
        pay = dot(push_ref[...], far_sum).astype(jnp.bfloat16)
        own_pay[:, lanes] = pay[:count]
        other_pay[:, lanes] = pay[count:]


def pick_kernel(
    heads, blocks, phase, k_hbm, v_hbm, cos_ref, sin_ref, after, out_ref, k_ref, v_ref, row_ref,
    load, save
):
    moves = [
        pltpu.make_async_copy(k_hbm, k_ref, load.at[0]),
        pltpu.make_async_copy(v_hbm, v_ref, load.at[1]),
    ]
    for move in moves:
        move.start()
    for move in moves:
        move.wait()
    spot = lax.broadcasted_iota(jnp.int32, (16, HEAD), 0)
    for head in range(heads):
        at = phase[head]
        start = pl.multiple_of(at // 16 * 16, 16)
        lanes = slice(head * HEAD, (head + 1) * HEAD)
        both = []
        for ref in (k_ref, v_ref):
            rows = []
            for k in range(blocks):
                tile = ref[pl.ds(pl.multiple_of(k * BLOCK + start, 16), 16), lanes]
                tile = jnp.where(spot == at - start, tile.astype(jnp.float32), 0.0)
                rows.append(jnp.sum(tile, axis=0, keepdims=True))
            both.append(jnp.concatenate(rows, axis=0))
        key, value = both
        key = key * cos_ref[:, lanes] + pltpu.roll(key, HEAD // 2, 1) * sin_ref[:, lanes]
        row_ref[:, lanes] = jnp.concatenate([key, value], axis=0).astype(jnp.bfloat16)
    copies = [
        pltpu.make_async_copy(row_ref, out_ref.at[d], save.at[d]) for d in range(out_ref.shape[0])
    ]
    for copy in copies:
        copy.start()
    for copy in copies:
        copy.wait()


def pack_kernel(jobs, blocks, owner, after, *rest):
    number = len(jobs)
    inputs, rest = rest[:4], rest[4:]
    outs, rooms, (load, save) = rest[:number], rest[number : 2 * number], rest[2 * number :]
    order = [(job, t) for job in range(number) for t in range(4)]
    bal = lax.axis_index("bal")
    base = (lax.axis_index("ctx") * blocks + bal) * blocks
    partners = [(owner[base + i] // blocks) % blocks ^ bal for i in range(blocks)]
    picks = []
    for k, _, _ in jobs:
        pick = jnp.int32(0)
        for i in range(1, blocks):
            pick = jnp.where(partners[i] == k, jnp.int32(i), pick)
        picks.append(pick)

    def fetch(job, t):
        _, start, width = jobs[job]
        rows = pl.ds(pl.multiple_of(picks[job] * BLOCK, BLOCK), BLOCK)
        source = inputs[t].at[rows, pl.ds(start, width)]
        return pltpu.make_async_copy(source, rooms[job].at[t], load.at[job, t])

    def store(job, t):
        return pltpu.make_async_copy(rooms[job].at[t], outs[job].at[t], save.at[job, t])

    for job, t in order:
        fetch(job, t).start()
    for job, t in order:
        fetch(job, t).wait()
        store(job, t).start()
    for job, t in order:
        store(job, t).wait()


def link_kernel(*refs):
    pass


def add_kernel(left, right, after, out):
    out[...] = (left[...].astype(jnp.float32) + right[...].astype(jnp.float32)).astype(out.dtype)


def place_kernel(items, slot, *rest):
    number = len(items)
    parts = rest[:number]
    finals = rest[number + 4 : number + 8]
    rooms, (load, save) = rest[number + 8 : 2 * number + 8], rest[2 * number + 8 :]

    def save_of(i, t):
        k, start, width = items[i]
        top = pl.multiple_of(slot[k] * BLOCK, BLOCK)
        where = finals[t].at[pl.ds(top, BLOCK), pl.ds(start, width)]
        return pltpu.make_async_copy(rooms[i].at[t], where, save.at[i, t])

    loads = [pltpu.make_async_copy(parts[i], rooms[i], load.at[i]) for i in range(number)]
    for move in loads:
        move.start()
    for i in range(number):
        loads[i].wait()
        for t in range(4):
            save_of(i, t).start()
    for i in range(number):
        for t in range(4):
            save_of(i, t).wait()


def far_rows(got, cos_ref, sin_ref, blocks):
    total = got[0].astype(jnp.float32)
    for sender in range(1, got.shape[0]):
        total = total + got[sender].astype(jnp.float32)
    far_k, far_v = total[:blocks], total[blocks:]
    heads = far_k.shape[1] // HEAD
    turned = []
    for head in range(heads):
        lanes = slice(head * HEAD, (head + 1) * HEAD)
        one = far_k[:, lanes]
        turned.append(
            one * cos_ref[:, lanes] - pltpu.roll(one, HEAD // 2, 1) * sin_ref[:, lanes]
        )
    values = [far_v[:, head * HEAD : (head + 1) * HEAD] for head in range(heads)]
    return turned, values


def overwrite(ref, lanes, at, source, pick):
    spot = lax.broadcasted_iota(jnp.int32, (16, HEAD), 0)
    line = lax.broadcasted_iota(jnp.int32, source.shape, 0)
    start = pl.multiple_of(at // 16 * 16, 16)
    row = jnp.sum(jnp.where(line == pick, source, 0.0), axis=0, keepdims=True)
    old = ref[pl.ds(start, 16), lanes].astype(jnp.float32)
    ref[pl.ds(start, 16), lanes] = jnp.where(spot == at - start, row, old).astype(jnp.bfloat16)


def patch_kernel(
    heads, blocks, late, edge, phase, slot, got_hbm, cos_ref, sin_ref, dk_in, dv_in, dk, dv, got,
    room, get, load, save
):
    outs = (dk, dv)
    width = room.shape[-1]
    order = [(k, t) for k in range(blocks) for t in range(2)]

    def span(k):
        return pl.ds(0, edge if k in late else width)

    def here(t, k):
        rows = pl.ds(pl.multiple_of(slot[k] * BLOCK, BLOCK), BLOCK)
        return outs[t].at[rows, span(k)]

    def fetch(t, k):
        return pltpu.make_async_copy(here(t, k), room.at[t, k, :, span(k)], load.at[t, k])

    def store(t, k):
        return pltpu.make_async_copy(room.at[t, k, :, span(k)], here(t, k), save.at[t, k])

    first = pltpu.make_async_copy(got_hbm, got, get)
    first.start()
    for k, t in order:
        fetch(t, k).start()
    first.wait()
    fresh = far_rows(got, cos_ref, sin_ref, blocks)
    for k, t in order:
        fetch(t, k).wait()
        for head in range(edge // HEAD if k in late else heads):
            lanes = slice(head * HEAD, (head + 1) * HEAD)
            overwrite(room.at[t, k], lanes, phase[head], fresh[t][head], slot[k])
        store(t, k).start()
    for k, t in order:
        store(t, k).wait()


def last_kernel(heads, late, edge, phase, slot, got_hbm, cos_ref, sin_ref, *rest):
    pieces = rest[:2]
    outs = rest[6:10]
    got, room, get, load, save = rest[10:]
    blocks = got.shape[1] // 2
    right = pl.ds(edge, room.shape[-1])
    rows = pl.ds(pl.multiple_of(slot[late] * BLOCK, BLOCK), BLOCK)
    first = pltpu.make_async_copy(got_hbm.at[:, :, right], got, get)
    loads, start = [], 0
    for i, piece in enumerate(pieces):
        part = pl.ds(start, piece.shape[-1])
        loads.append(pltpu.make_async_copy(piece, room.at[:, :, part], load.at[i]))
        start += piece.shape[-1]
    stores = [
        pltpu.make_async_copy(room.at[t], outs[t].at[rows, right], save.at[t]) for t in range(4)
    ]
    for move in loads + [first]:
        move.start()
    for move in loads:
        move.wait()
    for t in range(2):
        stores[t].start()
    first.wait()
    fresh = far_rows(got, cos_ref, sin_ref, blocks)
    for t in range(2):
        for head in range(edge // HEAD, heads):
            local_head = head - edge // HEAD
            lanes = slice(local_head * HEAD, (local_head + 1) * HEAD)
            overwrite(room.at[2 + t], lanes, phase[head], fresh[t][local_head], slot[late])
        stores[2 + t].start()
    for store in stores:
        store.wait()


def local(queries, keys, values, output_gradient, dilation_phase, segment_device_count, owner):
    rows, width = queries.shape
    heads = width // HEAD
    blocks = rows // BLOCK
    bal_size = lax.axis_size("bal")
    devices = lax.axis_size("ctx") * bal_size
    total = rows * devices
    count = owner.shape[0]
    assert blocks == bal_size == 4 and bal_size & (bal_size - 1) == 0
    bal = lax.axis_index("bal")
    device = lax.axis_index("ctx") * bal_size + bal
    room = 66_900_000
    big = pltpu.CompilerParams(vmem_limit_bytes=room)
    smem = pl.BlockSpec(memory_space=pltpu.SMEM)
    vmem = pl.BlockSpec(memory_space=pltpu.VMEM)
    anywhere = pl.BlockSpec(memory_space=pl.ANY)
    light = pl.CostEstimate(flops=2_000_000_000, bytes_accessed=5_000_000, transcendentals=0)
    heavy = pl.CostEstimate(flops=20_000_000_000, bytes_accessed=60_000_000, transcendentals=0)

    def tokens_of(ids):
        return (ids[:, None] * BLOCK + jnp.arange(BLOCK, dtype=jnp.int32)[None, :]).reshape(rows)

    def swap(array, k):
        return lax.ppermute(array, "bal", [(i, i ^ k) for i in range(bal_size)])

    steps = jnp.arange(blocks, dtype=jnp.int32)
    held = device * blocks + steps
    goes_to = lax.dynamic_slice_in_dim(owner, device * blocks, blocks) // blocks % bal_size
    partner = steps ^ bal
    which = jnp.sum(jnp.where(goes_to[None, :] == partner[:, None], steps[None, :], 0), axis=1)
    info = jnp.concatenate([which, device * blocks + which]).astype(jnp.int32)
    comes_from = jnp.sum(
        jnp.where(
            owner[None, :] == held[:, None], jnp.arange(count, dtype=jnp.int32)[None, :], 0
        ),
        axis=1,
    )

    first = heads * 3 // 10 * 2
    early = first // 4 * 2
    middle = heads - 2
    cut, edge, brim = early * HEAD, first * HEAD, middle * HEAD
    originals = (queries, keys, values, output_gradient)

    def send_inputs(jobs, after):
        sizes = [(4, BLOCK, width) for _, _, width in jobs]
        sent = pl.pallas_call(
            functools.partial(pack_kernel, jobs, blocks),
            in_specs=[smem] + [anywhere] * 5,
            out_specs=[anywhere] * len(jobs),
            out_shape=[jax.ShapeDtypeStruct(size, jnp.bfloat16) for size in sizes],
            scratch_shapes=[pltpu.VMEM(size, jnp.bfloat16) for size in sizes]
            + [pltpu.SemaphoreType.DMA((len(jobs), 4))] * 2,
            compiler_params=big,
        )(owner, after, *originals)
        return sent, [swap(one, job[0]) for one, job in zip(sent, jobs)]

    sent, come_early = send_inputs([(2, 0, cut)], queries)

    cq, sq, ck, sk = tables(tokens_of(held), total)
    own_phase = (held[:, None] * BLOCK + dilation_phase[None, :]).astype(jnp.int32)
    pick_cos, pick_sin = flat_tables(own_phase, total)
    own_far = pl.pallas_call(
        functools.partial(pick_kernel, heads, blocks),
        in_specs=[smem, anywhere, anywhere, vmem, vmem, anywhere],
        out_specs=anywhere,
        out_shape=jax.ShapeDtypeStruct((devices // 2, 2 * blocks, width), jnp.bfloat16),
        scratch_shapes=[
            pltpu.VMEM((rows, width), jnp.bfloat16),
            pltpu.VMEM((rows, width), jnp.bfloat16),
            pltpu.VMEM((2 * blocks, width), jnp.bfloat16),
            pltpu.SemaphoreType.DMA((2,)),
            pltpu.SemaphoreType.DMA((devices // 2,)),
        ],
        compiler_params=big,
    )(
        dilation_phase,
        keys,
        values,
        pick_cos,
        pick_sin,
        sent[0],
    )
    halves = [list(range(0, devices, 2)), list(range(1, devices, 2))]
    near_far = lax.all_to_all(
        own_far,
        ("ctx", "bal"),
        split_axis=0,
        concat_axis=0,
        tiled=True,
        axis_index_groups=halves,
    ).reshape(count, width)
    other_far = swap(near_far, 1)
    jobs = [(2, cut, edge - cut), (3, 0, edge), (1, 0, edge)]
    _, (come_rest, come_3, come_1) = send_inputs(jobs, own_far)
    come_2 = come_early[0]

    ids = (device ^ steps) * blocks
    came = jnp.sum(
        jnp.where(comes_from[None, :] // blocks * blocks == ids[:, None], comes_from[None, :], 0),
        axis=1,
    )
    moved = jnp.concatenate([which, came, partner]).astype(jnp.int32)
    moved_tables = tables(tokens_of(came), total)

    side = 2 * count
    wide = jnp.arange(side, dtype=jnp.int32)
    tall = wide[:, None]
    wide = wide[None, :]
    source = tall % count
    holder = source // blocks
    held_row = (holder ^ device) % 2 * count + holder // 2 * (2 * blocks)
    pull = (wide == held_row + tall // count * blocks + source % blocks).astype(jnp.bfloat16)
    lands = owner // blocks
    lands = (lands ^ device) % 2 * count + lands // 2 * (2 * blocks) + owner % blocks
    push = (jnp.concatenate([lands, lands + blocks])[None, :] == tall).astype(jnp.bfloat16)

    per_step = 2
    columns = per_step * HEAD
    fixed = lambda h, *_: (0, 0)
    square = pl.BlockSpec((side, side), fixed)
    table = pl.BlockSpec((rows, HEAD), fixed)
    part = pl.BlockSpec((4, BLOCK, columns), lambda h, *_: (0, 0, h))
    def attend_held(begin, end, waits, carried):
        skip = begin // per_step
        tensor = pl.BlockSpec((rows, columns), lambda h, *_: (0, h + skip))
        far = pl.BlockSpec((count, columns), lambda h, *_: (0, h + skip))
        extra = carried + waits
        results = pl.pallas_call(
            functools.partial(attend_kernel, per_step, blocks, count, begin, 0, len(extra)),
            grid_spec=pltpu.PrefetchScalarGridSpec(
                num_scalar_prefetch=3,
                grid=((end - begin) // per_step,),
                in_specs=[far, far, square, square]
                + [table] * 4
                + [tensor] * 4
                + [anywhere] * len(extra),
                out_specs=[part] * blocks + [far] * 2,
            ),
            out_shape=[jax.ShapeDtypeStruct((4, BLOCK, (end - begin) * HEAD), jnp.bfloat16)]
            * blocks
            + [jax.ShapeDtypeStruct((count, width), jnp.bfloat16)] * 2,
            input_output_aliases={15 + i: blocks + i for i in range(len(carried))},
            compiler_params=big,
            cost_estimate=heavy,
        )(
            info,
            dilation_phase,
            segment_device_count,
            near_far,
            other_far,
            pull,
            push,
            cq,
            sq,
            ck,
            sk,
            *originals,
            *extra,
        )
        return list(results[:blocks]), list(results[blocks:])

    waits = list(moved_tables) + [come_1, come_2]
    parts, payload = attend_held(first, middle, waits, [])
    parts_last, payload = attend_held(middle, heads, [], payload)
    for k in range(1, blocks):
        parts[k] = swap(parts[k], k)
        parts_last[k] = swap(parts_last[k], k)

    shapes = [jax.ShapeDtypeStruct((blocks, BLOCK, width), jnp.bfloat16)] * 4
    shapes = shapes + [jax.ShapeDtypeStruct((count, width), jnp.bfloat16)] * 2

    def attend_relaid(begin, end, come, carried):
        skip = begin // per_step
        tensor = pl.BlockSpec((BLOCK, columns), lambda h, info, *_: (info[0], h + skip))
        far = pl.BlockSpec((count, columns), lambda h, *_: (0, h + skip))
        whole = pl.BlockSpec((blocks, BLOCK, columns), lambda h, *_: (0, 0, h + skip))
        shifted = pl.BlockSpec((4, BLOCK, columns), lambda h, *_: (0, 0, h + skip))
        operands = 3 + 4 + 4 + 4 + blocks - 1
        return pl.pallas_call(
            functools.partial(attend_kernel, per_step, blocks, count, begin, len(carried), 0),
            grid_spec=pltpu.PrefetchScalarGridSpec(
                num_scalar_prefetch=3,
                grid=((end - begin) // per_step,),
                in_specs=[far, far, square, square]
                + [table] * 4
                + [tensor] * 4
                + [shifted, part, shifted]
                + [anywhere] * len(carried),
                out_specs=[whole] * 4 + [far] * 2,
                ),
            out_shape=shapes,
            input_output_aliases={
                operands + i: 6 - len(carried) + i for i in range(len(carried))
            },
            compiler_params=big,
            cost_estimate=light,
        )(
            moved,
            dilation_phase,
            segment_device_count,
            near_far,
            other_far,
            pull,
            push,
            *moved_tables,
            *originals,
            *come,
            *carried,
        )

    results = attend_relaid(0, early, [come_1, come_2, come_3], payload)
    results = attend_relaid(early, first, [come_1, come_rest, come_3], results)
    finals = [one.reshape(rows, width) for one in results[:4]]

    def after(array, wait):
        return pl.pallas_call(
            link_kernel,
            in_specs=[anywhere] * 2,
            out_specs=anywhere,
            out_shape=jax.ShapeDtypeStruct(array.shape, array.dtype),
            input_output_aliases={0: 0},
            compiler_params=pltpu.CompilerParams(vmem_limit_bytes=room, has_side_effects=True),
        )(array, wait)

    crossing = swap(after(results[5], parts[2]), 1)
    slab = pl.BlockSpec((count // 4, width), lambda i: (i, 0))
    payload = pl.pallas_call(
        add_kernel,
        grid=(4,),
        in_specs=[slab, slab, anywhere],
        out_specs=slab,
        out_shape=jax.ShapeDtypeStruct((count, width), jnp.bfloat16),
        compiler_params=big,
        cost_estimate=light,
    )(results[4], crossing, parts_last[2])
    got = lax.all_to_all(
        payload.reshape(devices // 2, 2 * blocks, width),
        ("ctx", "bal"),
        split_axis=0,
        concat_axis=0,
        tiled=True,
        axis_index_groups=halves,
    )

    new_phase = (comes_from[:, None] * BLOCK + dilation_phase[None, :]).astype(jnp.int32)
    new_cos, new_sin = flat_tables(new_phase, total)
    out = jax.ShapeDtypeStruct((rows, width), jnp.bfloat16)
    slots = partner.astype(jnp.int32)
    items = [(k, edge, brim - edge) for k in range(3)]
    items += [(k, brim, width - brim) for k in range(3)]
    number = len(items)
    finals = pl.pallas_call(
        functools.partial(place_kernel, items),
        in_specs=[smem] + [anywhere] * (number + 4),
        out_specs=[anywhere] * 4,
        out_shape=[out] * 4,
        input_output_aliases={1 + number + t: t for t in range(4)},
        scratch_shapes=[pltpu.VMEM((4, BLOCK, item[2]), jnp.bfloat16) for item in items]
        + [pltpu.SemaphoreType.DMA((number,)), pltpu.SemaphoreType.DMA((number, 4))],
        compiler_params=big,
        cost_estimate=light,
    )(slots, *parts[:3], *parts_last[:3], *finals)
    late = 3
    patched = pl.pallas_call(
        functools.partial(patch_kernel, heads, blocks, (late,), edge),
        in_specs=[smem, smem, anywhere, vmem, vmem, anywhere, anywhere],
        out_specs=[anywhere] * 2,
        out_shape=[out] * 2,
        input_output_aliases={5: 0, 6: 1},
        scratch_shapes=[
            pltpu.VMEM((devices // 2, 2 * blocks, width), jnp.bfloat16),
            pltpu.VMEM((2, blocks, BLOCK, width), jnp.bfloat16),
            pltpu.SemaphoreType.DMA(()),
            pltpu.SemaphoreType.DMA((2, blocks)),
            pltpu.SemaphoreType.DMA((2, blocks)),
        ],
        compiler_params=big,
        cost_estimate=light,
    )(dilation_phase, slots, got, new_cos, new_sin, finals[2], finals[3])
    return tuple(
        pl.pallas_call(
            functools.partial(last_kernel, heads, late, edge),
            in_specs=[smem, smem, anywhere, vmem, vmem] + [anywhere] * 6,
            out_specs=[anywhere] * 4,
            out_shape=[out] * 4,
            input_output_aliases={7 + t: t for t in range(4)},
            scratch_shapes=[
                pltpu.VMEM((devices // 2, 2 * blocks, width - edge), jnp.bfloat16),
                pltpu.VMEM((4, BLOCK, width - edge), jnp.bfloat16),
                pltpu.SemaphoreType.DMA(()),
                pltpu.SemaphoreType.DMA((2,)),
                pltpu.SemaphoreType.DMA((4,)),
            ],
            compiler_params=big,
        )(
            dilation_phase,
            slots,
            got,
            new_cos[:, edge:],
            new_sin[:, edge:],
            parts[late],
            parts_last[late],
            finals[0],
            finals[1],
            *patched,
        )
    )


def solution(mesh):
    token = P(("groups", "ctx", "bal"), "head")
    return jax.shard_map(
        local,
        mesh=mesh,
        in_specs=(token, token, token, token, P("head"), P("head"), P("groups")),
        out_specs=(token, token, token, token),
        check_vma=False,
    )
```

```python
import functools
import math

import jax
import jax.numpy as jnp
from jax import lax
from jax.experimental import pallas as pl
from jax.experimental.pallas import tpu as pltpu
from jax.sharding import PartitionSpec as P

BLOCK = 128
HEAD = 128
LOG2E = 1.4426950408889634
NT = (((1,), (1,)), ((), ()))
TN = (((0,), (0,)), ((), ()))


def tables(positions, total):
    half = HEAD // 2
    pair = jnp.arange(half, dtype=jnp.float32)
    inverse = jnp.exp(pair * (-2.0 * math.log(10000.0) / HEAD))
    where = positions.astype(jnp.float32)[..., None]
    angles = where * inverse
    base = (2.0 * pair / HEAD + 0.4) / 1.4
    growth = jnp.exp((2.0 * where - total) / total * jnp.log(base))
    cosine, sine = jnp.cos(angles), jnp.sin(angles)

    def pack(scale):
        first, second = cosine * scale, sine * scale
        return (
            jnp.concatenate([first, first], axis=-1),
            jnp.concatenate([-second, second], axis=-1),
        )

    return pack(growth) + pack(1.0 / growth)


def flat_tables(positions, total):
    half = HEAD // 2
    lane = jnp.arange(positions.shape[1] * HEAD, dtype=jnp.int32) % HEAD
    pair = (lane % half).astype(jnp.float32)
    inverse = jnp.exp(pair * (-2.0 * math.log(10000.0) / HEAD))
    where = jnp.repeat(positions.astype(jnp.float32), HEAD, axis=1)
    angles = where * inverse[None, :]
    base = (2.0 * pair / HEAD + 0.4) / 1.4
    growth = jnp.exp((2.0 * where - total) / total * jnp.log(base)[None, :])
    sine = jnp.where(lane[None, :] < half, -jnp.sin(angles), jnp.sin(angles))
    return jnp.cos(angles) / growth, sine / growth


def dot(left, right, dims=None):
    if dims is None:
        dims = (((1,), (0,)), ((), ()))
    return lax.dot_general(left, right, dims, preferred_element_type=jnp.float32)


def attend_kernel(
    per_step, blocks, count, first, relaid, waits, info, phase, seg, far_ref, other_ref, pull_ref, push_ref, *rest
):
    cq_ref, sq_ref, ck_ref, sk_ref = rest[:4]
    own = rest[4:8]
    rest = rest[8:]
    if relaid:
        come, rest = rest[: blocks - 1], rest[blocks - 1 + relaid :]
        finals, rest = rest[:4], rest[4:]
    else:
        finals, rest = rest[waits : waits + blocks], rest[waits + blocks :]
    own_pay, other_pay = rest
    scale = 1.0 / math.sqrt(HEAD)
    key_at = lax.broadcasted_iota(jnp.int32, (BLOCK, BLOCK), 0)
    query_at = lax.broadcasted_iota(jnp.int32, (BLOCK, BLOCK), 1)
    far_at = lax.broadcasted_iota(jnp.int32, (count, BLOCK), 0)
    far_query = lax.broadcasted_iota(jnp.int32, (count, BLOCK), 1)
    half = HEAD // 2
    for sub in range(per_step):
        head = first + pl.program_id(0) * per_step + sub
        lanes = slice(sub * HEAD, (sub + 1) * HEAD)
        held = jnp.concatenate([far_ref[:, lanes], other_ref[:, lanes]], axis=0)
        both = dot(pull_ref[...], held).astype(jnp.bfloat16)
        far_k, far_v = both[:count], both[count:]
        span = seg[head] * blocks
        at = phase[head]
        causal = (key_at <= query_at) & (key_at != at)
        behind = far_at * BLOCK + at - far_query
        p_far, d_far, q_all, g_all = [], [], [], []
        for k in range(blocks):
            if relaid:
                rows = slice(k * BLOCK, (k + 1) * BLOCK)
                source = [ref[:, lanes] for ref in own]
                if k:
                    source = [come[k - 1][t, :, lanes] for t in range(4)]
            else:
                rows = pl.ds(pl.multiple_of(info[k] * BLOCK, BLOCK), BLOCK)
                source = [ref[rows, lanes] for ref in own]
            block = info[blocks + k]
            low = block & (-span)
            cq, sq, ck, sk = cq_ref[rows, :], sq_ref[rows, :], ck_ref[rows, :], sk_ref[rows, :]
            raw_q, raw_k, value, grad = source
            raw_q = raw_q.astype(jnp.float32)
            raw_k = raw_k.astype(jnp.float32)
            tq = (raw_q * cq + pltpu.roll(raw_q, half, 1) * sq).astype(jnp.bfloat16)
            tk = (raw_k * ck + pltpu.roll(raw_k, half, 1) * sk).astype(jnp.bfloat16)
            keys = jnp.concatenate([tk, far_k], axis=0)
            vals = jnp.concatenate([value, far_v], axis=0)
            score = dot(keys, tq, NT)
            allowed = (far_at >= low) & (behind <= block * BLOCK)
            score = jnp.concatenate(
                [
                    jnp.where(causal, score[:BLOCK], -jnp.inf),
                    jnp.where(allowed, score[BLOCK:], -jnp.inf),
                ],
                axis=0,
            )
            top = jnp.max(score, axis=0, keepdims=True)
            weight = jnp.exp2((score - top) * (scale * LOG2E))
            prob = weight * (1.0 / jnp.sum(weight, axis=0, keepdims=True))
            p16 = prob.astype(jnp.bfloat16)
            dprob = dot(vals, grad, NT)
            delta = jnp.sum(p16.astype(jnp.float32) * dprob, axis=0, keepdims=True)
            d16 = (prob * (dprob - delta)).astype(jnp.bfloat16)
            out = dot(p16, vals, TN)
            dq = dot(d16, keys, TN) * scale
            dk = dot(d16[:BLOCK], tq) * scale
            dv = dot(p16[:BLOCK], grad)
            made = (
                out,
                dq * cq - pltpu.roll(dq, half, 1) * sq,
                dk * ck - pltpu.roll(dk, half, 1) * sk,
                dv,
            )
            for t in range(4):
                if relaid:
                    finals[t][info[2 * blocks + k], :, lanes] = made[t].astype(jnp.bfloat16)
                else:
                    finals[k][t, :, lanes] = made[t].astype(jnp.bfloat16)
            p_far.append(p16[BLOCK:])
            d_far.append(d16[BLOCK:])
            q_all.append(tq)
            g_all.append(grad)
        far_dk = dot(jnp.concatenate(d_far, axis=1), jnp.concatenate(q_all, axis=0)) * scale
        far_dv = dot(jnp.concatenate(p_far, axis=1), jnp.concatenate(g_all, axis=0))
        far_sum = jnp.concatenate([far_dk, far_dv], axis=0).astype(jnp.bfloat16)
        pay = dot(push_ref[...], far_sum).astype(jnp.bfloat16)
        own_pay[:, lanes] = pay[:count]
        other_pay[:, lanes] = pay[count:]


def pick_kernel(
    heads, blocks, phase, k_hbm, v_hbm, cos_ref, sin_ref, after, out_ref, k_ref, v_ref, row_ref,
    load, save
):
    moves = [
        pltpu.make_async_copy(k_hbm, k_ref, load.at[0]),
        pltpu.make_async_copy(v_hbm, v_ref, load.at[1]),
    ]
    for move in moves:
        move.start()
    for move in moves:
        move.wait()
    spot = lax.broadcasted_iota(jnp.int32, (16, HEAD), 0)
    for head in range(heads):
        at = phase[head]
        start = pl.multiple_of(at // 16 * 16, 16)
        lanes = slice(head * HEAD, (head + 1) * HEAD)
        both = []
        for ref in (k_ref, v_ref):
            rows = []
            for k in range(blocks):
                tile = ref[pl.ds(pl.multiple_of(k * BLOCK + start, 16), 16), lanes]
                tile = jnp.where(spot == at - start, tile.astype(jnp.float32), 0.0)
                rows.append(jnp.sum(tile, axis=0, keepdims=True))
            both.append(jnp.concatenate(rows, axis=0))
        key, value = both
        key = key * cos_ref[:, lanes] + pltpu.roll(key, HEAD // 2, 1) * sin_ref[:, lanes]
        row_ref[:, lanes] = jnp.concatenate([key, value], axis=0).astype(jnp.bfloat16)
    copies = [
        pltpu.make_async_copy(row_ref, out_ref.at[d], save.at[d]) for d in range(out_ref.shape[0])
    ]
    for copy in copies:
        copy.start()
    for copy in copies:
        copy.wait()


def pack_kernel(jobs, blocks, owner, after, *rest):
    number = len(jobs)
    inputs, rest = rest[:4], rest[4:]
    outs, rooms, (load, save) = rest[:number], rest[number : 2 * number], rest[2 * number :]
    order = [(job, t) for job in range(number) for t in range(4)]
    bal = lax.axis_index("bal")
    base = (lax.axis_index("ctx") * blocks + bal) * blocks
    partners = [(owner[base + i] // blocks) % blocks ^ bal for i in range(blocks)]
    picks = []
    for k, _, _ in jobs:
        pick = jnp.int32(0)
        for i in range(1, blocks):
            pick = jnp.where(partners[i] == k, jnp.int32(i), pick)
        picks.append(pick)

    def fetch(job, t):
        _, start, width = jobs[job]
        rows = pl.ds(pl.multiple_of(picks[job] * BLOCK, BLOCK), BLOCK)
        source = inputs[t].at[rows, pl.ds(start, width)]
        return pltpu.make_async_copy(source, rooms[job].at[t], load.at[job, t])

    def store(job, t):
        return pltpu.make_async_copy(rooms[job].at[t], outs[job].at[t], save.at[job, t])

    for job, t in order:
        fetch(job, t).start()
    for job, t in order:
        fetch(job, t).wait()
        store(job, t).start()
    for job, t in order:
        store(job, t).wait()


def link_kernel(*refs):
    pass


def place_kernel(items, slot, *rest):
    number = len(items)
    parts = rest[:number]
    finals = rest[number + 4 : number + 8]
    rooms, (load, save) = rest[number + 8 : 2 * number + 8], rest[2 * number + 8 :]

    def save_of(i, t):
        k, start, width = items[i]
        top = pl.multiple_of(slot[k] * BLOCK, BLOCK)
        where = finals[t].at[pl.ds(top, BLOCK), pl.ds(start, width)]
        return pltpu.make_async_copy(rooms[i].at[t], where, save.at[i, t])

    loads = [pltpu.make_async_copy(parts[i], rooms[i], load.at[i]) for i in range(number)]
    for move in loads:
        move.start()
    for i in range(number):
        loads[i].wait()
        for t in range(4):
            save_of(i, t).start()
    for i in range(number):
        for t in range(4):
            save_of(i, t).wait()


def far_rows(got, cos_ref, sin_ref, blocks):
    total = got[0].astype(jnp.float32)
    for sender in range(1, got.shape[0]):
        total = total + got[sender].astype(jnp.float32)
    far_k, far_v = total[:blocks], total[blocks:]
    heads = far_k.shape[1] // HEAD
    turned = []
    for head in range(heads):
        lanes = slice(head * HEAD, (head + 1) * HEAD)
        one = far_k[:, lanes]
        turned.append(
            one * cos_ref[:, lanes] - pltpu.roll(one, HEAD // 2, 1) * sin_ref[:, lanes]
        )
    values = [far_v[:, head * HEAD : (head + 1) * HEAD] for head in range(heads)]
    return turned, values


def overwrite(ref, lanes, at, source, pick):
    spot = lax.broadcasted_iota(jnp.int32, (16, HEAD), 0)
    line = lax.broadcasted_iota(jnp.int32, source.shape, 0)
    start = pl.multiple_of(at // 16 * 16, 16)
    row = jnp.sum(jnp.where(line == pick, source, 0.0), axis=0, keepdims=True)
    old = ref[pl.ds(start, 16), lanes].astype(jnp.float32)
    ref[pl.ds(start, 16), lanes] = jnp.where(spot == at - start, row, old).astype(jnp.bfloat16)


def patch_kernel(
    heads, blocks, late, edge, phase, slot, got_hbm, cos_ref, sin_ref, dk_in, dv_in, dk, dv, got,
    room, get, load, save
):
    outs = (dk, dv)
    width = room.shape[-1]
    order = [(k, t) for k in range(blocks) for t in range(2)]

    def span(k):
        return pl.ds(0, edge if k in late else width)

    def here(t, k):
        rows = pl.ds(pl.multiple_of(slot[k] * BLOCK, BLOCK), BLOCK)
        return outs[t].at[rows, span(k)]

    def fetch(t, k):
        return pltpu.make_async_copy(here(t, k), room.at[t, k, :, span(k)], load.at[t, k])

    def store(t, k):
        return pltpu.make_async_copy(room.at[t, k, :, span(k)], here(t, k), save.at[t, k])

    first = pltpu.make_async_copy(got_hbm, got, get)
    first.start()
    for k, t in order:
        fetch(t, k).start()
    first.wait()
    fresh = far_rows(got, cos_ref, sin_ref, blocks)
    for k, t in order:
        fetch(t, k).wait()
        for head in range(edge // HEAD if k in late else heads):
            lanes = slice(head * HEAD, (head + 1) * HEAD)
            overwrite(room.at[t, k], lanes, phase[head], fresh[t][head], slot[k])
        store(t, k).start()
    for k, t in order:
        store(t, k).wait()


def last_kernel(heads, late, edge, phase, slot, got_hbm, cos_ref, sin_ref, *rest):
    pieces = rest[:2]
    outs = rest[6:10]
    got, room, get, load, save = rest[10:]
    blocks = got.shape[1] // 2
    right = pl.ds(edge, room.shape[-1])
    rows = pl.ds(pl.multiple_of(slot[late] * BLOCK, BLOCK), BLOCK)
    first = pltpu.make_async_copy(got_hbm.at[:, :, right], got, get)
    loads, start = [], 0
    for i, piece in enumerate(pieces):
        part = pl.ds(start, piece.shape[-1])
        loads.append(pltpu.make_async_copy(piece, room.at[:, :, part], load.at[i]))
        start += piece.shape[-1]
    stores = [
        pltpu.make_async_copy(room.at[t], outs[t].at[rows, right], save.at[t]) for t in range(4)
    ]
    for move in loads + [first]:
        move.start()
    for move in loads:
        move.wait()
    for t in range(2):
        stores[t].start()
    first.wait()
    fresh = far_rows(got, cos_ref, sin_ref, blocks)
    for t in range(2):
        for head in range(edge // HEAD, heads):
            local_head = head - edge // HEAD
            lanes = slice(local_head * HEAD, (local_head + 1) * HEAD)
            overwrite(room.at[2 + t], lanes, phase[head], fresh[t][local_head], slot[late])
        stores[2 + t].start()
    for store in stores:
        store.wait()


def local(queries, keys, values, output_gradient, dilation_phase, segment_device_count, owner):
    rows, width = queries.shape
    heads = width // HEAD
    blocks = rows // BLOCK
    bal_size = lax.axis_size("bal")
    devices = lax.axis_size("ctx") * bal_size
    total = rows * devices
    count = owner.shape[0]
    assert blocks == bal_size == 4 and bal_size & (bal_size - 1) == 0
    bal = lax.axis_index("bal")
    device = lax.axis_index("ctx") * bal_size + bal
    room = 66_900_000
    big = pltpu.CompilerParams(vmem_limit_bytes=room)
    smem = pl.BlockSpec(memory_space=pltpu.SMEM)
    vmem = pl.BlockSpec(memory_space=pltpu.VMEM)
    anywhere = pl.BlockSpec(memory_space=pl.ANY)
    light = pl.CostEstimate(flops=2_000_000_000, bytes_accessed=5_000_000, transcendentals=0)
    heavy = pl.CostEstimate(flops=20_000_000_000, bytes_accessed=60_000_000, transcendentals=0)

    def tokens_of(ids):
        return (ids[:, None] * BLOCK + jnp.arange(BLOCK, dtype=jnp.int32)[None, :]).reshape(rows)

    def swap(array, k):
        return lax.ppermute(array, "bal", [(i, i ^ k) for i in range(bal_size)])

    steps = jnp.arange(blocks, dtype=jnp.int32)
    held = device * blocks + steps
    goes_to = lax.dynamic_slice_in_dim(owner, device * blocks, blocks) // blocks % bal_size
    partner = steps ^ bal
    which = jnp.sum(jnp.where(goes_to[None, :] == partner[:, None], steps[None, :], 0), axis=1)
    info = jnp.concatenate([which, device * blocks + which]).astype(jnp.int32)
    comes_from = jnp.sum(
        jnp.where(
            owner[None, :] == held[:, None], jnp.arange(count, dtype=jnp.int32)[None, :], 0
        ),
        axis=1,
    )

    first = heads * 3 // 10 * 2
    early = first // 4 * 2
    middle = heads - 2
    cut, edge, brim = early * HEAD, first * HEAD, middle * HEAD
    originals = (queries, keys, values, output_gradient)

    def send_inputs(jobs, after):
        sizes = [(4, BLOCK, width) for _, _, width in jobs]
        sent = pl.pallas_call(
            functools.partial(pack_kernel, jobs, blocks),
            in_specs=[smem] + [anywhere] * 5,
            out_specs=[anywhere] * len(jobs),
            out_shape=[jax.ShapeDtypeStruct(size, jnp.bfloat16) for size in sizes],
            scratch_shapes=[pltpu.VMEM(size, jnp.bfloat16) for size in sizes]
            + [pltpu.SemaphoreType.DMA((len(jobs), 4))] * 2,
            compiler_params=big,
        )(owner, after, *originals)
        return sent, [swap(one, job[0]) for one, job in zip(sent, jobs)]

    sent, come_early = send_inputs([(2, 0, cut)], queries)

    cq, sq, ck, sk = tables(tokens_of(held), total)
    own_phase = (held[:, None] * BLOCK + dilation_phase[None, :]).astype(jnp.int32)
    pick_cos, pick_sin = flat_tables(own_phase, total)
    own_far = pl.pallas_call(
        functools.partial(pick_kernel, heads, blocks),
        in_specs=[smem, anywhere, anywhere, vmem, vmem, anywhere],
        out_specs=anywhere,
        out_shape=jax.ShapeDtypeStruct((devices // 2, 2 * blocks, width), jnp.bfloat16),
        scratch_shapes=[
            pltpu.VMEM((rows, width), jnp.bfloat16),
            pltpu.VMEM((rows, width), jnp.bfloat16),
            pltpu.VMEM((2 * blocks, width), jnp.bfloat16),
            pltpu.SemaphoreType.DMA((2,)),
            pltpu.SemaphoreType.DMA((devices // 2,)),
        ],
        compiler_params=big,
    )(
        dilation_phase,
        keys,
        values,
        pick_cos,
        pick_sin,
        sent[0],
    )
    halves = [list(range(0, devices, 2)), list(range(1, devices, 2))]
    near_far = lax.all_to_all(
        own_far,
        ("ctx", "bal"),
        split_axis=0,
        concat_axis=0,
        tiled=True,
        axis_index_groups=halves,
    ).reshape(count, width)
    other_far = swap(near_far, 1)
    jobs = [(2, cut, edge - cut), (3, 0, edge), (1, 0, edge)]
    _, (come_rest, come_3, come_1) = send_inputs(jobs, own_far)
    come_2 = come_early[0]

    ids = (device ^ steps) * blocks
    came = jnp.sum(
        jnp.where(comes_from[None, :] // blocks * blocks == ids[:, None], comes_from[None, :], 0),
        axis=1,
    )
    moved = jnp.concatenate([which, came, partner]).astype(jnp.int32)
    moved_tables = tables(tokens_of(came), total)

    side = 2 * count
    wide = jnp.arange(side, dtype=jnp.int32)
    tall = wide[:, None]
    wide = wide[None, :]
    source = tall % count
    holder = source // blocks
    held_row = (holder ^ device) % 2 * count + holder // 2 * (2 * blocks)
    pull = (wide == held_row + tall // count * blocks + source % blocks).astype(jnp.bfloat16)
    lands = owner // blocks
    lands = (lands ^ device) % 2 * count + lands // 2 * (2 * blocks) + owner % blocks
    push = (jnp.concatenate([lands, lands + blocks])[None, :] == tall).astype(jnp.bfloat16)

    per_step = 2
    columns = per_step * HEAD
    fixed = lambda h, *_: (0, 0)
    square = pl.BlockSpec((side, side), fixed)
    table = pl.BlockSpec((rows, HEAD), fixed)
    part = pl.BlockSpec((4, BLOCK, columns), lambda h, *_: (0, 0, h))
    def attend_held(begin, end, waits, carried):
        skip = begin // per_step
        tensor = pl.BlockSpec((rows, columns), lambda h, *_: (0, h + skip))
        far = pl.BlockSpec((count, columns), lambda h, *_: (0, h + skip))
        extra = carried + waits
        results = pl.pallas_call(
            functools.partial(attend_kernel, per_step, blocks, count, begin, 0, len(extra)),
            grid_spec=pltpu.PrefetchScalarGridSpec(
                num_scalar_prefetch=3,
                grid=((end - begin) // per_step,),
                in_specs=[far, far, square, square]
                + [table] * 4
                + [tensor] * 4
                + [anywhere] * len(extra),
                out_specs=[part] * blocks + [far] * 2,
            ),
            out_shape=[jax.ShapeDtypeStruct((4, BLOCK, (end - begin) * HEAD), jnp.bfloat16)]
            * blocks
            + [jax.ShapeDtypeStruct((count, width), jnp.bfloat16)] * 2,
            input_output_aliases={15 + i: blocks + i for i in range(len(carried))},
            compiler_params=big,
            cost_estimate=heavy,
        )(
            info,
            dilation_phase,
            segment_device_count,
            near_far,
            other_far,
            pull,
            push,
            cq,
            sq,
            ck,
            sk,
            *originals,
            *extra,
        )
        return list(results[:blocks]), list(results[blocks:])

    waits = list(moved_tables) + [come_1, come_2]
    parts, payload = attend_held(first, middle, waits, [])
    parts_last, payload = attend_held(middle, heads, [], payload)
    for k in range(1, blocks):
        parts[k] = swap(parts[k], k)
        parts_last[k] = swap(parts_last[k], k)

    shapes = [jax.ShapeDtypeStruct((blocks, BLOCK, width), jnp.bfloat16)] * 4
    shapes = shapes + [jax.ShapeDtypeStruct((count, width), jnp.bfloat16)] * 2

    def attend_relaid(begin, end, come, carried):
        skip = begin // per_step
        tensor = pl.BlockSpec((BLOCK, columns), lambda h, info, *_: (info[0], h + skip))
        far = pl.BlockSpec((count, columns), lambda h, *_: (0, h + skip))
        whole = pl.BlockSpec((blocks, BLOCK, columns), lambda h, *_: (0, 0, h + skip))
        shifted = pl.BlockSpec((4, BLOCK, columns), lambda h, *_: (0, 0, h + skip))
        operands = 3 + 4 + 4 + 4 + blocks - 1
        return pl.pallas_call(
            functools.partial(attend_kernel, per_step, blocks, count, begin, len(carried), 0),
            grid_spec=pltpu.PrefetchScalarGridSpec(
                num_scalar_prefetch=3,
                grid=((end - begin) // per_step,),
                in_specs=[far, far, square, square]
                + [table] * 4
                + [tensor] * 4
                + [shifted, part, shifted]
                + [anywhere] * len(carried),
                out_specs=[whole] * 4 + [far] * 2,
                ),
            out_shape=shapes,
            input_output_aliases={
                operands + i: 6 - len(carried) + i for i in range(len(carried))
            },
            compiler_params=big,
            cost_estimate=light,
        )(
            moved,
            dilation_phase,
            segment_device_count,
            near_far,
            other_far,
            pull,
            push,
            *moved_tables,
            *originals,
            *come,
            *carried,
        )

    results = attend_relaid(0, early, [come_1, come_2, come_3], payload)
    results = attend_relaid(early, first, [come_1, come_rest, come_3], results)
    finals = [one.reshape(rows, width) for one in results[:4]]

    def after(array, wait):
        return pl.pallas_call(
            link_kernel,
            in_specs=[anywhere] * 2,
            out_specs=anywhere,
            out_shape=jax.ShapeDtypeStruct(array.shape, array.dtype),
            input_output_aliases={0: 0},
            compiler_params=pltpu.CompilerParams(vmem_limit_bytes=room, has_side_effects=True),
        )(array, wait)

    crossing = swap(after(results[5], parts[2]), 1)
    payload = results[4].astype(jnp.float32) + crossing.astype(jnp.float32)
    payload = after(payload.astype(jnp.bfloat16), parts_last[2])
    got = lax.all_to_all(
        payload.reshape(devices // 2, 2 * blocks, width),
        ("ctx", "bal"),
        split_axis=0,
        concat_axis=0,
        tiled=True,
        axis_index_groups=halves,
    )

    new_phase = (comes_from[:, None] * BLOCK + dilation_phase[None, :]).astype(jnp.int32)
    new_cos, new_sin = flat_tables(new_phase, total)
    out = jax.ShapeDtypeStruct((rows, width), jnp.bfloat16)
    slots = partner.astype(jnp.int32)
    items = [(k, edge, brim - edge) for k in range(3)]
    items += [(k, brim, width - brim) for k in range(3)]
    number = len(items)
    finals = pl.pallas_call(
        functools.partial(place_kernel, items),
        in_specs=[smem] + [anywhere] * (number + 4),
        out_specs=[anywhere] * 4,
        out_shape=[out] * 4,
        input_output_aliases={1 + number + t: t for t in range(4)},
        scratch_shapes=[pltpu.VMEM((4, BLOCK, item[2]), jnp.bfloat16) for item in items]
        + [pltpu.SemaphoreType.DMA((number,)), pltpu.SemaphoreType.DMA((number, 4))],
        compiler_params=big,
        cost_estimate=light,
    )(slots, *parts[:3], *parts_last[:3], *finals)
    late = 3
    patched = pl.pallas_call(
        functools.partial(patch_kernel, heads, blocks, (late,), edge),
        in_specs=[smem, smem, anywhere, vmem, vmem, anywhere, anywhere],
        out_specs=[anywhere] * 2,
        out_shape=[out] * 2,
        input_output_aliases={5: 0, 6: 1},
        scratch_shapes=[
            pltpu.VMEM((devices // 2, 2 * blocks, width), jnp.bfloat16),
            pltpu.VMEM((2, blocks, BLOCK, width), jnp.bfloat16),
            pltpu.SemaphoreType.DMA(()),
            pltpu.SemaphoreType.DMA((2, blocks)),
            pltpu.SemaphoreType.DMA((2, blocks)),
        ],
        compiler_params=big,
        cost_estimate=light,
    )(dilation_phase, slots, got, new_cos, new_sin, finals[2], finals[3])
    return tuple(
        pl.pallas_call(
            functools.partial(last_kernel, heads, late, edge),
            in_specs=[smem, smem, anywhere, vmem, vmem] + [anywhere] * 6,
            out_specs=[anywhere] * 4,
            out_shape=[out] * 4,
            input_output_aliases={7 + t: t for t in range(4)},
            scratch_shapes=[
                pltpu.VMEM((devices // 2, 2 * blocks, width - edge), jnp.bfloat16),
                pltpu.VMEM((4, BLOCK, width - edge), jnp.bfloat16),
                pltpu.SemaphoreType.DMA(()),
                pltpu.SemaphoreType.DMA((2,)),
                pltpu.SemaphoreType.DMA((4,)),
            ],
            compiler_params=big,
        )(
            dilation_phase,
            slots,
            got,
            new_cos[:, edge:],
            new_sin[:, edge:],
            parts[late],
            parts_last[late],
            finals[0],
            finals[1],
            *patched,
        )
    )


def solution(mesh):
    token = P(("groups", "ctx", "bal"), "head")
    return jax.shard_map(
        local,
        mesh=mesh,
        in_specs=(token, token, token, token, P("head"), P("head"), P("groups")),
        out_specs=(token, token, token, token),
        check_vma=False,
    )
```

```python
import functools
import math

import jax
import jax.numpy as jnp
from jax import lax
from jax.experimental import pallas as pl
from jax.experimental.pallas import tpu as pltpu
from jax.sharding import PartitionSpec as P

BLOCK = 128
HEAD = 128
LOG2E = 1.4426950408889634
NT = (((1,), (1,)), ((), ()))
TN = (((0,), (0,)), ((), ()))


def tables(positions, total):
    half = HEAD // 2
    pair = jnp.arange(half, dtype=jnp.float32)
    inverse = jnp.exp(pair * (-2.0 * math.log(10000.0) / HEAD))
    where = positions.astype(jnp.float32)[..., None]
    angles = where * inverse
    base = (2.0 * pair / HEAD + 0.4) / 1.4
    growth = jnp.exp((2.0 * where - total) / total * jnp.log(base))
    cosine, sine = jnp.cos(angles), jnp.sin(angles)

    def pack(scale):
        first, second = cosine * scale, sine * scale
        return (
            jnp.concatenate([first, first], axis=-1),
            jnp.concatenate([-second, second], axis=-1),
        )

    return pack(growth) + pack(1.0 / growth)


def flat_tables(positions, total):
    half = HEAD // 2
    lane = jnp.arange(positions.shape[1] * HEAD, dtype=jnp.int32) % HEAD
    pair = (lane % half).astype(jnp.float32)
    inverse = jnp.exp(pair * (-2.0 * math.log(10000.0) / HEAD))
    where = jnp.repeat(positions.astype(jnp.float32), HEAD, axis=1)
    angles = where * inverse[None, :]
    base = (2.0 * pair / HEAD + 0.4) / 1.4
    growth = jnp.exp((2.0 * where - total) / total * jnp.log(base)[None, :])
    sine = jnp.where(lane[None, :] < half, -jnp.sin(angles), jnp.sin(angles))
    return jnp.cos(angles) / growth, sine / growth


def dot(left, right, dims=None):
    if dims is None:
        dims = (((1,), (0,)), ((), ()))
    return lax.dot_general(left, right, dims, preferred_element_type=jnp.float32)


def attend_kernel(
    per_step, blocks, count, first, relaid, waits, info, phase, seg, far_ref, other_ref, pull_ref, push_ref, *rest
):
    cq_ref, sq_ref, ck_ref, sk_ref = rest[:4]
    own = rest[4:8]
    rest = rest[8:]
    if relaid:
        come, rest = rest[: blocks - 1], rest[blocks - 1 + relaid :]
        finals, rest = rest[:4], rest[4:]
    else:
        finals, rest = rest[waits : waits + blocks], rest[waits + blocks :]
    own_pay, other_pay = rest
    scale = 1.0 / math.sqrt(HEAD)
    key_at = lax.broadcasted_iota(jnp.int32, (BLOCK, BLOCK), 0)
    query_at = lax.broadcasted_iota(jnp.int32, (BLOCK, BLOCK), 1)
    far_at = lax.broadcasted_iota(jnp.int32, (count, BLOCK), 0)
    far_query = lax.broadcasted_iota(jnp.int32, (count, BLOCK), 1)
    half = HEAD // 2
    for sub in range(per_step):
        head = first + pl.program_id(0) * per_step + sub
        lanes = slice(sub * HEAD, (sub + 1) * HEAD)
        held = jnp.concatenate([far_ref[:, lanes], other_ref[:, lanes]], axis=0)
        both = dot(pull_ref[...], held).astype(jnp.bfloat16)
        far_k, far_v = both[:count], both[count:]
        span = seg[head] * blocks
        at = phase[head]
        causal = (key_at <= query_at) & (key_at != at)
        behind = far_at * BLOCK + at - far_query
        p_far, d_far, q_all, g_all = [], [], [], []
        for k in range(blocks):
            if relaid:
                rows = slice(k * BLOCK, (k + 1) * BLOCK)
                source = [ref[:, lanes] for ref in own]
                if k:
                    source = [come[k - 1][t, :, lanes] for t in range(4)]
            else:
                rows = pl.ds(pl.multiple_of(info[k] * BLOCK, BLOCK), BLOCK)
                source = [ref[rows, lanes] for ref in own]
            block = info[blocks + k]
            low = block & (-span)
            cq, sq, ck, sk = cq_ref[rows, :], sq_ref[rows, :], ck_ref[rows, :], sk_ref[rows, :]
            raw_q, raw_k, value, grad = source
            raw_q = raw_q.astype(jnp.float32)
            raw_k = raw_k.astype(jnp.float32)
            tq = (raw_q * cq + pltpu.roll(raw_q, half, 1) * sq).astype(jnp.bfloat16)
            tk = (raw_k * ck + pltpu.roll(raw_k, half, 1) * sk).astype(jnp.bfloat16)
            keys = jnp.concatenate([tk, far_k], axis=0)
            vals = jnp.concatenate([value, far_v], axis=0)
            score = dot(keys, tq, NT)
            allowed = (far_at >= low) & (behind <= block * BLOCK)
            score = jnp.concatenate(
                [
                    jnp.where(causal, score[:BLOCK], -jnp.inf),
                    jnp.where(allowed, score[BLOCK:], -jnp.inf),
                ],
                axis=0,
            )
            top = jnp.max(score, axis=0, keepdims=True)
            weight = jnp.exp2((score - top) * (scale * LOG2E))
            prob = weight * (1.0 / jnp.sum(weight, axis=0, keepdims=True))
            p16 = prob.astype(jnp.bfloat16)
            dprob = dot(vals, grad, NT)
            delta = jnp.sum(p16.astype(jnp.float32) * dprob, axis=0, keepdims=True)
            d16 = (prob * (dprob - delta)).astype(jnp.bfloat16)
            out = dot(p16, vals, TN)
            dq = dot(d16, keys, TN) * scale
            dk = dot(d16[:BLOCK], tq) * scale
            dv = dot(p16[:BLOCK], grad)
            made = (
                out,
                dq * cq - pltpu.roll(dq, half, 1) * sq,
                dk * ck - pltpu.roll(dk, half, 1) * sk,
                dv,
            )
            for t in range(4):
                if relaid:
                    finals[t][info[2 * blocks + k], :, lanes] = made[t].astype(jnp.bfloat16)
                else:
                    finals[k][t, :, lanes] = made[t].astype(jnp.bfloat16)
            p_far.append(p16[BLOCK:])
            d_far.append(d16[BLOCK:])
            q_all.append(tq)
            g_all.append(grad)
        far_dk = dot(jnp.concatenate(d_far, axis=1), jnp.concatenate(q_all, axis=0)) * scale
        far_dv = dot(jnp.concatenate(p_far, axis=1), jnp.concatenate(g_all, axis=0))
        far_sum = jnp.concatenate([far_dk, far_dv], axis=0).astype(jnp.bfloat16)
        pay = dot(push_ref[...], far_sum).astype(jnp.bfloat16)
        own_pay[:, lanes] = pay[:count]
        other_pay[:, lanes] = pay[count:]


def pick_kernel(
    heads, blocks, phase, k_hbm, v_hbm, cos_ref, sin_ref, after, out_ref, k_ref, v_ref, row_ref,
    load, save
):
    moves = [
        pltpu.make_async_copy(k_hbm, k_ref, load.at[0]),
        pltpu.make_async_copy(v_hbm, v_ref, load.at[1]),
    ]
    for move in moves:
        move.start()
    for move in moves:
        move.wait()
    spot = lax.broadcasted_iota(jnp.int32, (16, HEAD), 0)
    for head in range(heads):
        at = phase[head]
        start = pl.multiple_of(at // 16 * 16, 16)
        lanes = slice(head * HEAD, (head + 1) * HEAD)
        both = []
        for ref in (k_ref, v_ref):
            rows = []
            for k in range(blocks):
                tile = ref[pl.ds(pl.multiple_of(k * BLOCK + start, 16), 16), lanes]
                tile = jnp.where(spot == at - start, tile.astype(jnp.float32), 0.0)
                rows.append(jnp.sum(tile, axis=0, keepdims=True))
            both.append(jnp.concatenate(rows, axis=0))
        key, value = both
        key = key * cos_ref[:, lanes] + pltpu.roll(key, HEAD // 2, 1) * sin_ref[:, lanes]
        row_ref[:, lanes] = jnp.concatenate([key, value], axis=0).astype(jnp.bfloat16)
    copies = [
        pltpu.make_async_copy(row_ref, out_ref.at[d], save.at[d]) for d in range(out_ref.shape[0])
    ]
    for copy in copies:
        copy.start()
    for copy in copies:
        copy.wait()


def pack_kernel(jobs, blocks, owner, after, *rest):
    number = len(jobs)
    inputs, rest = rest[:4], rest[4:]
    outs, rooms, (load, save) = rest[:number], rest[number : 2 * number], rest[2 * number :]
    order = [(job, t) for job in range(number) for t in range(4)]
    bal = lax.axis_index("bal")
    base = (lax.axis_index("ctx") * blocks + bal) * blocks
    partners = [(owner[base + i] // blocks) % blocks ^ bal for i in range(blocks)]
    picks = []
    for k, _, _ in jobs:
        pick = jnp.int32(0)
        for i in range(1, blocks):
            pick = jnp.where(partners[i] == k, jnp.int32(i), pick)
        picks.append(pick)

    def fetch(job, t):
        _, start, width = jobs[job]
        rows = pl.ds(pl.multiple_of(picks[job] * BLOCK, BLOCK), BLOCK)
        source = inputs[t].at[rows, pl.ds(start, width)]
        return pltpu.make_async_copy(source, rooms[job].at[t], load.at[job, t])

    def store(job, t):
        return pltpu.make_async_copy(rooms[job].at[t], outs[job].at[t], save.at[job, t])

    for job, t in order:
        fetch(job, t).start()
    for job, t in order:
        fetch(job, t).wait()
        store(job, t).start()
    for job, t in order:
        store(job, t).wait()


def link_kernel(*refs):
    pass


def place_kernel(items, slot, *rest):
    number = len(items)
    parts = rest[:number]
    finals = rest[number + 4 : number + 8]
    rooms, (load, save) = rest[number + 8 : 2 * number + 8], rest[2 * number + 8 :]

    def save_of(i, t):
        k, start, width = items[i]
        top = pl.multiple_of(slot[k] * BLOCK, BLOCK)
        where = finals[t].at[pl.ds(top, BLOCK), pl.ds(start, width)]
        return pltpu.make_async_copy(rooms[i].at[t], where, save.at[i, t])

    loads = [pltpu.make_async_copy(parts[i], rooms[i], load.at[i]) for i in range(number)]
    for move in loads:
        move.start()
    for i in range(number):
        loads[i].wait()
        for t in range(4):
            save_of(i, t).start()
    for i in range(number):
        for t in range(4):
            save_of(i, t).wait()


def far_rows(got, cos_ref, sin_ref, blocks):
    total = got[0].astype(jnp.float32)
    for sender in range(1, got.shape[0]):
        total = total + got[sender].astype(jnp.float32)
    far_k, far_v = total[:blocks], total[blocks:]
    heads = far_k.shape[1] // HEAD
    turned = []
    for head in range(heads):
        lanes = slice(head * HEAD, (head + 1) * HEAD)
        one = far_k[:, lanes]
        turned.append(
            one * cos_ref[:, lanes] - pltpu.roll(one, HEAD // 2, 1) * sin_ref[:, lanes]
        )
    values = [far_v[:, head * HEAD : (head + 1) * HEAD] for head in range(heads)]
    return turned, values


def overwrite(ref, lanes, at, source, pick):
    spot = lax.broadcasted_iota(jnp.int32, (16, HEAD), 0)
    line = lax.broadcasted_iota(jnp.int32, source.shape, 0)
    start = pl.multiple_of(at // 16 * 16, 16)
    row = jnp.sum(jnp.where(line == pick, source, 0.0), axis=0, keepdims=True)
    old = ref[pl.ds(start, 16), lanes].astype(jnp.float32)
    ref[pl.ds(start, 16), lanes] = jnp.where(spot == at - start, row, old).astype(jnp.bfloat16)


def patch_kernel(
    heads, blocks, late, edge, phase, slot, got_hbm, cos_ref, sin_ref, dk_in, dv_in, dk, dv, got,
    room, get, load, save
):
    outs = (dk, dv)
    width = room.shape[-1]
    order = [(k, t) for k in range(blocks) for t in range(2)]

    def span(k):
        return pl.ds(0, edge if k in late else width)

    def here(t, k):
        rows = pl.ds(pl.multiple_of(slot[k] * BLOCK, BLOCK), BLOCK)
        return outs[t].at[rows, span(k)]

    def fetch(t, k):
        return pltpu.make_async_copy(here(t, k), room.at[t, k, :, span(k)], load.at[t, k])

    def store(t, k):
        return pltpu.make_async_copy(room.at[t, k, :, span(k)], here(t, k), save.at[t, k])

    first = pltpu.make_async_copy(got_hbm, got, get)
    first.start()
    for k, t in order:
        fetch(t, k).start()
    first.wait()
    fresh = far_rows(got, cos_ref, sin_ref, blocks)
    for k, t in order:
        fetch(t, k).wait()
        for head in range(edge // HEAD if k in late else heads):
            lanes = slice(head * HEAD, (head + 1) * HEAD)
            overwrite(room.at[t, k], lanes, phase[head], fresh[t][head], slot[k])
        store(t, k).start()
    for k, t in order:
        store(t, k).wait()


def last_kernel(late, begin, end, phase, slot, got_hbm, cos_ref, sin_ref, piece, *rest):
    outs = rest[4:8]
    got, room, get, load, save = rest[8:]
    blocks = got.shape[1] // 2
    right = pl.ds(begin * HEAD, room.shape[-1])
    rows = pl.ds(pl.multiple_of(slot[late] * BLOCK, BLOCK), BLOCK)
    first = pltpu.make_async_copy(got_hbm.at[:, :, right], got, get)
    whole = pltpu.make_async_copy(piece, room, load)
    stores = [
        pltpu.make_async_copy(room.at[t], outs[t].at[rows, right], save.at[t]) for t in range(4)
    ]
    whole.start()
    first.start()
    whole.wait()
    for t in range(2):
        stores[t].start()
    first.wait()
    fresh = far_rows(got, cos_ref, sin_ref, blocks)
    for t in range(2):
        for head in range(begin, end):
            here = head - begin
            lanes = slice(here * HEAD, (here + 1) * HEAD)
            overwrite(room.at[2 + t], lanes, phase[head], fresh[t][here], slot[late])
        stores[2 + t].start()
    for store in stores:
        store.wait()


def local(queries, keys, values, output_gradient, dilation_phase, segment_device_count, owner):
    rows, width = queries.shape
    heads = width // HEAD
    blocks = rows // BLOCK
    bal_size = lax.axis_size("bal")
    devices = lax.axis_size("ctx") * bal_size
    total = rows * devices
    count = owner.shape[0]
    assert blocks == bal_size == 4 and bal_size & (bal_size - 1) == 0
    bal = lax.axis_index("bal")
    device = lax.axis_index("ctx") * bal_size + bal
    room = 66_900_000
    big = pltpu.CompilerParams(vmem_limit_bytes=room)
    smem = pl.BlockSpec(memory_space=pltpu.SMEM)
    vmem = pl.BlockSpec(memory_space=pltpu.VMEM)
    anywhere = pl.BlockSpec(memory_space=pl.ANY)
    light = pl.CostEstimate(flops=2_000_000_000, bytes_accessed=5_000_000, transcendentals=0)
    heavy = pl.CostEstimate(flops=20_000_000_000, bytes_accessed=60_000_000, transcendentals=0)

    def tokens_of(ids):
        return (ids[:, None] * BLOCK + jnp.arange(BLOCK, dtype=jnp.int32)[None, :]).reshape(rows)

    def swap(array, k):
        return lax.ppermute(array, "bal", [(i, i ^ k) for i in range(bal_size)])

    steps = jnp.arange(blocks, dtype=jnp.int32)
    held = device * blocks + steps
    goes_to = lax.dynamic_slice_in_dim(owner, device * blocks, blocks) // blocks % bal_size
    partner = steps ^ bal
    which = jnp.sum(jnp.where(goes_to[None, :] == partner[:, None], steps[None, :], 0), axis=1)
    info = jnp.concatenate([which, device * blocks + which]).astype(jnp.int32)
    comes_from = jnp.sum(
        jnp.where(
            owner[None, :] == held[:, None], jnp.arange(count, dtype=jnp.int32)[None, :], 0
        ),
        axis=1,
    )

    first = heads * 3 // 10 * 2
    early = first // 4 * 2
    middle = heads - 2
    cut, edge, brim = early * HEAD, first * HEAD, middle * HEAD
    originals = (queries, keys, values, output_gradient)

    def send_inputs(jobs, after):
        sizes = [(4, BLOCK, width) for _, _, width in jobs]
        sent = pl.pallas_call(
            functools.partial(pack_kernel, jobs, blocks),
            in_specs=[smem] + [anywhere] * 5,
            out_specs=[anywhere] * len(jobs),
            out_shape=[jax.ShapeDtypeStruct(size, jnp.bfloat16) for size in sizes],
            scratch_shapes=[pltpu.VMEM(size, jnp.bfloat16) for size in sizes]
            + [pltpu.SemaphoreType.DMA((len(jobs), 4))] * 2,
            compiler_params=big,
        )(owner, after, *originals)
        return sent, [swap(one, job[0]) for one, job in zip(sent, jobs)]

    sent, come_early = send_inputs([(2, 0, cut)], queries)

    cq, sq, ck, sk = tables(tokens_of(held), total)
    own_phase = (held[:, None] * BLOCK + dilation_phase[None, :]).astype(jnp.int32)
    pick_cos, pick_sin = flat_tables(own_phase, total)
    own_far = pl.pallas_call(
        functools.partial(pick_kernel, heads, blocks),
        in_specs=[smem, anywhere, anywhere, vmem, vmem, anywhere],
        out_specs=anywhere,
        out_shape=jax.ShapeDtypeStruct((devices // 2, 2 * blocks, width), jnp.bfloat16),
        scratch_shapes=[
            pltpu.VMEM((rows, width), jnp.bfloat16),
            pltpu.VMEM((rows, width), jnp.bfloat16),
            pltpu.VMEM((2 * blocks, width), jnp.bfloat16),
            pltpu.SemaphoreType.DMA((2,)),
            pltpu.SemaphoreType.DMA((devices // 2,)),
        ],
        compiler_params=big,
    )(
        dilation_phase,
        keys,
        values,
        pick_cos,
        pick_sin,
        sent[0],
    )
    halves = [list(range(0, devices, 2)), list(range(1, devices, 2))]
    near_far = lax.all_to_all(
        own_far,
        ("ctx", "bal"),
        split_axis=0,
        concat_axis=0,
        tiled=True,
        axis_index_groups=halves,
    ).reshape(count, width)
    other_far = swap(near_far, 1)
    jobs = [(2, cut, edge - cut), (3, 0, edge), (1, 0, edge)]
    _, (come_rest, come_3, come_1) = send_inputs(jobs, own_far)
    come_2 = come_early[0]

    ids = (device ^ steps) * blocks
    came = jnp.sum(
        jnp.where(comes_from[None, :] // blocks * blocks == ids[:, None], comes_from[None, :], 0),
        axis=1,
    )
    moved = jnp.concatenate([which, came, partner]).astype(jnp.int32)
    moved_tables = tables(tokens_of(came), total)

    side = 2 * count
    wide = jnp.arange(side, dtype=jnp.int32)
    tall = wide[:, None]
    wide = wide[None, :]
    source = tall % count
    holder = source // blocks
    held_row = (holder ^ device) % 2 * count + holder // 2 * (2 * blocks)
    pull = (wide == held_row + tall // count * blocks + source % blocks).astype(jnp.bfloat16)
    lands = owner // blocks
    lands = (lands ^ device) % 2 * count + lands // 2 * (2 * blocks) + owner % blocks
    push = (jnp.concatenate([lands, lands + blocks])[None, :] == tall).astype(jnp.bfloat16)

    per_step = 2
    columns = per_step * HEAD
    fixed = lambda h, *_: (0, 0)
    square = pl.BlockSpec((side, side), fixed)
    table = pl.BlockSpec((rows, HEAD), fixed)
    part = pl.BlockSpec((4, BLOCK, columns), lambda h, *_: (0, 0, h))
    def attend_held(begin, end, waits, carried):
        skip = begin // per_step
        tensor = pl.BlockSpec((rows, columns), lambda h, *_: (0, h + skip))
        far = pl.BlockSpec((count, columns), lambda h, *_: (0, h + skip))
        extra = carried + waits
        results = pl.pallas_call(
            functools.partial(attend_kernel, per_step, blocks, count, begin, 0, len(extra)),
            grid_spec=pltpu.PrefetchScalarGridSpec(
                num_scalar_prefetch=3,
                grid=((end - begin) // per_step,),
                in_specs=[far, far, square, square]
                + [table] * 4
                + [tensor] * 4
                + [anywhere] * len(extra),
                out_specs=[part] * blocks + [far] * 2,
            ),
            out_shape=[jax.ShapeDtypeStruct((4, BLOCK, (end - begin) * HEAD), jnp.bfloat16)]
            * blocks
            + [jax.ShapeDtypeStruct((count, width), jnp.bfloat16)] * 2,
            input_output_aliases={15 + i: blocks + i for i in range(len(carried))},
            compiler_params=big,
            cost_estimate=heavy,
        )(
            info,
            dilation_phase,
            segment_device_count,
            near_far,
            other_far,
            pull,
            push,
            cq,
            sq,
            ck,
            sk,
            *originals,
            *extra,
        )
        return list(results[:blocks]), list(results[blocks:])

    waits = list(moved_tables) + [come_1, come_2]
    parts, payload = attend_held(first, middle, waits, [])
    parts_last, payload = attend_held(middle, heads, [], payload)
    for k in range(1, blocks):
        parts[k] = swap(parts[k], k)
        parts_last[k] = swap(parts_last[k], k)

    shapes = [jax.ShapeDtypeStruct((blocks, BLOCK, width), jnp.bfloat16)] * 4
    shapes = shapes + [jax.ShapeDtypeStruct((count, width), jnp.bfloat16)] * 2

    def attend_relaid(begin, end, come, carried):
        skip = begin // per_step
        tensor = pl.BlockSpec((BLOCK, columns), lambda h, info, *_: (info[0], h + skip))
        far = pl.BlockSpec((count, columns), lambda h, *_: (0, h + skip))
        whole = pl.BlockSpec((blocks, BLOCK, columns), lambda h, *_: (0, 0, h + skip))
        shifted = pl.BlockSpec((4, BLOCK, columns), lambda h, *_: (0, 0, h + skip))
        operands = 3 + 4 + 4 + 4 + blocks - 1
        return pl.pallas_call(
            functools.partial(attend_kernel, per_step, blocks, count, begin, len(carried), 0),
            grid_spec=pltpu.PrefetchScalarGridSpec(
                num_scalar_prefetch=3,
                grid=((end - begin) // per_step,),
                in_specs=[far, far, square, square]
                + [table] * 4
                + [tensor] * 4
                + [shifted, part, shifted]
                + [anywhere] * len(carried),
                out_specs=[whole] * 4 + [far] * 2,
                ),
            out_shape=shapes,
            input_output_aliases={
                operands + i: 6 - len(carried) + i for i in range(len(carried))
            },
            compiler_params=big,
            cost_estimate=light,
        )(
            moved,
            dilation_phase,
            segment_device_count,
            near_far,
            other_far,
            pull,
            push,
            *moved_tables,
            *originals,
            *come,
            *carried,
        )

    results = attend_relaid(0, early, [come_1, come_2, come_3], payload)
    results = attend_relaid(early, first, [come_1, come_rest, come_3], results)
    finals = [one.reshape(rows, width) for one in results[:4]]

    def after(array, wait):
        return pl.pallas_call(
            link_kernel,
            in_specs=[anywhere] * 2,
            out_specs=anywhere,
            out_shape=jax.ShapeDtypeStruct(array.shape, array.dtype),
            input_output_aliases={0: 0},
            compiler_params=pltpu.CompilerParams(vmem_limit_bytes=room, has_side_effects=True),
        )(array, wait)

    crossing = swap(after(results[5], parts[2]), 1)
    payload = results[4].astype(jnp.float32) + crossing.astype(jnp.float32)
    payload = after(payload.astype(jnp.bfloat16), parts_last[2])
    got = lax.all_to_all(
        payload.reshape(devices // 2, 2 * blocks, width),
        ("ctx", "bal"),
        split_axis=0,
        concat_axis=0,
        tiled=True,
        axis_index_groups=halves,
    )

    new_phase = (comes_from[:, None] * BLOCK + dilation_phase[None, :]).astype(jnp.int32)
    new_cos, new_sin = flat_tables(new_phase, total)
    out = jax.ShapeDtypeStruct((rows, width), jnp.bfloat16)
    slots = partner.astype(jnp.int32)
    items = [(k, edge, brim - edge) for k in range(3)]
    items += [(k, brim, width - brim) for k in range(3)]
    number = len(items)
    finals = pl.pallas_call(
        functools.partial(place_kernel, items),
        in_specs=[smem] + [anywhere] * (number + 4),
        out_specs=[anywhere] * 4,
        out_shape=[out] * 4,
        input_output_aliases={1 + number + t: t for t in range(4)},
        scratch_shapes=[pltpu.VMEM((4, BLOCK, item[2]), jnp.bfloat16) for item in items]
        + [pltpu.SemaphoreType.DMA((number,)), pltpu.SemaphoreType.DMA((number, 4))],
        compiler_params=big,
        cost_estimate=light,
    )(slots, *parts[:3], *parts_last[:3], *finals)
    late = 3
    patched = pl.pallas_call(
        functools.partial(patch_kernel, heads, blocks, (late,), edge),
        in_specs=[smem, smem, anywhere, vmem, vmem, anywhere, anywhere],
        out_specs=[anywhere] * 2,
        out_shape=[out] * 2,
        input_output_aliases={5: 0, 6: 1},
        scratch_shapes=[
            pltpu.VMEM((devices // 2, 2 * blocks, width), jnp.bfloat16),
            pltpu.VMEM((2, blocks, BLOCK, width), jnp.bfloat16),
            pltpu.SemaphoreType.DMA(()),
            pltpu.SemaphoreType.DMA((2, blocks)),
            pltpu.SemaphoreType.DMA((2, blocks)),
        ],
        compiler_params=big,
        cost_estimate=light,
    )(dilation_phase, slots, got, new_cos, new_sin, finals[2], finals[3])
    def finish(begin, end, piece, arrays):
        lanes = slice(begin * HEAD, end * HEAD)
        size = (end - begin) * HEAD
        return pl.pallas_call(
            functools.partial(last_kernel, late, begin, end),
            in_specs=[smem, smem, anywhere, vmem, vmem] + [anywhere] * 5,
            out_specs=[anywhere] * 4,
            out_shape=[out] * 4,
            input_output_aliases={6 + t: t for t in range(4)},
            scratch_shapes=[
                pltpu.VMEM((devices // 2, 2 * blocks, size), jnp.bfloat16),
                pltpu.VMEM((4, BLOCK, size), jnp.bfloat16),
                pltpu.SemaphoreType.DMA(()),
                pltpu.SemaphoreType.DMA(()),
                pltpu.SemaphoreType.DMA((4,)),
            ],
            compiler_params=big,
        )(dilation_phase, slots, got, new_cos[:, lanes], new_sin[:, lanes], piece, *arrays)

    finals = finish(first, middle, parts[late], [finals[0], finals[1], *patched])
    return tuple(finish(middle, heads, parts_last[late], finals))


def solution(mesh):
    token = P(("groups", "ctx", "bal"), "head")
    return jax.shard_map(
        local,
        mesh=mesh,
        in_specs=(token, token, token, token, P("head"), P("head"), P("groups")),
        out_specs=(token, token, token, token),
        check_vma=False,
    )
```
